128 devices in a mesh: elem: 64 (over z, y, x), face: 2 (over core).
Axes of the slice: x: 4, y: 4, z: 4, core: 2. Of those that a mesh axis runs over, the one named last changes fastest.
Arguments:
- forcing: float32 [32768, 512], P(('elem', 'face')), may hold values from -15 to 15, as said below
- kappa: float32 [32768], P(('elem', 'face')), may hold values from 0.3 to 3
- elem_order: int32 [128, 256], P(('elem', 'face')), may hold values from 0 to 255, each once within a row
Outputs:
- solution: float32 [32768, 512], P(('elem', 'face'))
- residual: float32 [32768, 512], P(('elem', 'face'))
The draws below stay inside these ranges and needn't reach their ends.
Inputs may be any that keep to these rules, and one draw needn't show every extreme that they name: `forcing`: element loads of order one, with a scale that varies by element and along z. `elem_order`: each row is a permutation of the 256 grid positions of the device's block.
All inputs are finite; a program needn't handle non-finite values.
Results may differ from the reference program's by a relative error of at most 0.0004.
Values sent between devices are 32-bit elements; how exact they have to be, the bound alone decides.
A program may use at most 192 MiB of HBM per device.

```python
import math
import jax
import jax.numpy as jnp
import numpy as np
from jax import lax

EX = 8
EY = 32
SWEEPS = 4
ITERS = 2
E_DEV = 256
GZ = 128
ELEMENTS = 32768
N_ELEM = 64
N_FACE = 2


def draw_forcing(key, part):
    key = jax.random.fold_in(key, 11)
    base_key, scale_key = jax.random.split(key)
    shape = (ELEMENTS, 512)
    rows = jnp.arange(ELEMENTS, dtype=jnp.int32) // E_DEV
    devices = ELEMENTS // E_DEV
    ramp = 0.6 + 1.2 * rows.astype(jnp.float32) / max(devices - 1, 1)
    rough = jnp.exp(jax.random.uniform(scale_key, (ELEMENTS, 1), jnp.float32, -0.7, 0.7))
    base = jnp.clip(jax.random.normal(base_key, shape, jnp.float32), -4.0, 4.0)
    return (base * ramp[:, None] * rough).astype(jnp.float32)


def levels(key, dims, shards, low, high):
    gain = 1.0
    for dim, shards_of in shards:
        heights = jax.random.uniform(jax.random.fold_in(jax.random.fold_in(key, 6), dim), (shards_of,), jnp.float32, low / len(shards), high / len(shards))
        gain = gain * jnp.repeat(jnp.exp(heights), dims[dim] // shards_of).reshape((-1,) + (1,) * (len(dims) - 1 - dim))
    return gain


def setup_inputs(seed: int = 0) -> dict:
    seeds = jax.random.split(jax.random.key(seed), 4)
    return {
        "forcing": draw_forcing(jax.random.fold_in(seeds[3], 71), 0),
        "kappa": jnp.clip(jnp.exp(math.log(3.0) - 2.3025851 * jax.random.uniform(seeds[1], (ELEMENTS,), jnp.float32) ** levels(seeds[1], (ELEMENTS,), ((0, 128),), -0.2, 0.2)), 0.3, 3.0),
        "elem_order": jax.vmap(lambda own: jax.random.permutation(own, E_DEV))(jax.random.split(seeds[2], (N_ELEM * N_FACE))).reshape((N_ELEM * N_FACE, E_DEV)).astype(jnp.int32),
    }


REACT = 0.02
OMEGA = 0.6


def legendre_seven(points):
    before = np.ones(8)
    current = np.array(points)
    for degree in range(1, 7):
        following = ((2 * degree + 1) * points * current - degree * before) / (degree + 1)
        before = current
        current = following
    return current


def element_tables():
    points = np.array([-1.0, -0.8717401485096066, -0.5917001814331423, -0.2092992179024789, 0.2092992179024789, 0.5917001814331423, 0.8717401485096066, 1.0])
    weights = np.array([1.0 / 28.0, 0.2107042271435061, 0.3411226924835044, 0.4124587946587038, 0.4124587946587038, 0.3411226924835044, 0.2107042271435061, 1.0 / 28.0])
    legendre = legendre_seven(points)
    derivative = np.zeros((8, 8))
    for left_node in range(8):
        for right_node in range(8):
            if left_node != right_node:
                derivative[left_node, right_node] = legendre[left_node] / (legendre[right_node] * (points[left_node] - points[right_node]))
    derivative[0, 0] = -14.0
    derivative[7, 7] = 14.0
    stiffness = derivative.T @ (weights[:, None] * derivative)
    mass = np.eye(8) * weights[None, :]
    full_stiff = np.kron(np.kron(mass, mass), stiffness) + np.kron(np.kron(mass, stiffness), mass) + np.kron(np.kron(stiffness, mass), mass)
    mass_nodes = np.kron(np.kron(weights, weights), weights)
    interp = np.stack([(1.0 - points) / 2.0, (1.0 + points) / 2.0], 1)
    prolong = np.kron(np.kron(interp, interp), interp)
    coarse_stiff = prolong.T @ full_stiff @ prolong
    coarse_mass = prolong.T @ (mass_nodes[:, None] * prolong)
    ends = np.ones(8)
    ends[0] = 2.0
    ends[7] = 2.0
    inverse_mult = 1.0 / np.kron(np.kron(ends, ends), ends)
    return stiffness, weights, full_stiff, mass_nodes, prolong, coarse_stiff, coarse_mass, inverse_mult


def pair_sum(grid, elem_axis, node_axis):
    upper = lax.index_in_dim(grid, 7, node_axis, keepdims=True)
    lower = lax.index_in_dim(grid, 0, node_axis, keepdims=True)
    shared = upper + jnp.roll(lower, -1, elem_axis)
    middle = lax.slice_in_dim(grid, 1, 7, axis=node_axis)
    return jnp.concatenate([jnp.roll(shared, 1, elem_axis), middle, shared], node_axis)


def direct_sum(field):
    grid = field.reshape(GZ, EY, EX, 8, 8, 8)
    grid = pair_sum(grid, 2, 5)
    grid = pair_sum(grid, 1, 4)
    grid = pair_sum(grid, 0, 3)
    return grid.reshape(-1, 512)


def full_corners(vert):
    parts = []
    for corner in range(8):
        along_z, along_y, along_x = corner // 4, corner // 2 % 2, corner % 2
        parts.append(jnp.roll(vert, (-along_z, -along_y, -along_x), (0, 1, 2)))
    return jnp.stack(parts, -1)


def full_assemble(contrib):
    total = jnp.zeros(contrib.shape[:3], jnp.float32)
    for corner in range(8):
        along_z, along_y, along_x = corner // 4, corner // 2 % 2, corner % 2
        total = total + jnp.roll(contrib[..., corner], (along_z, along_y, along_x), (0, 1, 2))
    return total


def reference(forcing, kappa, elem_order):
    tabs = [jnp.asarray(table, jnp.float32) for table in element_tables()]
    stiffness, weights, full_stiff, mass_nodes = tabs[0], tabs[1], tabs[2], tabs[3]
    prolong, coarse_stiff, coarse_mass, inverse_mult = tabs[4], tabs[5], tabs[6], tabs[7]
    highest = lax.Precision.HIGHEST
    devices = elem_order.shape[0]
    per_dev = elem_order.shape[1]
    where = (jnp.arange(devices, dtype=jnp.int32)[:, None] * per_dev + elem_order).reshape(-1).astype(jnp.int32)
    load = jnp.zeros_like(forcing).at[where].set(forcing)
    coeff = jnp.zeros_like(kappa).at[where].set(kappa)

    def apply_op(field):
        cube = field.reshape(-1, 8, 8, 8)
        term_x = jnp.einsum('xa,ecba->ecbx', stiffness, cube, precision=highest) * (weights[:, None, None] * weights[None, :, None])
        term_y = jnp.einsum('yb,ecba->ecya', stiffness, cube, precision=highest) * (weights[:, None, None] * weights[None, None, :])
        term_z = jnp.einsum('zc,ecba->ezba', stiffness, cube, precision=highest) * (weights[None, :, None] * weights[None, None, :])
        local = coeff[:, None] * (term_x + term_y + term_z).reshape(-1, 512) + REACT * mass_nodes[None, :] * field
        return direct_sum(local)

    diag_fine = direct_sum(coeff[:, None] * jnp.diag(full_stiff)[None, :] + REACT * mass_nodes[None, :])
    coeff_grid = coeff.reshape(GZ, EY, EX)
    coarse_diag = full_assemble(coeff_grid[..., None] * jnp.diag(coarse_stiff) + REACT * jnp.diag(coarse_mass))

    def coarse_apply(vert):
        values = full_corners(vert).reshape(-1, 8)
        contrib = coeff[:, None] * jnp.dot(values, coarse_stiff, precision=highest) + REACT * jnp.dot(values, coarse_mass, precision=highest)
        return full_assemble(contrib.reshape(GZ, EY, EX, 8))

    def precondition(resid):
        restricted = jnp.dot(resid * inverse_mult[None, :], prolong, precision=highest).reshape(GZ, EY, EX, 8)
        target = full_assemble(restricted)
        vert = jnp.zeros_like(target)
        for sweep in range(SWEEPS):
            vert = vert + OMEGA * (target - coarse_apply(vert)) / coarse_diag
        values = full_corners(vert).reshape(-1, 8)
        return resid / diag_fine + jnp.dot(values, prolong.T, precision=highest)

    def inner(left, right):
        return jnp.sum(left * right * inverse_mult[None, :])

    resid = direct_sum(load)
    solution = jnp.zeros_like(resid)
    precond = precondition(resid)
    direction = precond
    gamma = inner(resid, precond)
    for step in range(ITERS):
        image = apply_op(direction)
        alpha = gamma / inner(direction, image)
        solution = solution + alpha * direction
        resid = resid - alpha * image
        if step + 1 < ITERS:
            precond = precondition(resid)
            gamma_new = inner(resid, precond)
            direction = precond + (gamma_new / gamma) * direction
            gamma = gamma_new
    return solution[where], resid[where]
```

```python
import functools

import jax
import jax.numpy as jnp
import numpy as np
from jax import lax
from jax.experimental import pallas as pl
from jax.experimental.pallas import tpu as pltpu
from jax.sharding import PartitionSpec as P

EX = 8
EY = 32
ROWS = EX * EY
NODES = 512
REACT = 0.02
OMEGA = 0.6
REACH = 4
GROUP = 8
MESH = pl.DeviceIdType.MESH
F32 = jnp.float32
BF16 = jnp.bfloat16


def legendre_seven(points):
    before = np.ones(8)
    current = np.array(points)
    for degree in range(1, 7):
        following = ((2 * degree + 1) * points * current - degree * before) / (degree + 1)
        before = current
        current = following
    return current


def element_tables():
    points = np.array(
        [
            -1.0,
            -0.8717401485096066,
            -0.5917001814331423,
            -0.2092992179024789,
            0.2092992179024789,
            0.5917001814331423,
            0.8717401485096066,
            1.0,
        ]
    )
    weights = np.array(
        [
            1.0 / 28.0,
            0.2107042271435061,
            0.3411226924835044,
            0.4124587946587038,
            0.4124587946587038,
            0.3411226924835044,
            0.2107042271435061,
            1.0 / 28.0,
        ]
    )
    legendre = legendre_seven(points)
    derivative = np.zeros((8, 8))
    for left_node in range(8):
        for right_node in range(8):
            if left_node != right_node:
                derivative[left_node, right_node] = legendre[left_node] / (
                    legendre[right_node] * (points[left_node] - points[right_node])
                )
    derivative[0, 0] = -14.0
    derivative[7, 7] = 14.0
    stiffness = derivative.T @ (weights[:, None] * derivative)
    mass = np.eye(8) * weights[None, :]
    full_stiff = (
        np.kron(np.kron(mass, mass), stiffness)
        + np.kron(np.kron(mass, stiffness), mass)
        + np.kron(np.kron(stiffness, mass), mass)
    )
    mass_nodes = np.kron(np.kron(weights, weights), weights)
    interp = np.stack([(1.0 - points) / 2.0, (1.0 + points) / 2.0], 1)
    prolong = np.kron(np.kron(interp, interp), interp)
    return full_stiff, mass_nodes, prolong


def diagonal_tables(full_stiff, mass_nodes):
    diag = np.diag(full_stiff).reshape(8, 8, 8)
    mass = mass_nodes.reshape(8, 8, 8)
    share = np.zeros((32, 8, 8, 8))
    fixed = np.zeros((8, 8, 8))

    def ends(offset):
        if offset == 0:
            return list(range(8)), list(range(8))
        return ([7], [0]) if offset == 1 else ([0], [7])

    for index in range(27):
        offsets = (index // 9 - 1, index // 3 % 3 - 1, index % 3 - 1)
        mine = np.ix_(*[ends(offset)[0] for offset in offsets])
        theirs = np.ix_(*[ends(offset)[1] for offset in offsets])
        share[index][mine] += diag[theirs]
        fixed[mine] += REACT * mass[theirs]
    return share.reshape(32, NODES), fixed.reshape(1, NODES)


def split(value, pieces):
    parts = []
    for _ in range(pieces):
        part = value.astype(BF16)
        parts.append(part)
        value = value - part.astype(F32)
    return parts


def dot(left, right, dims=((1,), (0,))):
    return lax.dot_general(
        left, right, (dims, ((), ())), precision=lax.Precision.HIGHEST, preferred_element_type=F32
    )


def dot16(left, right, dims=((1,), (0,))):
    return lax.dot_general(left, right, (dims, ((), ())), preferred_element_type=F32)


def lanes(shape):
    return lax.broadcasted_iota(jnp.int32, shape, len(shape) - 1)


def roll_x(plane, by):
    size = plane.shape[1]
    along = lanes(plane.shape) % EX
    inside = pltpu.roll(plane, by % size, 1)
    around = pltpu.roll(plane, (by - EX * by) % size, 1)
    return jnp.where(along == (0 if by == 1 else EX - 1), around, inside)


def roll_y(plane, by):
    return pltpu.roll(plane, (by * EX) % plane.shape[1], 1)


def down(plane):
    return pltpu.roll(plane, plane.shape[0] - 1, 0)


def up(plane):
    return pltpu.roll(plane, 1, 0)


def shared_xy(tile):
    cube = tile.reshape(EY, EX, 128)
    lane = lanes(cube.shape)
    nx, ny = lane % 8, lane // 8 % 8
    after = pltpu.roll(pltpu.roll(cube, EX - 1, 1), 7, 2)
    before = pltpu.roll(pltpu.roll(cube, 1, 1), 128 - 7, 2)
    cube = cube + jnp.where(nx == 7, after, jnp.where(nx == 0, before, 0.0))
    after = pltpu.roll(jnp.concatenate([cube[1:], cube[:1]], 0), 56, 2)
    before = pltpu.roll(jnp.concatenate([cube[-1:], cube[:-1]], 0), 128 - 56, 2)
    cube = cube + jnp.where(ny == 7, after, jnp.where(ny == 0, before, 0.0))
    return cube.reshape(ROWS, 128)


def kernel(
    size,
    forcing_ref,
    kappa_ref,
    order_ref,
    stiff_ref,
    mass_ref,
    prolong_ref,
    share_ref,
    fixed_ref,
    solution_ref,
    residual_ref,
    r0_ref,
    z0_ref,
    q_ref,
    y_ref,
    w_ref,
    inverse_ref,
    coeff_ref,
    edge_out,
    edge_in,
    kap,
    rest,
    sum_a,
    sum_b,
    kap_send,
    kap_recv,
    rest_send,
    rest_recv,
    edge_send,
    edge_recv,
    a_send,
    a_recv,
    b_send,
    b_recv,
):
    me = lax.axis_index("elem") * 2 + lax.axis_index("face")
    groups = size // GROUP
    mine, place = lax.div(me, GROUP), lax.rem(me, GROUP)

    def ident(device):
        return lax.div(device, 2), lax.rem(device, 2)

    def ring(by):
        return ident(lax.rem(me + by + size, size))

    def group_mate(by):
        return ident(mine * GROUP + lax.rem(place + by, GROUP))

    def far_mate(by):
        return ident(lax.rem(mine + by, groups) * GROUP + place)

    near = [by for by in range(-REACH, REACH + 1) if by != 0]
    barrier = pltpu.get_barrier_semaphore()
    partners = [ring(by) for by in near]
    partners += [group_mate(by) for by in range(1, GROUP)]
    partners += [far_mate(by) for by in range(1, groups)]
    for partner in partners:
        pl.semaphore_signal(barrier, inc=1, device_id=partner, device_id_type=MESH)

    def remote(source, target, send, recv, device):
        return pltpu.make_async_remote_copy(
            src_ref=source,
            dst_ref=target,
            send_sem=send,
            recv_sem=recv,
            device_id=device,
            device_id_type=MESH,
        )

    def halo(buffer, send, recv):
        return [
            remote(
                buffer.at[REACH],
                buffer.at[REACH - by],
                send.at[REACH - by],
                recv.at[REACH - by],
                ring(by),
            )
            for by in near
        ]

    row = lax.broadcasted_iota(jnp.int32, (ROWS, ROWS), 0)
    pick = jnp.where(row == order_ref[...], 1.0, 0.0)
    pick16 = pick.astype(BF16)
    back16 = pick.T.astype(BF16)

    def permuted(matrix, value):
        return sum(dot16(matrix, part) for part in split(value, 3))

    kappa_rows = jnp.broadcast_to(kappa_ref[...], (16, ROWS))
    kappa_grid = sum(
        dot16(part, pick16, ((1,), (1,))) for part in split(kappa_rows, 3)
    )
    pl.semaphore_wait(barrier, len(partners))
    kap[REACH] = kappa_grid[0:1]
    kap_copies = halo(kap, kap_send, kap_recv)
    for copy in kap_copies:
        copy.start()

    load = permuted(pick16, forcing_ref[...])
    prolong = prolong_ref[...]

    def restrict(value, turn):
        each = dot(prolong, value, ((1,), (1,)))
        corner = lax.broadcasted_iota(jnp.int32, each.shape, 0)
        each = jnp.where(corner % 2 == 1, roll_x(each, 1), each)
        each = jnp.where(corner // 2 % 2 == 1, roll_y(each, 1), each)
        low = jnp.sum(each[0:4], axis=0, keepdims=True)
        high = jnp.sum(each[4:8], axis=0, keepdims=True)
        rest[turn, REACH] = jnp.concatenate([low, high], 0)
        copies = halo(rest.at[turn], rest_send.at[turn], rest_recv.at[turn])
        for copy in copies:
            copy.start()
        return copies

    half = lanes((ROWS // 2, 128)) < 64

    def faces(value, turn, target_ref):
        first = shared_xy(value[:, 0:128])
        last = shared_xy(value[:, 384:512])
        top, bottom = last[0:128], last[128:256]
        edge_out[turn, 0] = jnp.where(half, pltpu.roll(top, 64, 1), bottom)
        top, bottom = first[0:128], first[128:256]
        edge_out[turn, 1] = jnp.where(half, top, pltpu.roll(bottom, 64, 1))
        copies = [
            remote(
                edge_out.at[turn, way],
                edge_in.at[turn, way],
                edge_send.at[turn, way],
                edge_recv.at[turn, way],
                ring(by),
            )
            for way, by in ((0, 1), (1, -1))
        ]
        for copy in copies:
            copy.start()
        target_ref[:, 0:128] = first
        target_ref[:, 384:512] = last
        target_ref[:, 128:256] = shared_xy(value[:, 128:256])
        target_ref[:, 256:384] = shared_xy(value[:, 256:384])
        return copies

    def join(copies, turn, target_ref):
        for copy in copies:
            copy.wait_recv()
        below = edge_in[turn, 0]
        above = edge_in[turn, 1]
        zero = jnp.zeros_like(below)
        target_ref[0:128, 0:128] += jnp.where(half, below, zero)
        target_ref[128:256, 0:128] += jnp.where(half, pltpu.roll(below, 64, 1), zero)
        target_ref[0:128, 384:512] += jnp.where(half, zero, pltpu.roll(above, 64, 1))
        target_ref[128:256, 384:512] += jnp.where(half, zero, above)

    rest_copies = [restrict(load, 0)]
    edge_copies = [faces(load, 0, r0_ref)]

    for copy in kap_copies:
        copy.wait_recv()
    layers = [kap[m] for m in range(2 * REACH + 1)]
    under = jnp.concatenate(layers[:-1], 0)
    over = jnp.concatenate(layers[1:], 0)

    def four(layer):
        moved = [layer, roll_x(layer, 1)]
        return moved + [roll_y(moved[0], 1), roll_y(moved[1], 1)]

    under4, over4 = four(under), four(over)
    both4 = [a + b for a, b in zip(under4, over4)]
    diag = (2.0 / 3.0) * (both4[0] + both4[1] + both4[2] + both4[3]) + REACT * 64.0 / 27.0
    damp = -OMEGA / diag
    damp_down, damp_up = up(damp), down(damp)

    def stencil(layer4, planes):
        found = {}
        for dy in (-1, 0, 1):
            for dx in (-1, 0, 1):
                rows = (0, 1) if dy == 0 else ((0,) if dy == 1 else (1,))
                cols = (0, 1) if dx == 0 else ((0,) if dx == 1 else (1,))
                differ = abs(dy) + abs(dx) + (1 - planes)
                count = len(rows) * len(cols) * (1 + planes)
                weight = REACT * count * 2.0 ** (3 - differ) / 27.0
                if differ >= 2:
                    total = sum(layer4[2 * a + b] for a in rows for b in cols)
                    found[dy, dx] = (-1.0 / 6.0) * total + weight
                elif differ == 1:
                    found[dy, dx] = weight
        return found

    level = {key: damp * value for key, value in stencil(both4, 1).items()}
    from_above = {key: damp_down * value for key, value in stencil(under4, 0).items()}
    from_below = {key: damp_up * value for key, value in stencil(over4, 0).items()}

    def coarse(copies, turn):
        for copy in copies:
            copy.wait_recv()
        arrived = [rest[turn, m] for m in range(2 * REACH + 1)]
        target = jnp.concatenate([block[0:1] for block in arrived[1:]], 0) + jnp.concatenate(
            [block[1:2] for block in arrived[:-1]], 0
        )
        start = -damp * target
        vert = start
        for _ in range(3):
            along = {0: vert, 1: roll_x(vert, -1), -1: roll_x(vert, 1)}
            spread = {}
            for dx, value in along.items():
                spread[0, dx] = value
                spread[1, dx] = roll_y(value, -1)
                spread[-1, dx] = roll_y(value, 1)
            total = start + (1.0 - OMEGA) * vert
            total += sum(level[key] * spread[key] for key in level)
            total += down(sum(from_above[key] * spread[key] for key in from_above))
            total += up(sum(from_below[key] * spread[key] for key in from_below))
            vert = total
        one = roll_x(vert, -1)
        corners = [vert, one, roll_y(vert, -1), roll_y(one, -1)]
        return jnp.concatenate(
            [c[REACH - 1 : REACH] for c in corners] + [c[REACH : REACH + 1] for c in corners], 0
        )

    column = jnp.broadcast_to(kap[REACH], (8, ROWS)).T
    coeff_ref[...] = jnp.broadcast_to(column[:, 0:1], (ROWS, 128))
    around = []
    for m in (REACH - 1, REACH, REACH + 1):
        layer = jnp.broadcast_to(kap[m], (8, ROWS))
        side = {0: layer, 1: roll_x(layer, -1), -1: roll_x(layer, 1)}
        for dy in (-1, 0, 1):
            for dx in (-1, 0, 1):
                around.append(side[dx] if dy == 0 else roll_y(side[dx], -dy))
    around = jnp.concatenate([a[0:1] for a in around] + [jnp.zeros((5, ROWS), F32)], 0)
    inverse_ref[...] = 1.0 / (dot(around.T, share_ref[...]) + fixed_ref[...])

    def apply(value_ref, target_ref):
        product = dot(value_ref[...], stiff_ref[...])
        for tile in range(4):
            at = pl.ds(128 * tile, 128)
            target_ref[:, at] = (
                coeff_ref[...] * product[:, 128 * tile : 128 * tile + 128]
                + mass_ref[:, at] * value_ref[:, at]
            )
        return target_ref[...]

    def total(value):
        return jnp.sum(value.reshape(ROWS // 8, 8, 4, 128), axis=(0, 2))

    join(edge_copies[0], 0, r0_ref)
    corners = coarse(rest_copies[0], 0)
    z0_ref[...] = r0_ref[...] * inverse_ref[...] + dot(corners.T, prolong)
    z0 = z0_ref[...]
    partial = [total(load * z0)]
    image = apply(z0_ref, q_ref)
    rest_copies.append(restrict(image, 1))
    edge_copies.append(faces(image, 1, q_ref))
    partial.append(total(image * z0))
    join(edge_copies[1], 1, q_ref)
    corners = coarse(rest_copies[1], 1)
    y_ref[...] = q_ref[...] * inverse_ref[...] + dot(corners.T, prolong)
    y = y_ref[...]
    partial.append(total(image * y))
    image = apply(y_ref, w_ref)
    partial.append(total(image * y))

    which = lax.broadcasted_iota(jnp.int32, (8, 128), 0)
    sums = jnp.zeros((8, 128), F32)
    for index, value in enumerate(partial):
        sums = jnp.where(which == index, jnp.sum(value, axis=0, keepdims=True), sums)
    sum_a[0] = sums
    a_copies = [
        remote(sum_a.at[0], sum_a.at[by], a_send.at[by], a_recv.at[by], group_mate(by))
        for by in range(1, GROUP)
    ]
    for copy in a_copies:
        copy.start()
    edge_copies.append(faces(image, 2, w_ref))
    for copy in a_copies:
        copy.wait_recv()
    sum_b[0] = sum(sum_a[by] for by in range(GROUP))
    b_copies = [
        remote(sum_b.at[0], sum_b.at[by], b_send.at[by], b_recv.at[by], far_mate(by))
        for by in range(1, groups)
    ]
    for copy in b_copies:
        copy.start()
    join(edge_copies[2], 2, w_ref)
    for copy in b_copies:
        copy.wait_recv()
    sums = jnp.sum(sum(sum_b[by] for by in range(groups)), axis=1, keepdims=True)
    rz, zq, qy, yw = (sums[index : index + 1] for index in range(4))
    first = rz / zq
    gamma = first * first * qy - rz
    grown = 1.0 + gamma / rz
    second = gamma / (grown * grown * zq - 2.0 * first * grown * qy + first * first * yw)
    straight, bent = first + second * grown, first * second
    solution_ref[...] = permuted(back16, straight * z0_ref[...] - bent * y_ref[...])
    residual_ref[...] = permuted(
        back16, r0_ref[...] - straight * q_ref[...] + bent * w_ref[...]
    )

    for copies in [kap_copies, a_copies, b_copies] + rest_copies + edge_copies:
        for copy in copies:
            copy.wait_send()


def per_device(size, forcing, kappa, elem_order):
    full_stiff, mass_nodes, prolong = element_tables()
    share, fixed = diagonal_tables(full_stiff, mass_nodes)
    tables = [full_stiff, REACT * mass_nodes[None, :], prolong.T, share, fixed]
    groups = size // GROUP
    field = jax.ShapeDtypeStruct((ROWS, NODES), F32)
    count = 2 * REACH + 1
    dma = pltpu.SemaphoreType.DMA
    return pl.pallas_call(
        functools.partial(kernel, size),
        out_shape=(field, field),
        in_specs=[pl.BlockSpec(memory_space=pltpu.VMEM)] * 8,
        out_specs=(pl.BlockSpec(memory_space=pltpu.VMEM),) * 2,
        scratch_shapes=[pltpu.VMEM((ROWS, NODES), F32)] * 6
        + [
            pltpu.VMEM((ROWS, 128), F32),
            pltpu.VMEM((3, 2, 128, 128), F32),
            pltpu.VMEM((3, 2, 128, 128), F32),
            pltpu.VMEM((count, 1, ROWS), F32),
            pltpu.VMEM((2, count, 2, ROWS), F32),
            pltpu.VMEM((GROUP, 8, 128), F32),
            pltpu.VMEM((groups, 8, 128), F32),
            dma((count,)),
            dma((count,)),
            dma((2, count)),
            dma((2, count)),
            dma((3, 2)),
            dma((3, 2)),
            dma((GROUP,)),
            dma((GROUP,)),
            dma((groups,)),
            dma((groups,)),
        ],
        compiler_params=pltpu.CompilerParams(
            collective_id=0, has_side_effects=True, vmem_limit_bytes=48 * 1024 * 1024
        ),
    )(
        forcing,
        kappa.reshape(1, ROWS),
        elem_order,
        *[jnp.asarray(table, F32) for table in tables],
    )


def solution(mesh):
    in_specs = (P(("elem", "face"), None), P(("elem", "face")), P(("elem", "face"), None))
    out_specs = (P(("elem", "face"), None), P(("elem", "face"), None))
    size = mesh.shape["elem"] * mesh.shape["face"]
    return jax.shard_map(
        functools.partial(per_device, size),
        mesh=mesh,
        in_specs=in_specs,
        out_specs=out_specs,
        check_vma=False,
    )
```

```python
import functools

import jax
import jax.numpy as jnp
import numpy as np
from jax import lax
from jax.experimental import pallas as pl
from jax.experimental.pallas import tpu as pltpu
from jax.sharding import PartitionSpec as P

EX = 8
EY = 32
ROWS = EX * EY
NODES = 512
REACT = 0.02
OMEGA = 0.6
REACH = 8
NEAR = 4
PIECES = ((0, 0), (0, 1), (0, 2), (1, 0), (1, 1), (2, 0))
MESH = pl.DeviceIdType.MESH
F32 = jnp.float32
BF16 = jnp.bfloat16


def legendre_seven(points):
    before = np.ones(8)
    current = np.array(points)
    for degree in range(1, 7):
        following = ((2 * degree + 1) * points * current - degree * before) / (degree + 1)
        before = current
        current = following
    return current


def element_tables():
    points = np.array(
        [
            -1.0,
            -0.8717401485096066,
            -0.5917001814331423,
            -0.2092992179024789,
            0.2092992179024789,
            0.5917001814331423,
            0.8717401485096066,
            1.0,
        ]
    )
    weights = np.array(
        [
            1.0 / 28.0,
            0.2107042271435061,
            0.3411226924835044,
            0.4124587946587038,
            0.4124587946587038,
            0.3411226924835044,
            0.2107042271435061,
            1.0 / 28.0,
        ]
    )
    legendre = legendre_seven(points)
    derivative = np.zeros((8, 8))
    for left_node in range(8):
        for right_node in range(8):
            if left_node != right_node:
                derivative[left_node, right_node] = legendre[left_node] / (
                    legendre[right_node] * (points[left_node] - points[right_node])
                )
    derivative[0, 0] = -14.0
    derivative[7, 7] = 14.0
    stiffness = derivative.T @ (weights[:, None] * derivative)
    mass = np.eye(8) * weights[None, :]
    full_stiff = (
        np.kron(np.kron(mass, mass), stiffness)
        + np.kron(np.kron(mass, stiffness), mass)
        + np.kron(np.kron(stiffness, mass), mass)
    )
    mass_nodes = np.kron(np.kron(weights, weights), weights)
    interp = np.stack([(1.0 - points) / 2.0, (1.0 + points) / 2.0], 1)
    prolong = np.kron(np.kron(interp, interp), interp)
    return full_stiff, mass_nodes, prolong


def pieces_of(table, count):
    parts = []
    for _ in range(count):
        part = table.astype(BF16).astype(np.float64)
        parts.append(part)
        table = table - part
    return parts


def ends(offset):
    if offset == 0:
        return list(range(8)), list(range(8))
    return ([7], [0]) if offset == 1 else ([0], [7])


def all_tables():
    full_stiff, mass_nodes, prolong = element_tables()
    face = np.concatenate([np.arange(64), np.arange(448, 512)])
    facing = np.concatenate([np.arange(448, 512), np.arange(64)])
    diag = np.diag(full_stiff).reshape(8, 8, 8)
    mass = mass_nodes.reshape(8, 8, 8)
    share = np.zeros((16, 8, 8, 8))
    fixed = np.zeros((8, 8, 8))
    for index in range(9):
        offsets = (0, index // 3 - 1, index % 3 - 1)
        mine = np.ix_(*[ends(offset)[0] for offset in offsets])
        theirs = np.ix_(*[ends(offset)[1] for offset in offsets])
        share[index][mine] += diag[theirs]
        fixed[mine] += REACT * mass[theirs]
    share, fixed = share.reshape(16, NODES), fixed.reshape(NODES)
    fixed_face = 2.0 * fixed[face]
    share_face = np.zeros((48, 128))
    share_face[0:16] = share[:, face]
    share_face[16:32, :64] = share[:, facing[:64]]
    share_face[32:48, 64:] = share[:, facing[64:]]

    steep = full_stiff @ prolong
    heavy = REACT * mass_nodes[:, None] * prolong

    def stacked(table):
        parts = pieces_of(table, 3)
        return np.concatenate([parts[right] for _, right in PIECES], 0)

    spread = stacked(np.concatenate([prolong.T, steep.T], 1))
    facing_tables = np.concatenate([steep[facing].T, heavy[facing].T], 1)
    lower = facing_tables.copy()
    lower[:, 64:128] = 0.0
    lower[:, 192:256] = 0.0
    spread_face = np.concatenate([stacked(lower), stacked(facing_tables - lower)], 0)

    gather = pieces_of(np.concatenate([steep.T, heavy.T], 0), 2)
    gather = np.concatenate(gather, 0)
    first = np.concatenate(pieces_of(prolong.T, 2), 0)
    return {
        "stiff": full_stiff,
        "spread": spread,
        "spread_face": spread_face,
        "gather": np.concatenate([gather, first], 0),
        "share": share,
        "share_face": share_face,
        "rows": np.concatenate(
            [
                np.stack([fixed, REACT * mass_nodes]),
                np.pad(np.stack([fixed_face, REACT * mass_nodes[face]]), ((0, 0), (0, 384))),
            ],
            0,
        ),
    }


def split(value, pieces):
    parts = []
    for _ in range(pieces):
        part = value.astype(BF16)
        parts.append(part)
        value = value - part.astype(F32)
    return parts


def dot(left, right, dims=((1,), (0,))):
    return lax.dot_general(
        left, right, (dims, ((), ())), precision=lax.Precision.HIGHEST, preferred_element_type=F32
    )


def dot16(left, right, dims=((1,), (0,))):
    return lax.dot_general(left, right, (dims, ((), ())), preferred_element_type=F32)


def lanes(shape):
    return lax.broadcasted_iota(jnp.int32, shape, len(shape) - 1)


def roll_x(plane, by):
    size = plane.shape[1]
    along = lanes(plane.shape) % EX
    inside = pltpu.roll(plane, by % size, 1)
    around = pltpu.roll(plane, (by - EX * by) % size, 1)
    return jnp.where(along == (0 if by == 1 else EX - 1), around, inside)


def roll_y(plane, by):
    return pltpu.roll(plane, (by * EX) % plane.shape[1], 1)


def down(plane):
    return pltpu.roll(plane, plane.shape[0] - 1, 0)


def up(plane):
    return pltpu.roll(plane, 1, 0)


def shared_xy(tile):
    cube = tile.reshape(EY, EX, 128)
    lane = lanes(cube.shape)
    nx, ny = lane % 8, lane // 8 % 8
    after = pltpu.roll(pltpu.roll(cube, EX - 1, 1), 7, 2)
    before = pltpu.roll(pltpu.roll(cube, 1, 1), 128 - 7, 2)
    cube = cube + jnp.where(nx == 7, after, jnp.where(nx == 0, before, 0.0))
    after = pltpu.roll(jnp.concatenate([cube[1:], cube[:1]], 0), 56, 2)
    before = pltpu.roll(jnp.concatenate([cube[-1:], cube[:-1]], 0), 128 - 56, 2)
    cube = cube + jnp.where(ny == 7, after, jnp.where(ny == 0, before, 0.0))
    return cube.reshape(ROWS, 128)


def four(layer):
    moved = [layer, roll_x(layer, 1)]
    return moved + [roll_y(moved[0], 1), roll_y(moved[1], 1)]


def nine(layer):
    side = {0: layer, 1: roll_x(layer, -1), -1: roll_x(layer, 1)}
    return [
        side[dx] if dy == 0 else roll_y(side[dx], -dy) for dy in (-1, 0, 1) for dx in (-1, 0, 1)
    ]


def coarse_stencil(layer4, planes):
    found = {}
    for dy in (-1, 0, 1):
        for dx in (-1, 0, 1):
            rows = (0, 1) if dy == 0 else ((0,) if dy == 1 else (1,))
            cols = (0, 1) if dx == 0 else ((0,) if dx == 1 else (1,))
            differ = abs(dy) + abs(dx) + (1 - planes)
            count = len(rows) * len(cols) * (1 + planes)
            weight = REACT * count * 2.0 ** (3 - differ) / 27.0
            if differ >= 2:
                total = sum(layer4[2 * a + b] for a in rows for b in cols)
                found[dy, dx] = (-1.0 / 6.0) * total + weight
            elif differ == 1:
                found[dy, dx] = weight
    return found


def swept(vert, level, from_above, from_below):
    along = {0: vert, 1: roll_x(vert, -1), -1: roll_x(vert, 1)}
    spread = {}
    for dx, value in along.items():
        spread[0, dx] = value
        spread[1, dx] = roll_y(value, -1)
        spread[-1, dx] = roll_y(value, 1)
    total = (1.0 - OMEGA) * vert
    total += sum(level[key] * spread[key] for key in level)
    total += down(sum(from_above[key] * spread[key] for key in from_above))
    total += up(sum(from_below[key] * spread[key] for key in from_below))
    return total


NAMES = (
    "stiff",
    "spread",
    "spread_face",
    "gather",
    "share",
    "share_face",
    "rows",
)
FIELDS = ("load", "r0", "x0", "z0", "q", "qloc", "x1", "y", "w", "inverse", "stiffened")


def kernel(size, *refs):
    refs = list(refs)

    def take(count):
        taken = refs[:count]
        del refs[:count]
        return taken

    sources = take(3 + len(NAMES))
    solution_ref, residual_ref = take(2)
    inputs = take(3 + len(NAMES))
    forcing_ref, kappa_ref, order_ref = inputs[:3]
    table = dict(zip(NAMES, inputs[3:]))
    field = dict(zip(FIELDS, take(len(FIELDS))))
    coeff_ref, sent_z0, sent_q, sent_r0, sent_y, sent_w = take(6)
    stiff_ref, stiff_face_ref = take(2)
    edge_out, edge_in, halo, rest, sums_ref = take(5)
    in_sem, halo_send, halo_recv, rest_send, rest_recv = take(5)
    edge_send, edge_recv, sum_send, sum_recv = take(4)

    me = lax.axis_index("elem") * 2 + lax.axis_index("face")

    def ring(by):
        device = lax.rem(me + by + size, size)
        return lax.div(device, 2), lax.rem(device, 2)

    barrier = pltpu.get_barrier_semaphore()

    def greet(by, carry):
        pl.semaphore_signal(barrier, inc=1, device_id=ring(by), device_id_type=MESH)
        return carry

    loads = [
        pltpu.make_async_copy(source, target, in_sem.at[index])
        for index, (source, target) in enumerate(zip(sources, inputs))
    ]
    for index in (2, 1, 0, *range(len(loads) - 1, 2, -1)):
        loads[index].start()
    lax.fori_loop(1, size, greet, 0)

    def remote(source, target, send, recv, device):
        return pltpu.make_async_remote_copy(
            src_ref=source,
            dst_ref=target,
            send_sem=send,
            recv_sem=recv,
            device_id=device,
            device_id_type=MESH,
        )

    def to_ring(buffer, send, recv, reach):
        found = {}
        for by in sorted(range(-reach, reach + 1), key=abs):
            if by != 0:
                at = reach - by
                found[by] = remote(buffer.at[reach], buffer.at[at], send.at[at], recv.at[at], ring(by))
        return found

    half = lanes((ROWS, 128)) < 64

    def tile(ref, index):
        return ref[:, 128 * index : 128 * index + 128]

    def put(ref, index, value):
        ref[:, 128 * index : 128 * index + 128] = value

    def face_of(ref):
        return jnp.where(half, tile(ref, 0), tile(ref, 3))

    def put_face(ref, value):
        put(ref, 0, jnp.where(half, value, tile(ref, 0)))
        put(ref, 3, jnp.where(half, tile(ref, 3), value))

    def send_faces(face, turn):
        top, bottom, part = face[0:128], face[128:256], half[0:128]
        edge_out[turn, 0] = jnp.where(part, pltpu.roll(top, 64, 1), bottom)
        edge_out[turn, 1] = jnp.where(part, top, pltpu.roll(bottom, 64, 1))
        copies = [
            remote(
                edge_out.at[turn, way],
                edge_in.at[turn, way],
                edge_send.at[turn, way],
                edge_recv.at[turn, way],
                ring(by),
            )
            for way, by in ((0, 1), (1, -1))
        ]
        for copy in copies:
            copy.start()
        return copies

    def faces_arrived(copies, turn):
        for copy in copies:
            copy.wait_recv()
        below, above, part = edge_in[turn, 0], edge_in[turn, 1], half[0:128]
        top = jnp.where(part, below, pltpu.roll(above, 64, 1))
        bottom = jnp.where(part, pltpu.roll(below, 64, 1), above)
        return jnp.concatenate([top, bottom], 0)

    def vertex_sums(each):
        corner = lax.broadcasted_iota(jnp.int32, each.shape, 0)
        each = jnp.where(corner % 2 == 1, roll_x(each, 1), each)
        each = jnp.where(corner // 2 % 2 == 1, roll_y(each, 1), each)
        low = jnp.sum(each[0:4], axis=0, keepdims=True)
        high = jnp.sum(each[4:8], axis=0, keepdims=True)
        return low, high

    def gathered(matrix, parts):
        whole = dot16(matrix, parts[0], ((1,), (1,)))
        return whole[0:16] + whole[16:32] + dot16(matrix[0:16], parts[1], ((1,), (1,)))

    def face_lanes(value):
        return jnp.concatenate([value[:, 0:64], value[:, 448:512]], 1)

    def columns(planes):
        return jnp.concatenate(planes, 0).T

    def corner_pieces(corners):
        parts = [part.astype(F32) for part in split(corners, 3)]
        return [parts[left] for left, _ in PIECES]

    row = lax.broadcasted_iota(jnp.int32, (ROWS, ROWS), 0)
    loads[2].wait()
    pick = jnp.where(row == order_ref[...], 1.0, 0.0)
    pick16 = pick.astype(BF16)
    loads[1].wait()
    kappa_rows = jnp.broadcast_to(kappa_ref[...], (16, ROWS))
    kappa = sum(dot16(part, pick16, ((1,), (1,))) for part in split(kappa_rows, 3))[0:8]
    halo[REACH, 2:3] = kappa[0:1]
    loads[0].wait()
    load_ref, r0_ref = field["load"], field["r0"]
    load_ref[...] = sum(dot16(pick16, part) for part in split(forcing_ref[...], 3))
    put(r0_ref, 0, shared_xy(tile(load_ref, 0)))
    put(r0_ref, 3, shared_xy(tile(load_ref, 3)))
    for copy in loads[3:]:
        copy.wait()
    parts = split(load_ref[...], 2)
    gather = table["gather"][0:32].astype(BF16)
    gather_face = face_lanes(gather)
    first = table["gather"][32:48].astype(BF16)
    each = dot16(first, parts[0], ((1,), (1,)))
    each = each[0:8] + each[8:16] + dot16(first, parts[1], ((1,), (1,)))[0:8]
    low, high = vertex_sums(each)
    halo[REACH, 0:1] = low
    halo[REACH, 1:2] = high
    stiff = table["stiff"][...]
    upper_piece = stiff.astype(BF16)
    stiff_ref[0:NODES] = upper_piece
    stiff_ref[NODES:] = (stiff - upper_piece.astype(F32)).astype(BF16)
    for at, piece in ((0, 0), (128, 0), (256, NODES)):
        stiff_face_ref[at : at + 64] = stiff_ref[piece : piece + 64]
        stiff_face_ref[at + 64 : at + 128] = stiff_ref[piece + 448 : piece + 512]
    stiff_face_face = face_lanes(stiff_face_ref[...])
    spread_table = table["spread"][...].astype(BF16)
    spread_face_table = table["spread_face"][...].astype(BF16)
    pl.semaphore_wait(barrier, size - 1)
    halo_copies = to_ring(halo, halo_send, halo_recv, REACH)
    halo_copies[1].start()
    halo_copies[-1].start()
    edges = [send_faces(face_of(r0_ref), 0)]
    for by, copy in halo_copies.items():
        if abs(by) > 1:
            copy.start()

    put(r0_ref, 1, shared_xy(tile(load_ref, 1)))
    put(r0_ref, 2, shared_xy(tile(load_ref, 2)))
    own9 = nine(kappa)
    own_rows = [plane[0:1] for plane in own9] + [jnp.zeros((7, ROWS), F32)]
    own_columns = columns(own_rows)
    coeff_ref[...] = jnp.broadcast_to(own_columns[:, 4:5], (ROWS, 128))
    fixed, mass = table["rows"][0:1], table["rows"][1:2]
    fixed_face, mass_face = table["rows"][2:3, 0:128], table["rows"][3:4, 0:128]
    field["inverse"][...] = 1.0 / (dot(own_columns, table["share"][...]) + fixed)
    back16 = pick.T.astype(BF16)

    def interior(value, x_ref):
        inverse = field["inverse"]
        zero = jnp.zeros((ROWS, 128), F32)
        put(x_ref, 0, jnp.where(half, zero, tile(inverse, 0) * tile(value, 0)))
        put(x_ref, 1, tile(inverse, 1) * tile(value, 1))
        put(x_ref, 2, tile(inverse, 2) * tile(value, 2))
        put(x_ref, 3, jnp.where(half, tile(inverse, 3) * tile(value, 3), zero))
        parts = split(x_ref[...], 2)
        high, low = stiff_ref[0:NODES], stiff_ref[NODES:]
        field["stiffened"][...] = (
            dot16(parts[0], high) + dot16(parts[1], high) + dot16(parts[0], low)
        )
        return gathered(gather, parts)

    inner_rows = interior(r0_ref, field["x0"])

    for by in (1, -1):
        halo_copies[by].wait_recv()
    below9 = nine(jnp.broadcast_to(halo[REACH - 1, 2:3], (8, ROWS)))
    above9 = nine(jnp.broadcast_to(halo[REACH + 1, 2:3], (8, ROWS)))
    pad = [jnp.zeros((7, ROWS), F32)]
    three = columns(
        own_rows + [p[0:1] for p in below9] + pad + [p[0:1] for p in above9] + pad
    )
    inverse_face = 1.0 / (dot(three, table["share_face"][...]) + fixed_face)
    coeff_beside = jnp.where(half, three[:, 20:21], three[:, 36:37])
    coeff = coeff_ref[...]
    face = face_of(r0_ref) + faces_arrived(edges[0], 0)
    put_face(r0_ref, face)

    def outer(face, x_ref, rows):
        x_face = inverse_face * face
        put_face(x_ref, x_face)
        parts = split(x_face, 2)
        rows = rows + gathered(gather_face, parts)
        return x_face, jnp.concatenate([parts[0], parts[1], parts[0]], 1), rows

    x_face, stacked, rows0 = outer(face, field["x0"], inner_rows)
    rough = coeff * (
        face_of(field["stiffened"]) + dot16(stacked, stiff_face_face)
    ) + mass_face * x_face
    edges.append(send_faces(shared_xy(rough), 1))
    low, high = vertex_sums(kappa * rows0[0:8] + rows0[8:16])
    rest[NEAR, 0:1] = low
    rest[NEAR, 1:2] = high
    rest_copies = to_ring(rest, rest_send, rest_recv, NEAR)
    for copy in rest_copies.values():
        copy.start()

    field["stiffened"][...] += dot16(stacked, stiff_face_ref[...])
    for by, copy in halo_copies.items():
        if abs(by) > 1:
            copy.wait_recv()
    planes = list(range(-3, REACH + 1)) + list(range(1 - REACH, -3))

    def halo_rows(shift, which):
        return jnp.concatenate([halo[REACH + p + shift, which : which + 1] for p in planes], 0)

    under4, over4 = four(halo_rows(-1, 2)), four(halo_rows(0, 2))
    both4 = [a + b for a, b in zip(under4, over4)]
    diag = (2.0 / 3.0) * (both4[0] + both4[1] + both4[2] + both4[3]) + REACT * 64.0 / 27.0
    damp = -OMEGA / diag
    damp_down, damp_up = up(damp), down(damp)
    level = {key: damp * value for key, value in coarse_stencil(both4, 1).items()}
    from_above = {key: damp_down * value for key, value in coarse_stencil(under4, 0).items()}
    from_below = {key: damp_up * value for key, value in coarse_stencil(over4, 0).items()}
    start = -damp * (halo_rows(0, 0) + halo_rows(-1, 1))
    vert = start
    for _ in range(3):
        vert = start + swept(vert, level, from_above, from_below)
    remainder = (vert - swept(vert, level, from_above, from_below))[0:8]

    def corners_of(vert, lower):
        one = roll_x(vert, -1)
        found = [vert, one, roll_y(vert, -1), roll_y(one, -1)]
        return [
            jnp.concatenate(
                [c[k : k + 1] for c in found] + [c[k + 1 : k + 2] for c in found], 0
            )
            for k in lower
        ]

    own, under, over = corners_of(vert[0:8], (3, 2, 4))
    spread = dot16(columns(corner_pieces(own)).astype(BF16), spread_table)
    beside = dot16(
        columns(corner_pieces(under) + corner_pieces(over)).astype(BF16),
        spread_face_table,
    )
    beside = shared_xy(coeff_beside * beside[:, 0:128] + beside[:, 128:256])

    def total(value):
        return jnp.sum(jnp.sum(value.reshape(ROWS // 8, 8, 128), axis=0), axis=(0, 1), keepdims=True)

    def applied(x_ref, spread, z_ref, image_ref):
        for index in range(4):
            at = 128 * index
            z = tile(x_ref, index) + spread[:, at : at + 128]
            put(z_ref, index, z)
            put(
                image_ref,
                index,
                coeff * (tile(field["stiffened"], index) + spread[:, 512 + at : 640 + at])
                + mass[:, at : at + 128] * z,
            )

    def inner(left, right):
        return total(sum(tile(left, index) * tile(right, index) for index in range(4)))

    applied(field["x0"], spread, field["z0"], field["qloc"])
    rz = inner(load_ref, field["z0"])
    zq = inner(field["qloc"], field["z0"])
    for index in range(4):
        put(field["q"], index, shared_xy(tile(field["qloc"], index)))
    partial_face = face_of(field["q"]) + beside
    inner_rows = interior(field["q"], field["x1"])

    face = partial_face + faces_arrived(edges[1], 1)
    put_face(field["q"], face)
    x_face, stacked, _ = outer(face, field["x1"], inner_rows)
    field["stiffened"][...] += dot16(stacked, stiff_face_ref[...])
    for copy in rest_copies.values():
        copy.wait_recv()
    target = jnp.concatenate([rest[NEAR + p, 0:1] for p in range(-3, 5)], 0) + jnp.concatenate(
        [rest[NEAR + p - 1, 1:2] for p in range(-3, 5)], 0
    )

    def top(parts):
        return {key: value[0:8] for key, value in parts.items()}

    level, from_above, from_below = top(level), top(from_above), top(from_below)
    start = remainder - damp[0:8] * target
    vert = start
    for _ in range(3):
        vert = start + swept(vert, level, from_above, from_below)
    (own,) = corners_of(vert, (3,))
    spread = dot16(columns(corner_pieces(own)).astype(BF16), spread_table)
    applied(field["x1"], spread, field["y"], field["w"])
    qy = inner(field["qloc"], field["y"])
    yw = inner(field["w"], field["y"])

    lane = lanes((1, 128))
    mine = jnp.zeros((1, 128), F32)
    for index, value in enumerate((rz, zq, qy, yw)):
        mine = jnp.where(lane == index, value, mine)
    sums_ref[0] = mine

    def spread_sums(by, carry):
        remote(sums_ref.at[0], sums_ref.at[by], sum_send, sum_recv, ring(by)).start()
        return carry

    lax.fori_loop(1, size, spread_sums, 0)
    put(field["w"], 0, shared_xy(tile(field["w"], 0)))
    put(field["w"], 3, shared_xy(tile(field["w"], 3)))
    edges.append(send_faces(face_of(field["w"]), 2))
    put(field["w"], 1, shared_xy(tile(field["w"], 1)))
    put(field["w"], 2, shared_xy(tile(field["w"], 2)))

    def stored(value):
        return sum(dot16(back16, part) for part in split(value, 3))

    sent_z0[...] = stored(field["z0"][...])
    sent_y[...] = stored(field["y"][...])
    sent_r0[...] = stored(r0_ref[...])
    sent_q[...] = stored(field["q"][...])
    face = face_of(field["w"]) + faces_arrived(edges[2], 2)
    put_face(field["w"], face)
    sent_w[...] = stored(field["w"][...])
    others = sums_ref.at[pl.ds(1, size - 1)]
    all_sums = remote(others, others, sum_send, sum_recv, ring(1))
    all_sums.wait_recv()
    sums = jnp.sum(sums_ref[...], axis=0)
    rz, zq, qy, yw = (sums[:, index : index + 1] for index in range(4))
    first = rz / zq
    gamma = first * first * qy - rz
    grown = 1.0 + gamma / rz
    second = gamma / (grown * grown * zq - 2.0 * first * grown * qy + first * first * yw)
    straight, bent = first + second * grown, first * second
    solution_ref[...] = straight * sent_z0[...] - bent * sent_y[...]
    residual_ref[...] = sent_r0[...] - straight * sent_q[...] + bent * sent_w[...]

    all_sums.wait_send()
    for copies in [halo_copies.values(), rest_copies.values()] + edges:
        for copy in copies:
            copy.wait_send()


def per_device(size, forcing, kappa, elem_order):
    tables = all_tables()
    operands = [forcing, kappa.reshape(1, ROWS), elem_order]
    operands += [jnp.asarray(tables[name], F32) for name in NAMES]
    out = jax.ShapeDtypeStruct((ROWS, NODES), F32)
    count, close = 2 * REACH + 1, 2 * NEAR + 1
    dma = pltpu.SemaphoreType.DMA
    return pl.pallas_call(
        functools.partial(kernel, size),
        out_shape=(out, out),
        in_specs=[pl.BlockSpec(memory_space=pl.ANY)] * len(operands),
        out_specs=(pl.BlockSpec(memory_space=pltpu.VMEM),) * 2,
        scratch_shapes=[pltpu.VMEM(operand.shape, operand.dtype) for operand in operands]
        + [pltpu.VMEM((ROWS, NODES), F32)] * len(FIELDS)
        + [pltpu.VMEM((ROWS, 128), F32)]
        + [pltpu.VMEM((ROWS, NODES), F32)] * 5
        + [pltpu.VMEM((2 * NODES, NODES), BF16), pltpu.VMEM((384, NODES), BF16)]
        + [
            pltpu.VMEM((3, 2, 128, 128), F32),
            pltpu.VMEM((3, 2, 128, 128), F32),
            pltpu.VMEM((count, 3, ROWS), F32),
            pltpu.VMEM((close, 2, ROWS), F32),
            pltpu.VMEM((size, 1, 128), F32),
            dma((len(operands),)),
            dma((count,)),
            dma((count,)),
            dma((close,)),
            dma((close,)),
            dma((3, 2)),
            dma((3, 2)),
            dma,
            dma,
        ],
        compiler_params=pltpu.CompilerParams(
            collective_id=0, has_side_effects=True, vmem_limit_bytes=56 * 1024 * 1024
        ),
    )(*operands)


def solution(mesh):
    in_specs = (P(("elem", "face"), None), P(("elem", "face")), P(("elem", "face"), None))
    out_specs = (P(("elem", "face"), None), P(("elem", "face"), None))
    size = mesh.shape["elem"] * mesh.shape["face"]
    return jax.shard_map(
        functools.partial(per_device, size),
        mesh=mesh,
        in_specs=in_specs,
        out_specs=out_specs,
        check_vma=False,
    )
```

```python
import functools

import jax
import jax.numpy as jnp
import numpy as np
from jax import lax
from jax.experimental import pallas as pl
from jax.experimental.pallas import tpu as pltpu
from jax.sharding import PartitionSpec as P

EX = 8
EY = 32
ROWS = EX * EY
NODES = 512
REACT = 0.02
OMEGA = 0.6
REACH = 8
NEAR = 4
PARTS = 4
PIECES = ((0, 0), (0, 1), (0, 2), (1, 0), (1, 1), (2, 0))
MESH = pl.DeviceIdType.MESH
F32 = jnp.float32
BF16 = jnp.bfloat16


def legendre_seven(points):
    before = np.ones(8)
    current = np.array(points)
    for degree in range(1, 7):
        following = ((2 * degree + 1) * points * current - degree * before) / (degree + 1)
        before = current
        current = following
    return current


def element_tables():
    points = np.array(
        [
            -1.0,
            -0.8717401485096066,
            -0.5917001814331423,
            -0.2092992179024789,
            0.2092992179024789,
            0.5917001814331423,
            0.8717401485096066,
            1.0,
        ]
    )
    weights = np.array(
        [
            1.0 / 28.0,
            0.2107042271435061,
            0.3411226924835044,
            0.4124587946587038,
            0.4124587946587038,
            0.3411226924835044,
            0.2107042271435061,
            1.0 / 28.0,
        ]
    )
    legendre = legendre_seven(points)
    derivative = np.zeros((8, 8))
    for left_node in range(8):
        for right_node in range(8):
            if left_node != right_node:
                derivative[left_node, right_node] = legendre[left_node] / (
                    legendre[right_node] * (points[left_node] - points[right_node])
                )
    derivative[0, 0] = -14.0
    derivative[7, 7] = 14.0
    stiffness = derivative.T @ (weights[:, None] * derivative)
    mass = np.eye(8) * weights[None, :]
    full_stiff = (
        np.kron(np.kron(mass, mass), stiffness)
        + np.kron(np.kron(mass, stiffness), mass)
        + np.kron(np.kron(stiffness, mass), mass)
    )
    mass_nodes = np.kron(np.kron(weights, weights), weights)
    interp = np.stack([(1.0 - points) / 2.0, (1.0 + points) / 2.0], 1)
    prolong = np.kron(np.kron(interp, interp), interp)
    return full_stiff, mass_nodes, prolong


def pieces_of(table, count):
    parts = []
    for _ in range(count):
        part = table.astype(BF16).astype(np.float64)
        parts.append(part)
        table = table - part
    return parts


def ends(offset):
    if offset == 0:
        return list(range(8)), list(range(8))
    return ([7], [0]) if offset == 1 else ([0], [7])


def all_tables():
    full_stiff, mass_nodes, prolong = element_tables()
    face = np.concatenate([np.arange(64), np.arange(448, 512)])
    facing = np.concatenate([np.arange(448, 512), np.arange(64)])
    diag = np.diag(full_stiff).reshape(8, 8, 8)
    mass = mass_nodes.reshape(8, 8, 8)
    share = np.zeros((16, 8, 8, 8))
    fixed = np.zeros((8, 8, 8))
    for index in range(9):
        offsets = (0, index // 3 - 1, index % 3 - 1)
        mine = np.ix_(*[ends(offset)[0] for offset in offsets])
        theirs = np.ix_(*[ends(offset)[1] for offset in offsets])
        share[index][mine] += diag[theirs]
        fixed[mine] += REACT * mass[theirs]
    share, fixed = share.reshape(16, NODES), fixed.reshape(NODES)
    fixed_face = 2.0 * fixed[face]
    share_face = np.zeros((48, 128))
    share_face[0:16] = share[:, face]
    share_face[16:32, :64] = share[:, facing[:64]]
    share_face[32:48, 64:] = share[:, facing[64:]]

    steep = full_stiff @ prolong
    heavy = REACT * mass_nodes[:, None] * prolong

    def stacked(table):
        parts = pieces_of(table, 3)
        return np.concatenate([parts[right] for _, right in PIECES], 0)

    spread = stacked(np.concatenate([prolong.T, steep.T], 1))
    facing_tables = np.concatenate([steep[facing].T, heavy[facing].T], 1)
    lower = facing_tables.copy()
    lower[:, 64:128] = 0.0
    lower[:, 192:256] = 0.0
    spread_face = np.concatenate([stacked(lower), stacked(facing_tables - lower)], 0)

    gather = pieces_of(np.concatenate([steep.T, heavy.T], 0), 2)
    gather = np.concatenate(gather, 0)
    first = np.concatenate(pieces_of(prolong.T, 2), 0)
    return {
        "stiff": full_stiff,
        "spread": spread,
        "spread_face": spread_face,
        "gather": np.concatenate([gather, first], 0),
        "share": share,
        "share_face": share_face,
        "rows": np.concatenate(
            [
                np.stack([fixed, REACT * mass_nodes]),
                np.pad(np.stack([fixed_face, REACT * mass_nodes[face]]), ((0, 0), (0, 384))),
            ],
            0,
        ),
    }


def split(value, pieces):
    parts = []
    for _ in range(pieces):
        part = value.astype(BF16)
        parts.append(part)
        value = value - part.astype(F32)
    return parts


def dot(left, right, dims=((1,), (0,))):
    return lax.dot_general(
        left, right, (dims, ((), ())), precision=lax.Precision.HIGHEST, preferred_element_type=F32
    )


def dot16(left, right, dims=((1,), (0,))):
    return lax.dot_general(left, right, (dims, ((), ())), preferred_element_type=F32)


def lanes(shape):
    return lax.broadcasted_iota(jnp.int32, shape, len(shape) - 1)


def roll_x(plane, by):
    size = plane.shape[1]
    along = lanes(plane.shape) % EX
    inside = pltpu.roll(plane, by % size, 1)
    around = pltpu.roll(plane, (by - EX * by) % size, 1)
    return jnp.where(along == (0 if by == 1 else EX - 1), around, inside)


def roll_y(plane, by):
    return pltpu.roll(plane, (by * EX) % plane.shape[1], 1)


def down(plane):
    return pltpu.roll(plane, plane.shape[0] - 1, 0)


def up(plane):
    return pltpu.roll(plane, 1, 0)


def shared_xy(tile):
    cube = tile.reshape(EY, EX, 128)
    lane = lanes(cube.shape)
    nx, ny = lane % 8, lane // 8 % 8
    after = pltpu.roll(pltpu.roll(cube, EX - 1, 1), 7, 2)
    before = pltpu.roll(pltpu.roll(cube, 1, 1), 128 - 7, 2)
    cube = cube + jnp.where(nx == 7, after, jnp.where(nx == 0, before, 0.0))
    after = pltpu.roll(jnp.concatenate([cube[1:], cube[:1]], 0), 56, 2)
    before = pltpu.roll(jnp.concatenate([cube[-1:], cube[:-1]], 0), 128 - 56, 2)
    cube = cube + jnp.where(ny == 7, after, jnp.where(ny == 0, before, 0.0))
    return cube.reshape(ROWS, 128)


def four(layer):
    moved = [layer, roll_x(layer, 1)]
    return moved + [roll_y(moved[0], 1), roll_y(moved[1], 1)]


def nine(layer):
    side = {0: layer, 1: roll_x(layer, -1), -1: roll_x(layer, 1)}
    return [
        side[dx] if dy == 0 else roll_y(side[dx], -dy) for dy in (-1, 0, 1) for dx in (-1, 0, 1)
    ]


def coarse_stencil(layer4, planes):
    found = {}
    for dy in (-1, 0, 1):
        for dx in (-1, 0, 1):
            rows = (0, 1) if dy == 0 else ((0,) if dy == 1 else (1,))
            cols = (0, 1) if dx == 0 else ((0,) if dx == 1 else (1,))
            differ = abs(dy) + abs(dx) + (1 - planes)
            count = len(rows) * len(cols) * (1 + planes)
            weight = REACT * count * 2.0 ** (3 - differ) / 27.0
            if differ >= 2:
                total = sum(layer4[2 * a + b] for a in rows for b in cols)
                found[dy, dx] = (-1.0 / 6.0) * total + weight
            elif differ == 1:
                found[dy, dx] = weight
    return found


def swept(vert, level, from_above, from_below):
    along = {0: vert, 1: roll_x(vert, -1), -1: roll_x(vert, 1)}
    spread = {}
    for dx, value in along.items():
        spread[0, dx] = value
        spread[1, dx] = roll_y(value, -1)
        spread[-1, dx] = roll_y(value, 1)
    total = (1.0 - OMEGA) * vert
    total += sum(level[key] * spread[key] for key in level)
    total += down(sum(from_above[key] * spread[key] for key in from_above))
    total += up(sum(from_below[key] * spread[key] for key in from_below))
    return total


NAMES = (
    "stiff",
    "spread",
    "spread_face",
    "gather",
    "share",
    "share_face",
    "rows",
)
FIELDS = ("load", "r0", "x0", "z0", "q", "qloc", "x1", "y", "w", "inverse", "stiffened")


def kernel(size, *refs):
    refs = list(refs)

    def take(count):
        taken = refs[:count]
        del refs[:count]
        return taken

    sources = take(3 + len(NAMES))
    sent_z0, sent_y, sent_r0, sent_q, sent_w, steps_ref = take(6)
    inputs = take(3 + len(NAMES))
    forcing_ref, kappa_ref, order_ref = inputs[:3]
    table = dict(zip(NAMES, inputs[3:]))
    field = dict(zip(FIELDS, take(len(FIELDS))))
    coeff_ref, stiff_ref, stiff_face_ref = take(3)
    edge_out, edge_in, layer, halo, rest, sums_ref = take(6)
    in_sem, layer_send, layer_recv, halo_send, halo_recv = take(5)
    rest_send, rest_recv, edge_send, edge_recv, sum_send, sum_recv, known_sem = take(7)

    me = lax.axis_index("elem") * 2 + lax.axis_index("face")

    def ring(by):
        device = lax.rem(me + by + size, size)
        return lax.div(device, 2), lax.rem(device, 2)

    barrier = pltpu.get_barrier_semaphore()

    loads = [
        pltpu.make_async_copy(source, target, in_sem.at[index])
        for index, (source, target) in enumerate(zip(sources, inputs))
    ]
    for index in (2, 1, 0, *range(len(loads) - 1, 2, -1)):
        loads[index].start()
    greeted = [by for by in range(-REACH, REACH + 1) if by != 0]
    for by in greeted:
        pl.semaphore_signal(barrier, inc=1, device_id=ring(by), device_id_type=MESH)

    stages = []
    while REACH << len(stages) < size // 2:
        stages.append(REACH << len(stages))

    def tell(stage):
        if stage < len(stages):
            for way, by in enumerate((stages[stage], -stages[stage])):
                pl.semaphore_signal(
                    known_sem.at[stage, way], inc=1, device_id=ring(by), device_id_type=MESH
                )

    def hear(stage):
        if stage < len(stages):
            for way in range(2):
                pl.semaphore_wait(known_sem.at[stage, way], 1)

    def remote(source, target, send, recv, device):
        return pltpu.make_async_remote_copy(
            src_ref=source,
            dst_ref=target,
            send_sem=send,
            recv_sem=recv,
            device_id=device,
            device_id_type=MESH,
        )

    def to_ring(buffer, send, recv, reach):
        found = {}
        for by in sorted(range(-reach, reach + 1), key=abs):
            if by != 0:
                at = reach - by
                found[by] = remote(buffer.at[reach], buffer.at[at], send.at[at], recv.at[at], ring(by))
        return found

    half = lanes((ROWS, 128)) < 64

    def tile(ref, index):
        return ref[:, 128 * index : 128 * index + 128]

    def put(ref, index, value):
        ref[:, 128 * index : 128 * index + 128] = value

    def face_of(ref):
        return jnp.where(half, tile(ref, 0), tile(ref, 3))

    def put_face(ref, value):
        put(ref, 0, jnp.where(half, value, tile(ref, 0)))
        put(ref, 3, jnp.where(half, tile(ref, 3), value))

    def send_faces(face, turn):
        top, bottom, part = face[0:128], face[128:256], half[0:128]
        edge_out[turn, 0] = jnp.where(part, pltpu.roll(top, 64, 1), bottom)
        edge_out[turn, 1] = jnp.where(part, top, pltpu.roll(bottom, 64, 1))
        copies = [
            remote(
                edge_out.at[turn, way],
                edge_in.at[turn, way],
                edge_send.at[turn, way],
                edge_recv.at[turn, way],
                ring(by),
            )
            for way, by in ((0, 1), (1, -1))
        ]
        for copy in copies:
            copy.start()
        return copies

    def faces_arrived(copies, turn):
        for copy in copies:
            copy.wait_recv()
        below, above, part = edge_in[turn, 0], edge_in[turn, 1], half[0:128]
        top = jnp.where(part, below, pltpu.roll(above, 64, 1))
        bottom = jnp.where(part, pltpu.roll(below, 64, 1), above)
        return jnp.concatenate([top, bottom], 0)

    def vertex_sums(each):
        corner = lax.broadcasted_iota(jnp.int32, each.shape, 0)
        each = jnp.where(corner % 2 == 1, roll_x(each, 1), each)
        each = jnp.where(corner // 2 % 2 == 1, roll_y(each, 1), each)
        low = jnp.sum(each[0:4], axis=0, keepdims=True)
        high = jnp.sum(each[4:8], axis=0, keepdims=True)
        return low, high

    def gathered(matrix, parts):
        whole = dot16(matrix, parts[0], ((1,), (1,)))
        return whole[0:16] + whole[16:32] + dot16(matrix[0:16], parts[1], ((1,), (1,)))

    def face_lanes(value):
        return jnp.concatenate([value[:, 0:64], value[:, 448:512]], 1)

    def columns(planes):
        return jnp.concatenate(planes, 0).T

    def corner_pieces(corners):
        parts = [part.astype(F32) for part in split(corners, 3)]
        return [parts[left] for left, _ in PIECES]

    row = lax.broadcasted_iota(jnp.int32, (ROWS, ROWS), 0)
    loads[2].wait()
    pick = jnp.where(row == order_ref[...], 1.0, 0.0)
    pick16 = pick.astype(BF16)
    loads[1].wait()
    kappa_rows = jnp.broadcast_to(kappa_ref[...], (16, ROWS))
    kappa = sum(dot16(part, pick16, ((1,), (1,))) for part in split(kappa_rows, 3))[0:8]
    layer[1] = kappa[0:1]
    halo[REACH, 2:3] = kappa[0:1]
    loads[0].wait()
    load_ref, r0_ref = field["load"], field["r0"]

    def permuted(matrix, value):
        return sum(dot16(matrix, part) for part in split(value, 3))

    for index in (0, 3):
        put(load_ref, index, permuted(pick16, tile(forcing_ref, index)))
        put(r0_ref, index, shared_xy(tile(load_ref, index)))
    first_face = face_of(r0_ref)
    pl.semaphore_wait(barrier, len(greeted))
    layer_copies = [
        remote(layer.at[1], layer.at[1 - by], layer_send.at[1 - by], layer_recv.at[1 - by], ring(by))
        for by in (1, -1)
    ]
    for copy in layer_copies:
        copy.start()
    edges = [send_faces(first_face, 0)]
    tell(0)

    for index in (1, 2):
        put(load_ref, index, permuted(pick16, tile(forcing_ref, index)))
    for copy in loads[3:]:
        copy.wait()
    parts = split(load_ref[...], 2)
    first = table["gather"][32:48].astype(BF16)
    each = dot16(first, parts[0], ((1,), (1,)))
    each = each[0:8] + each[8:16] + dot16(first, parts[1], ((1,), (1,)))[0:8]
    low, high = vertex_sums(each)
    halo[REACH, 0:1] = low
    halo[REACH, 1:2] = high
    halo_copies = to_ring(halo, halo_send, halo_recv, REACH)
    for copy in halo_copies.values():
        copy.start()
    own9 = nine(kappa)
    own_rows = [plane[0:1] for plane in own9] + [jnp.zeros((7, ROWS), F32)]
    own_columns = columns(own_rows)
    coeff_ref[...] = jnp.broadcast_to(own_columns[:, 4:5], (ROWS, 128))
    fixed, mass = table["rows"][0:1], table["rows"][1:2]
    fixed_face, mass_face = table["rows"][2:3, 0:128], table["rows"][3:4, 0:128]
    field["inverse"][...] = 1.0 / (dot(own_columns, table["share"][...]) + fixed)
    stiff = table["stiff"][...]
    upper_piece = stiff.astype(BF16)
    stiff_ref[0:NODES] = upper_piece
    stiff_ref[NODES:] = (stiff - upper_piece.astype(F32)).astype(BF16)
    put(r0_ref, 1, shared_xy(tile(load_ref, 1)))
    put(r0_ref, 2, shared_xy(tile(load_ref, 2)))
    gather = table["gather"][0:32].astype(BF16)
    gather_face = face_lanes(gather)

    def interior(value, x_ref):
        inverse = field["inverse"]
        zero = jnp.zeros((ROWS, 128), F32)
        put(x_ref, 0, jnp.where(half, zero, tile(inverse, 0) * tile(value, 0)))
        put(x_ref, 1, tile(inverse, 1) * tile(value, 1))
        put(x_ref, 2, tile(inverse, 2) * tile(value, 2))
        put(x_ref, 3, jnp.where(half, tile(inverse, 3) * tile(value, 3), zero))
        parts = split(x_ref[...], 2)
        high, low = stiff_ref[0:NODES], stiff_ref[NODES:]
        field["stiffened"][...] = (
            dot16(parts[0], high) + dot16(parts[1], high) + dot16(parts[0], low)
        )
        return gathered(gather, parts)

    inner_rows = interior(r0_ref, field["x0"])
    for at, piece in ((0, 0), (128, 0), (256, NODES)):
        stiff_face_ref[at : at + 64] = stiff_ref[piece : piece + 64]
        stiff_face_ref[at + 64 : at + 128] = stiff_ref[piece + 448 : piece + 512]
    stiff_face_face = face_lanes(stiff_face_ref[...])

    for copy in layer_copies:
        copy.wait_recv()
    below9 = nine(jnp.broadcast_to(layer[0], (8, ROWS)))
    above9 = nine(jnp.broadcast_to(layer[2], (8, ROWS)))
    pad = [jnp.zeros((7, ROWS), F32)]
    three = columns(
        own_rows + [p[0:1] for p in below9] + pad + [p[0:1] for p in above9] + pad
    )
    inverse_face = 1.0 / (dot(three, table["share_face"][...]) + fixed_face)
    coeff_beside = jnp.where(half, three[:, 20:21], three[:, 36:37])
    coeff = coeff_ref[...]
    face = first_face + faces_arrived(edges[0], 0)
    put_face(r0_ref, face)

    def outer(face, x_ref, rows):
        x_face = inverse_face * face
        put_face(x_ref, x_face)
        parts = split(x_face, 2)
        rows = rows + gathered(gather_face, parts)
        return x_face, jnp.concatenate([parts[0], parts[1], parts[0]], 1), rows

    x_face, stacked, rows0 = outer(face, field["x0"], inner_rows)
    rough = coeff * (
        face_of(field["stiffened"]) + dot16(stacked, stiff_face_face)
    ) + mass_face * x_face
    edges.append(send_faces(shared_xy(rough), 1))
    low, high = vertex_sums(kappa * rows0[0:8] + rows0[8:16])
    rest[NEAR, 0:1] = low
    rest[NEAR, 1:2] = high
    rest_copies = to_ring(rest, rest_send, rest_recv, NEAR)
    for copy in rest_copies.values():
        copy.start()

    hear(0)
    tell(1)
    field["stiffened"][...] += dot16(stacked, stiff_face_ref[...])
    spread_table = table["spread"][...].astype(BF16)
    spread_face_table = table["spread_face"][...].astype(BF16)
    for copy in halo_copies.values():
        copy.wait_recv()
    planes = list(range(-3, REACH + 1)) + list(range(1 - REACH, -3))

    def halo_rows(shift, which):
        return jnp.concatenate([halo[REACH + p + shift, which : which + 1] for p in planes], 0)

    under4, over4 = four(halo_rows(-1, 2)), four(halo_rows(0, 2))
    both4 = [a + b for a, b in zip(under4, over4)]
    diag = (2.0 / 3.0) * (both4[0] + both4[1] + both4[2] + both4[3]) + REACT * 64.0 / 27.0
    damp = -OMEGA / diag
    damp_down, damp_up = up(damp), down(damp)
    level = {key: damp * value for key, value in coarse_stencil(both4, 1).items()}
    from_above = {key: damp_down * value for key, value in coarse_stencil(under4, 0).items()}
    from_below = {key: damp_up * value for key, value in coarse_stencil(over4, 0).items()}
    start = -damp * (halo_rows(0, 0) + halo_rows(-1, 1))
    vert = start
    for _ in range(3):
        vert = start + swept(vert, level, from_above, from_below)
    remainder = (vert - swept(vert, level, from_above, from_below))[0:8]

    def corners_of(vert, lower):
        one = roll_x(vert, -1)
        found = [vert, one, roll_y(vert, -1), roll_y(one, -1)]
        return [
            jnp.concatenate(
                [c[k : k + 1] for c in found] + [c[k + 1 : k + 2] for c in found], 0
            )
            for k in lower
        ]

    own, under, over = corners_of(vert[0:8], (3, 2, 4))
    spread = dot16(columns(corner_pieces(own)).astype(BF16), spread_table)
    beside = dot16(
        columns(corner_pieces(under) + corner_pieces(over)).astype(BF16),
        spread_face_table,
    )
    beside = shared_xy(coeff_beside * beside[:, 0:128] + beside[:, 128:256])

    def total(value):
        return jnp.sum(jnp.sum(value.reshape(ROWS // 8, 8, 128), axis=0), axis=(0, 1), keepdims=True)

    def applied(x_ref, spread, z_ref, image_ref):
        for index in range(4):
            at = 128 * index
            z = tile(x_ref, index) + spread[:, at : at + 128]
            put(z_ref, index, z)
            put(
                image_ref,
                index,
                coeff * (tile(field["stiffened"], index) + spread[:, 512 + at : 640 + at])
                + mass[:, at : at + 128] * z,
            )

    def inner(left, right):
        return total(sum(tile(left, index) * tile(right, index) for index in range(4)))

    applied(field["x0"], spread, field["z0"], field["qloc"])
    rz = inner(load_ref, field["z0"])
    zq = inner(field["qloc"], field["z0"])
    for index in range(4):
        put(field["q"], index, shared_xy(tile(field["qloc"], index)))
    partial_face = face_of(field["q"]) + beside
    inner_rows = interior(field["q"], field["x1"])

    face_image = face_of(field["qloc"])
    zero = jnp.zeros((ROWS, 128), F32)
    qy = inner(field["qloc"], field["x1"])
    hear(1)
    tell(2)
    back16 = pick.T.astype(BF16)

    def stored(value):
        return permuted(back16, value)

    sent_z0[...] = stored(field["z0"][...])
    sent_r0[...] = stored(r0_ref[...])

    face = partial_face + faces_arrived(edges[1], 1)
    x_face, stacked, rows1 = outer(face, field["x1"], inner_rows)
    field["stiffened"][...] += dot16(stacked, stiff_face_ref[...])
    for copy in rest_copies.values():
        copy.wait_recv()
    target = jnp.concatenate([rest[NEAR + p, 0:1] for p in range(-3, 5)], 0) + jnp.concatenate(
        [rest[NEAR + p - 1, 1:2] for p in range(-3, 5)], 0
    )

    def top(parts):
        return {key: value[0:8] for key, value in parts.items()}

    level, from_above, from_below = top(level), top(from_above), top(from_below)
    start = remainder - damp[0:8] * target
    vert = start
    for _ in range(3):
        vert = start + swept(vert, level, from_above, from_below)
    (own,) = corners_of(vert, (3,))

    def flipped(value, bit):
        corner = lax.broadcasted_iota(jnp.int32, value.shape, 0)
        return jnp.where(
            corner // bit % 2 == 0, pltpu.roll(value, 8 - bit, 0), pltpu.roll(value, bit, 0)
        )

    edge_sum = flipped(own, 1) + flipped(own, 2) + flipped(own, 4)
    all_sum = jnp.sum(own, axis=0, keepdims=True)
    weighed = own
    for bit in (1, 2, 4):
        weighed = (2.0 * weighed + flipped(weighed, bit)) * (1.0 / 3.0)
    steep = (5.0 / 6.0) * own + (1.0 / 6.0) * (edge_sum - all_sum)
    energy = own * (
        kappa * (steep + 2.0 * rows1[0:8]) + (REACT * weighed + 2.0 * rows1[8:16])
    )
    qy = qy + total(face_image * x_face) + jnp.sum((start * vert / -damp[0:8])[3:4], keepdims=True)
    yw = jnp.sum(energy, keepdims=True)
    image = [
        coeff * tile(field["stiffened"], index)
        + mass[:, 128 * index : 128 * index + 128] * tile(field["x1"], index)
        for index in range(4)
    ]
    yw = yw + total(sum(image[index] * tile(field["x1"], index) for index in range(4)))

    hear(2)
    lane = lanes((1, 128))
    mine = jnp.zeros((1, 128), F32)
    for index, value in enumerate((rz, zq, qy, yw)):
        mine = jnp.where(lane == index, value, mine)
    sums_ref[0] = mine

    def spread_sums(by, carry):
        remote(sums_ref.at[0], sums_ref.at[by], sum_send, sum_recv, ring(by)).start()
        return carry

    lax.fori_loop(1, size, spread_sums, 0)

    spread = dot16(columns(corner_pieces(own)).astype(BF16), spread_table)
    applied(field["x1"], spread, field["y"], field["w"])
    put(field["w"], 0, shared_xy(tile(field["w"], 0)))
    put(field["w"], 3, shared_xy(tile(field["w"], 3)))
    edges.append(send_faces(face_of(field["w"]), 2))
    put(field["w"], 1, shared_xy(tile(field["w"], 1)))
    put(field["w"], 2, shared_xy(tile(field["w"], 2)))
    put_face(field["q"], face)
    sent_y[...] = stored(field["y"][...])
    sent_q[...] = stored(field["q"][...])
    sent_w[...] = stored(field["w"][...])
    face = stored(faces_arrived(edges[2], 2))
    sent_w[:, 0:128] += jnp.where(half, face, zero)
    sent_w[:, 384:512] += jnp.where(half, zero, face)
    others = sums_ref.at[pl.ds(1, size - 1)]
    all_sums = remote(others, others, sum_send, sum_recv, ring(1))
    all_sums.wait_recv()
    sums = jnp.sum(sums_ref[...], axis=0)
    rz, zq, qy, yw = (sums[:, index : index + 1] for index in range(4))
    first = rz / zq
    gamma = first * first * qy - rz
    grown = 1.0 + gamma / rz
    second = gamma / (grown * grown * zq - 2.0 * first * grown * qy + first * first * yw)
    straight, bent = first + second * grown, first * second
    steps_ref[0:1] = jnp.broadcast_to(straight, (1, 128))
    steps_ref[1:2] = jnp.broadcast_to(bent, (1, 128))

    all_sums.wait_send()
    for copies in [layer_copies, halo_copies.values(), rest_copies.values()] + edges:
        for copy in copies:
            copy.wait_send()


def combine(z0, y, r0, q, w, steps, solution_ref, residual_ref, solution_part, residual_part, sem):
    straight, bent = steps[0:1, 0:1], steps[1:2, 0:1]
    copies = []
    rows = ROWS // PARTS
    for part in range(PARTS):
        at = pl.ds(part * rows, rows)
        solution_part[at] = straight * z0[at] - bent * y[at]
        copies.append(
            pltpu.make_async_copy(solution_part.at[at], solution_ref.at[at], sem.at[0, part])
        )
        copies[-1].start()
        residual_part[at] = r0[at] - straight * q[at] + bent * w[at]
        copies.append(
            pltpu.make_async_copy(residual_part.at[at], residual_ref.at[at], sem.at[1, part])
        )
        copies[-1].start()
    for copy in copies:
        copy.wait()


def per_device(size, forcing, kappa, elem_order):
    tables = all_tables()
    operands = [forcing, kappa.reshape(1, ROWS), elem_order]
    operands += [jnp.asarray(tables[name], F32) for name in NAMES]
    out = jax.ShapeDtypeStruct((ROWS, NODES), F32)
    steps = jax.ShapeDtypeStruct((8, 128), F32)
    count, close = 2 * REACH + 1, 2 * NEAR + 1
    dma = pltpu.SemaphoreType.DMA
    vmem = pl.BlockSpec(memory_space=pltpu.VMEM)
    hbm = pl.BlockSpec(memory_space=pltpu.HBM)
    stored = pl.pallas_call(
        functools.partial(kernel, size),
        out_shape=(out,) * 5 + (steps,),
        in_specs=[hbm] * len(operands),
        out_specs=(vmem,) * 6,
        scratch_shapes=[pltpu.VMEM(operand.shape, operand.dtype) for operand in operands]
        + [pltpu.VMEM((ROWS, NODES), F32)] * len(FIELDS)
        + [
            pltpu.VMEM((ROWS, 128), F32),
            pltpu.VMEM((2 * NODES, NODES), BF16),
            pltpu.VMEM((384, NODES), BF16),
            pltpu.VMEM((3, 2, 128, 128), F32),
            pltpu.VMEM((3, 2, 128, 128), F32),
            pltpu.VMEM((3, 1, ROWS), F32),
            pltpu.VMEM((count, 3, ROWS), F32),
            pltpu.VMEM((close, 2, ROWS), F32),
            pltpu.VMEM((size, 1, 128), F32),
            dma((len(operands),)),
            dma((3,)),
            dma((3,)),
            dma((count,)),
            dma((count,)),
            dma((close,)),
            dma((close,)),
            dma((3, 2)),
            dma((3, 2)),
            dma,
            dma,
            pltpu.SemaphoreType.REGULAR((3, 2)),
        ],
        compiler_params=pltpu.CompilerParams(
            collective_id=0, has_side_effects=True, vmem_limit_bytes=32 * 1024 * 1024
        ),
        name="solve",
    )(*[pltpu.with_memory_space_constraint(operand, pltpu.HBM) for operand in operands])
    return pl.pallas_call(
        combine,
        out_shape=(out, out),
        in_specs=[vmem] * 6,
        out_specs=(hbm, hbm),
        scratch_shapes=[
            pltpu.VMEM((ROWS, NODES), F32),
            pltpu.VMEM((ROWS, NODES), F32),
            dma((2, PARTS)),
        ],
        compiler_params=pltpu.CompilerParams(vmem_limit_bytes=16 * 1024 * 1024),
        name="combine",
    )(*stored)


def solution(mesh):
    in_specs = (P(("elem", "face"), None), P(("elem", "face")), P(("elem", "face"), None))
    out_specs = (P(("elem", "face"), None), P(("elem", "face"), None))
    size = mesh.shape["elem"] * mesh.shape["face"]
    return jax.shard_map(
        functools.partial(per_device, size),
        mesh=mesh,
        in_specs=in_specs,
        out_specs=out_specs,
        check_vma=False,
    )
```

```python
import functools

import jax
import jax.numpy as jnp
import numpy as np
from jax import lax
from jax.experimental import pallas as pl
from jax.experimental.pallas import tpu as pltpu
from jax.sharding import PartitionSpec as P

EX = 8
EY = 32
ROWS = EX * EY
NODES = 512
REACT = 0.02
OMEGA = 0.6
REACH = 8
NEAR = 4
PARTS = 4
PIECES = ((0, 0), (0, 1), (0, 2), (1, 0), (1, 1), (2, 0))
MESH = pl.DeviceIdType.MESH
F32 = jnp.float32
BF16 = jnp.bfloat16


def legendre_seven(points):
    before = np.ones(8)
    current = np.array(points)
    for degree in range(1, 7):
        following = ((2 * degree + 1) * points * current - degree * before) / (degree + 1)
        before = current
        current = following
    return current


def element_tables():
    points = np.array(
        [
            -1.0,
            -0.8717401485096066,
            -0.5917001814331423,
            -0.2092992179024789,
            0.2092992179024789,
            0.5917001814331423,
            0.8717401485096066,
            1.0,
        ]
    )
    weights = np.array(
        [
            1.0 / 28.0,
            0.2107042271435061,
            0.3411226924835044,
            0.4124587946587038,
            0.4124587946587038,
            0.3411226924835044,
            0.2107042271435061,
            1.0 / 28.0,
        ]
    )
    legendre = legendre_seven(points)
    derivative = np.zeros((8, 8))
    for left_node in range(8):
        for right_node in range(8):
            if left_node != right_node:
                derivative[left_node, right_node] = legendre[left_node] / (
                    legendre[right_node] * (points[left_node] - points[right_node])
                )
    derivative[0, 0] = -14.0
    derivative[7, 7] = 14.0
    stiffness = derivative.T @ (weights[:, None] * derivative)
    mass = np.eye(8) * weights[None, :]
    full_stiff = (
        np.kron(np.kron(mass, mass), stiffness)
        + np.kron(np.kron(mass, stiffness), mass)
        + np.kron(np.kron(stiffness, mass), mass)
    )
    mass_nodes = np.kron(np.kron(weights, weights), weights)
    interp = np.stack([(1.0 - points) / 2.0, (1.0 + points) / 2.0], 1)
    prolong = np.kron(np.kron(interp, interp), interp)
    return full_stiff, mass_nodes, prolong


def pieces_of(table, count):
    parts = []
    for _ in range(count):
        part = table.astype(BF16).astype(np.float64)
        parts.append(part)
        table = table - part
    return parts


def ends(offset):
    if offset == 0:
        return list(range(8)), list(range(8))
    return ([7], [0]) if offset == 1 else ([0], [7])


def all_tables():
    full_stiff, mass_nodes, prolong = element_tables()
    face = np.concatenate([np.arange(64), np.arange(448, 512)])
    facing = np.concatenate([np.arange(448, 512), np.arange(64)])
    diag = np.diag(full_stiff).reshape(8, 8, 8)
    mass = mass_nodes.reshape(8, 8, 8)
    share = np.zeros((16, 8, 8, 8))
    fixed = np.zeros((8, 8, 8))
    for index in range(9):
        offsets = (0, index // 3 - 1, index % 3 - 1)
        mine = np.ix_(*[ends(offset)[0] for offset in offsets])
        theirs = np.ix_(*[ends(offset)[1] for offset in offsets])
        share[index][mine] += diag[theirs]
        fixed[mine] += REACT * mass[theirs]
    share, fixed = share.reshape(16, NODES), fixed.reshape(NODES)
    fixed_face = 2.0 * fixed[face]
    share_face = np.zeros((48, 128))
    share_face[0:16] = share[:, face]
    share_face[16:32, :64] = share[:, facing[:64]]
    share_face[32:48, 64:] = share[:, facing[64:]]

    steep = full_stiff @ prolong
    heavy = REACT * mass_nodes[:, None] * prolong

    def stacked(table):
        parts = pieces_of(table, 3)
        return np.concatenate([parts[right] for _, right in PIECES], 0)

    spread = stacked(np.concatenate([prolong.T, steep.T], 1))
    facing_tables = np.concatenate([steep[facing].T, heavy[facing].T], 1)
    lower = facing_tables.copy()
    lower[:, 64:128] = 0.0
    lower[:, 192:256] = 0.0
    spread_face = np.concatenate([stacked(lower), stacked(facing_tables - lower)], 0)

    gather = pieces_of(np.concatenate([steep.T, heavy.T], 0), 2)
    gather = np.concatenate(gather, 0)
    first = np.concatenate(pieces_of(prolong.T, 2), 0)
    return {
        "stiff": full_stiff,
        "spread": spread,
        "spread_face": spread_face,
        "gather": np.concatenate([gather, first], 0),
        "share": share,
        "share_face": share_face,
        "rows": np.concatenate(
            [
                np.stack([fixed, REACT * mass_nodes]),
                np.pad(np.stack([fixed_face, REACT * mass_nodes[face]]), ((0, 0), (0, 384))),
            ],
            0,
        ),
    }


def split(value, pieces):
    parts = []
    for _ in range(pieces):
        part = value.astype(BF16)
        parts.append(part)
        value = value - part.astype(F32)
    return parts


def dot(left, right, dims=((1,), (0,))):
    return lax.dot_general(
        left, right, (dims, ((), ())), precision=lax.Precision.HIGHEST, preferred_element_type=F32
    )


def dot16(left, right, dims=((1,), (0,))):
    return lax.dot_general(left, right, (dims, ((), ())), preferred_element_type=F32)


def lanes(shape):
    return lax.broadcasted_iota(jnp.int32, shape, len(shape) - 1)


def roll_x(plane, by):
    size = plane.shape[1]
    along = lanes(plane.shape) % EX
    inside = pltpu.roll(plane, by % size, 1)
    around = pltpu.roll(plane, (by - EX * by) % size, 1)
    return jnp.where(along == (0 if by == 1 else EX - 1), around, inside)


def roll_y(plane, by):
    return pltpu.roll(plane, (by * EX) % plane.shape[1], 1)


def down(plane):
    return pltpu.roll(plane, plane.shape[0] - 1, 0)


def up(plane):
    return pltpu.roll(plane, 1, 0)


def shared_xy(tile):
    cube = tile.reshape(EY, EX, 128)
    lane = lanes(cube.shape)
    nx, ny = lane % 8, lane // 8 % 8
    after = pltpu.roll(pltpu.roll(cube, EX - 1, 1), 7, 2)
    before = pltpu.roll(pltpu.roll(cube, 1, 1), 128 - 7, 2)
    cube = cube + jnp.where(nx == 7, after, jnp.where(nx == 0, before, 0.0))
    after = pltpu.roll(jnp.concatenate([cube[1:], cube[:1]], 0), 56, 2)
    before = pltpu.roll(jnp.concatenate([cube[-1:], cube[:-1]], 0), 128 - 56, 2)
    cube = cube + jnp.where(ny == 7, after, jnp.where(ny == 0, before, 0.0))
    return cube.reshape(ROWS, 128)


def four(layer):
    moved = [layer, roll_x(layer, 1)]
    return moved + [roll_y(moved[0], 1), roll_y(moved[1], 1)]


def nine(layer):
    side = {0: layer, 1: roll_x(layer, -1), -1: roll_x(layer, 1)}
    return [
        side[dx] if dy == 0 else roll_y(side[dx], -dy) for dy in (-1, 0, 1) for dx in (-1, 0, 1)
    ]


def coarse_stencil(layer4, planes):
    found = {}
    for dy in (-1, 0, 1):
        for dx in (-1, 0, 1):
            rows = (0, 1) if dy == 0 else ((0,) if dy == 1 else (1,))
            cols = (0, 1) if dx == 0 else ((0,) if dx == 1 else (1,))
            differ = abs(dy) + abs(dx) + (1 - planes)
            count = len(rows) * len(cols) * (1 + planes)
            weight = REACT * count * 2.0 ** (3 - differ) / 27.0
            if differ >= 2:
                total = sum(layer4[2 * a + b] for a in rows for b in cols)
                found[dy, dx] = (-1.0 / 6.0) * total + weight
            elif differ == 1:
                found[dy, dx] = weight
    return found


def swept(vert, level, from_above, from_below):
    along = {0: vert, 1: roll_x(vert, -1), -1: roll_x(vert, 1)}
    spread = {}
    for dx, value in along.items():
        spread[0, dx] = value
        spread[1, dx] = roll_y(value, -1)
        spread[-1, dx] = roll_y(value, 1)
    total = (1.0 - OMEGA) * vert
    total += sum(level[key] * spread[key] for key in level)
    total += down(sum(from_above[key] * spread[key] for key in from_above))
    total += up(sum(from_below[key] * spread[key] for key in from_below))
    return total


NAMES = (
    "stiff",
    "spread",
    "spread_face",
    "gather",
    "share",
    "share_face",
    "rows",
)
FIELDS = ("load", "r0", "x0", "z0", "q", "qloc", "x1", "y", "w", "inverse", "stiffened")


def kernel(size, *refs):
    refs = list(refs)

    def take(count):
        taken = refs[:count]
        del refs[:count]
        return taken

    sources = take(3 + len(NAMES))
    sent_z0, sent_y, sent_r0, sent_q, sent_w, steps_ref = take(6)
    inputs = take(3 + len(NAMES))
    forcing_ref, kappa_ref, order_ref = inputs[:3]
    table = dict(zip(NAMES, inputs[3:]))
    field = dict(zip(FIELDS, take(len(FIELDS))))
    coeff_ref, stiff_ref, stiff_face_ref = take(3)
    edge_out, edge_in, layer, halo, rest, sums_ref = take(6)
    in_sem, layer_send, layer_recv, halo_send, halo_recv = take(5)
    rest_send, rest_recv, edge_send, edge_recv, sum_send, sum_recv, known_sem = take(7)

    me = lax.axis_index("elem") * 2 + lax.axis_index("face")

    def ring(by):
        device = lax.rem(me + by + size, size)
        return lax.div(device, 2), lax.rem(device, 2)

    barrier = pltpu.get_barrier_semaphore()

    loads = {
        index: pltpu.make_async_copy(sources[index], inputs[index], in_sem.at[index])
        for index in range(1, len(inputs))
    }
    forcing_loads = [
        pltpu.make_async_copy(
            sources[0].at[:, pl.ds(at, width)],
            forcing_ref.at[:, pl.ds(at, width)],
            in_sem.at[len(inputs) + index],
        )
        for index, (at, width) in enumerate(((0, 128), (384, 128), (128, 256)))
    ]
    loads[2].start()
    forcing_loads[0].start()
    forcing_loads[1].start()
    loads[1].start()
    greeted = [by for by in range(-REACH, REACH + 1) if by != 0]
    for by in greeted:
        pl.semaphore_signal(barrier, inc=1, device_id=ring(by), device_id_type=MESH)
    forcing_loads[2].start()
    for index in range(len(inputs) - 1, 2, -1):
        loads[index].start()

    stages = []
    while REACH << len(stages) < size // 2:
        stages.append(REACH << len(stages))

    def tell(stage):
        if stage < len(stages):
            for way, by in enumerate((stages[stage], -stages[stage])):
                pl.semaphore_signal(
                    known_sem.at[stage, way], inc=1, device_id=ring(by), device_id_type=MESH
                )

    def hear(stage):
        if stage < len(stages):
            for way in range(2):
                pl.semaphore_wait(known_sem.at[stage, way], 1)

    def remote(source, target, send, recv, device):
        return pltpu.make_async_remote_copy(
            src_ref=source,
            dst_ref=target,
            send_sem=send,
            recv_sem=recv,
            device_id=device,
            device_id_type=MESH,
        )

    def to_ring(buffer, send, recv, reach):
        found = {}
        for by in sorted(range(-reach, reach + 1), key=abs):
            if by != 0:
                at = reach - by
                found[by] = remote(buffer.at[reach], buffer.at[at], send.at[at], recv.at[at], ring(by))
        return found

    half = lanes((ROWS, 128)) < 64

    def tile(ref, index):
        return ref[:, 128 * index : 128 * index + 128]

    def put(ref, index, value):
        ref[:, 128 * index : 128 * index + 128] = value

    def face_of(ref):
        return jnp.where(half, tile(ref, 0), tile(ref, 3))

    def put_face(ref, value):
        put(ref, 0, jnp.where(half, value, tile(ref, 0)))
        put(ref, 3, jnp.where(half, tile(ref, 3), value))

    def send_faces(face, turn):
        top, bottom, part = face[0:128], face[128:256], half[0:128]
        edge_out[turn, 0] = jnp.where(part, pltpu.roll(top, 64, 1), bottom)
        edge_out[turn, 1] = jnp.where(part, top, pltpu.roll(bottom, 64, 1))
        copies = [
            remote(
                edge_out.at[turn, way],
                edge_in.at[turn, way],
                edge_send.at[turn, way],
                edge_recv.at[turn, way],
                ring(by),
            )
            for way, by in ((0, 1), (1, -1))
        ]
        for copy in copies:
            copy.start()
        return copies

    def faces_arrived(copies, turn):
        for copy in copies:
            copy.wait_recv()
        below, above, part = edge_in[turn, 0], edge_in[turn, 1], half[0:128]
        top = jnp.where(part, below, pltpu.roll(above, 64, 1))
        bottom = jnp.where(part, pltpu.roll(below, 64, 1), above)
        return jnp.concatenate([top, bottom], 0)

    def vertex_sums(each):
        corner = lax.broadcasted_iota(jnp.int32, each.shape, 0)
        each = jnp.where(corner % 2 == 1, roll_x(each, 1), each)
        each = jnp.where(corner // 2 % 2 == 1, roll_y(each, 1), each)
        low = jnp.sum(each[0:4], axis=0, keepdims=True)
        high = jnp.sum(each[4:8], axis=0, keepdims=True)
        return low, high

    def gathered(matrix, parts):
        whole = dot16(matrix, parts[0], ((1,), (1,)))
        return whole[0:16] + whole[16:32] + dot16(matrix[0:16], parts[1], ((1,), (1,)))

    def face_lanes(value):
        return jnp.concatenate([value[:, 0:64], value[:, 448:512]], 1)

    def columns(planes):
        return jnp.concatenate(planes, 0).T

    def corner_pieces(corners):
        parts = [part.astype(F32) for part in split(corners, 3)]
        return [parts[left] for left, _ in PIECES]

    row = lax.broadcasted_iota(jnp.int32, (ROWS, ROWS), 0)
    loads[2].wait()
    pick = jnp.where(row == order_ref[...], 1.0, 0.0)
    pick16 = pick.astype(BF16)
    loads[1].wait()
    kappa_rows = jnp.broadcast_to(kappa_ref[...], (16, ROWS))
    kappa = sum(dot16(part, pick16, ((1,), (1,))) for part in split(kappa_rows, 3))[0:8]
    layer[1] = kappa[0:1]
    halo[REACH, 2:3] = kappa[0:1]
    load_ref, r0_ref = field["load"], field["r0"]

    def permuted(matrix, value):
        return sum(dot16(matrix, part) for part in split(value, 3))

    for copy in forcing_loads[:2]:
        copy.wait()
    first_face = shared_xy(permuted(pick16, face_of(forcing_ref)))
    pl.semaphore_wait(barrier, len(greeted))
    layer_copies = [
        remote(layer.at[1], layer.at[1 - by], layer_send.at[1 - by], layer_recv.at[1 - by], ring(by))
        for by in (1, -1)
    ]
    for copy in layer_copies:
        copy.start()
    edges = [send_faces(first_face, 0)]
    tell(0)

    forcing_loads[2].wait()
    load_ref[...] = permuted(pick16, forcing_ref[...])
    for index in range(3, len(inputs)):
        loads[index].wait()
    parts = split(load_ref[...], 2)
    first = table["gather"][32:48].astype(BF16)
    each = dot16(first, parts[0], ((1,), (1,)))
    each = each[0:8] + each[8:16] + dot16(first, parts[1], ((1,), (1,)))[0:8]
    low, high = vertex_sums(each)
    halo[REACH, 0:1] = low
    halo[REACH, 1:2] = high
    halo_copies = to_ring(halo, halo_send, halo_recv, REACH)
    for copy in halo_copies.values():
        copy.start()
    own9 = nine(kappa)
    own_rows = [plane[0:1] for plane in own9] + [jnp.zeros((7, ROWS), F32)]
    own_columns = columns(own_rows)
    coeff_ref[...] = jnp.broadcast_to(own_columns[:, 4:5], (ROWS, 128))
    fixed, mass = table["rows"][0:1], table["rows"][1:2]
    fixed_face, mass_face = table["rows"][2:3, 0:128], table["rows"][3:4, 0:128]
    field["inverse"][...] = 1.0 / (dot(own_columns, table["share"][...]) + fixed)
    stiff = table["stiff"][...]
    upper_piece = stiff.astype(BF16)
    stiff_ref[0:NODES] = upper_piece
    stiff_ref[NODES:] = (stiff - upper_piece.astype(F32)).astype(BF16)
    for index in range(4):
        put(r0_ref, index, shared_xy(tile(load_ref, index)))
    gather = table["gather"][0:32].astype(BF16)
    gather_face = face_lanes(gather)

    def interior(value, x_ref):
        inverse = field["inverse"]
        zero = jnp.zeros((ROWS, 128), F32)
        put(x_ref, 0, jnp.where(half, zero, tile(inverse, 0) * tile(value, 0)))
        put(x_ref, 1, tile(inverse, 1) * tile(value, 1))
        put(x_ref, 2, tile(inverse, 2) * tile(value, 2))
        put(x_ref, 3, jnp.where(half, tile(inverse, 3) * tile(value, 3), zero))
        parts = split(x_ref[...], 2)
        high, low = stiff_ref[0:NODES], stiff_ref[NODES:]
        field["stiffened"][...] = (
            dot16(parts[0], high) + dot16(parts[1], high) + dot16(parts[0], low)
        )
        return gathered(gather, parts)

    inner_rows = interior(r0_ref, field["x0"])
    for at, piece in ((0, 0), (128, 0), (256, NODES)):
        stiff_face_ref[at : at + 64] = stiff_ref[piece : piece + 64]
        stiff_face_ref[at + 64 : at + 128] = stiff_ref[piece + 448 : piece + 512]
    stiff_face_face = face_lanes(stiff_face_ref[...])

    hear(0)
    tell(1)
    for copy in layer_copies:
        copy.wait_recv()
    below9 = nine(jnp.broadcast_to(layer[0], (8, ROWS)))
    above9 = nine(jnp.broadcast_to(layer[2], (8, ROWS)))
    pad = [jnp.zeros((7, ROWS), F32)]
    three = columns(
        own_rows + [p[0:1] for p in below9] + pad + [p[0:1] for p in above9] + pad
    )
    inverse_face = 1.0 / (dot(three, table["share_face"][...]) + fixed_face)
    coeff_beside = jnp.where(half, three[:, 20:21], three[:, 36:37])
    coeff = coeff_ref[...]
    face = first_face + faces_arrived(edges[0], 0)
    put_face(r0_ref, face)

    def outer(face, x_ref, rows):
        x_face = inverse_face * face
        put_face(x_ref, x_face)
        parts = split(x_face, 2)
        rows = rows + gathered(gather_face, parts)
        return x_face, jnp.concatenate([parts[0], parts[1], parts[0]], 1), rows

    x_face, stacked, rows0 = outer(face, field["x0"], inner_rows)
    rough = coeff * (
        face_of(field["stiffened"]) + dot16(stacked, stiff_face_face)
    ) + mass_face * x_face
    low, high = vertex_sums(kappa * rows0[0:8] + rows0[8:16])
    rest[NEAR, 0:1] = low
    rest[NEAR, 1:2] = high
    rest_copies = to_ring(rest, rest_send, rest_recv, NEAR)
    for copy in rest_copies.values():
        copy.start()
    edges.append(send_faces(shared_xy(rough), 1))

    hear(1)
    tell(2)
    field["stiffened"][...] += dot16(stacked, stiff_face_ref[...])
    spread_table = table["spread"][...].astype(BF16)
    spread_face_table = table["spread_face"][...].astype(BF16)
    spread_own_face = jnp.concatenate(
        [face_lanes(spread_table[:, 0:NODES]), face_lanes(spread_table[:, NODES:])], 1
    )
    for copy in halo_copies.values():
        copy.wait_recv()
    planes = list(range(-3, REACH + 1)) + list(range(1 - REACH, -3))

    def halo_rows(shift, which):
        return jnp.concatenate([halo[REACH + p + shift, which : which + 1] for p in planes], 0)

    under4, over4 = four(halo_rows(-1, 2)), four(halo_rows(0, 2))
    both4 = [a + b for a, b in zip(under4, over4)]
    diag = (2.0 / 3.0) * (both4[0] + both4[1] + both4[2] + both4[3]) + REACT * 64.0 / 27.0
    damp = -OMEGA / diag
    damp_down, damp_up = up(damp), down(damp)
    level = {key: damp * value for key, value in coarse_stencil(both4, 1).items()}
    from_above = {key: damp_down * value for key, value in coarse_stencil(under4, 0).items()}
    from_below = {key: damp_up * value for key, value in coarse_stencil(over4, 0).items()}
    start = -damp * (halo_rows(0, 0) + halo_rows(-1, 1))
    vert = start
    for _ in range(3):
        vert = start + swept(vert, level, from_above, from_below)
    remainder = (vert - swept(vert, level, from_above, from_below))[0:8]

    def corners_of(vert, lower):
        one = roll_x(vert, -1)
        found = [vert, one, roll_y(vert, -1), roll_y(one, -1)]
        return [
            jnp.concatenate(
                [c[k : k + 1] for c in found] + [c[k + 1 : k + 2] for c in found], 0
            )
            for k in lower
        ]

    own, under, over = corners_of(vert[0:8], (3, 2, 4))
    spread = dot16(columns(corner_pieces(own)).astype(BF16), spread_table)
    beside = dot16(
        columns(corner_pieces(under) + corner_pieces(over)).astype(BF16),
        spread_face_table,
    )
    beside = shared_xy(coeff_beside * beside[:, 0:128] + beside[:, 128:256])

    def total(value):
        return jnp.sum(jnp.sum(value.reshape(ROWS // 8, 8, 128), axis=0), axis=(0, 1), keepdims=True)

    def applied(x_ref, spread, z_ref, image_ref):
        for index in range(4):
            at = 128 * index
            z = tile(x_ref, index) + spread[:, at : at + 128]
            put(z_ref, index, z)
            put(
                image_ref,
                index,
                coeff * (tile(field["stiffened"], index) + spread[:, 512 + at : 640 + at])
                + mass[:, at : at + 128] * z,
            )

    def inner(left, right):
        return total(sum(tile(left, index) * tile(right, index) for index in range(4)))

    applied(field["x0"], spread, field["z0"], field["qloc"])
    rz = inner(load_ref, field["z0"])
    zq = inner(field["qloc"], field["z0"])
    for index in range(4):
        put(field["q"], index, shared_xy(tile(field["qloc"], index)))
    partial_face = face_of(field["q"]) + beside
    inner_rows = interior(field["q"], field["x1"])

    face_image = face_of(field["qloc"])
    zero = jnp.zeros((ROWS, 128), F32)
    qy = inner(field["qloc"], field["x1"])
    back16 = pick.T.astype(BF16)

    def stored(value):
        return permuted(back16, value)

    sent_z0[...] = stored(field["z0"][...])
    sent_r0[...] = stored(r0_ref[...])

    for copy in rest_copies.values():
        copy.wait_recv()
    face = partial_face + faces_arrived(edges[1], 1)
    x_face, stacked, rows1 = outer(face, field["x1"], inner_rows)
    field["stiffened"][...] += dot16(stacked, stiff_face_ref[...])
    target = jnp.concatenate([rest[NEAR + p, 0:1] for p in range(-3, 5)], 0) + jnp.concatenate(
        [rest[NEAR + p - 1, 1:2] for p in range(-3, 5)], 0
    )

    def top(parts):
        return {key: value[0:8] for key, value in parts.items()}

    level, from_above, from_below = top(level), top(from_above), top(from_below)
    start = remainder - damp[0:8] * target
    vert = start
    for _ in range(3):
        vert = start + swept(vert, level, from_above, from_below)
    (own,) = corners_of(vert, (3,))

    own_pieces = columns(corner_pieces(own)).astype(BF16)
    spread = dot16(own_pieces, spread_own_face)
    y_face = x_face + spread[:, 0:128]
    w_face = coeff * (face_of(field["stiffened"]) + spread[:, 128:256]) + mass_face * y_face
    edges.append(send_faces(shared_xy(w_face), 2))

    def flipped(value, bit):
        corner = lax.broadcasted_iota(jnp.int32, value.shape, 0)
        return jnp.where(
            corner // bit % 2 == 0, pltpu.roll(value, 8 - bit, 0), pltpu.roll(value, bit, 0)
        )

    edge_sum = flipped(own, 1) + flipped(own, 2) + flipped(own, 4)
    all_sum = jnp.sum(own, axis=0, keepdims=True)
    weighed = own
    for bit in (1, 2, 4):
        weighed = (2.0 * weighed + flipped(weighed, bit)) * (1.0 / 3.0)
    steep = (5.0 / 6.0) * own + (1.0 / 6.0) * (edge_sum - all_sum)
    energy = own * (
        kappa * (steep + 2.0 * rows1[0:8]) + (REACT * weighed + 2.0 * rows1[8:16])
    )
    qy = qy + total(face_image * x_face) + jnp.sum((start * vert / -damp[0:8])[3:4], keepdims=True)
    yw = jnp.sum(energy, keepdims=True)
    image = [
        coeff * tile(field["stiffened"], index)
        + mass[:, 128 * index : 128 * index + 128] * tile(field["x1"], index)
        for index in range(4)
    ]
    yw = yw + total(sum(image[index] * tile(field["x1"], index) for index in range(4)))

    hear(2)
    lane = lanes((1, 128))
    mine = jnp.zeros((1, 128), F32)
    for index, value in enumerate((rz, zq, qy, yw)):
        mine = jnp.where(lane == index, value, mine)
    sums_ref[0] = mine

    def spread_sums(by, carry):
        remote(sums_ref.at[0], sums_ref.at[by], sum_send, sum_recv, ring(by)).start()
        return carry

    lax.fori_loop(size // 4, size, spread_sums, 0)
    lax.fori_loop(1, size // 4, spread_sums, 0)

    applied(field["x1"], dot16(own_pieces, spread_table), field["y"], field["w"])
    for index in range(4):
        put(field["w"], index, shared_xy(tile(field["w"], index)))
    put_face(field["q"], face)
    sent_y[...] = stored(field["y"][...])
    sent_q[...] = stored(field["q"][...])
    sent_w[...] = stored(field["w"][...])
    face = stored(faces_arrived(edges[2], 2))
    sent_w[:, 0:128] += jnp.where(half, face, zero)
    sent_w[:, 384:512] += jnp.where(half, zero, face)
    others = sums_ref.at[pl.ds(1, size - 1)]
    all_sums = remote(others, others, sum_send, sum_recv, ring(1))
    all_sums.wait_recv()
    sums = jnp.sum(sums_ref[...], axis=0)
    rz, zq, qy, yw = (sums[:, index : index + 1] for index in range(4))
    first = rz / zq
    gamma = first * first * qy - rz
    grown = 1.0 + gamma / rz
    second = gamma / (grown * grown * zq - 2.0 * first * grown * qy + first * first * yw)
    straight, bent = first + second * grown, first * second
    steps_ref[0:1] = jnp.broadcast_to(straight, (1, 128))
    steps_ref[1:2] = jnp.broadcast_to(bent, (1, 128))

    all_sums.wait_send()
    for copies in [layer_copies, halo_copies.values(), rest_copies.values()] + edges:
        for copy in copies:
            copy.wait_send()


def combine(z0, y, r0, q, w, steps, solution_ref, residual_ref, solution_part, residual_part, sem):
    straight, bent = steps[0:1, 0:1], steps[1:2, 0:1]
    copies = []
    rows = ROWS // PARTS
    for part in range(PARTS):
        at = pl.ds(part * rows, rows)
        solution_part[at] = straight * z0[at] - bent * y[at]
        copies.append(
            pltpu.make_async_copy(solution_part.at[at], solution_ref.at[at], sem.at[0, part])
        )
        copies[-1].start()
        residual_part[at] = r0[at] - straight * q[at] + bent * w[at]
        copies.append(
            pltpu.make_async_copy(residual_part.at[at], residual_ref.at[at], sem.at[1, part])
        )
        copies[-1].start()
    for copy in copies:
        copy.wait()


def per_device(size, forcing, kappa, elem_order):
    tables = all_tables()
    operands = [forcing, kappa.reshape(1, ROWS), elem_order]
    operands += [jnp.asarray(tables[name], F32) for name in NAMES]
    out = jax.ShapeDtypeStruct((ROWS, NODES), F32)
    steps = jax.ShapeDtypeStruct((8, 128), F32)
    count, close = 2 * REACH + 1, 2 * NEAR + 1
    dma = pltpu.SemaphoreType.DMA
    vmem = pl.BlockSpec(memory_space=pltpu.VMEM)
    hbm = pl.BlockSpec(memory_space=pltpu.HBM)
    stored = pl.pallas_call(
        functools.partial(kernel, size),
        out_shape=(out,) * 5 + (steps,),
        in_specs=[hbm] * len(operands),
        out_specs=(vmem,) * 6,
        scratch_shapes=[pltpu.VMEM(operand.shape, operand.dtype) for operand in operands]
        + [pltpu.VMEM((ROWS, NODES), F32)] * len(FIELDS)
        + [
            pltpu.VMEM((ROWS, 128), F32),
            pltpu.VMEM((2 * NODES, NODES), BF16),
            pltpu.VMEM((384, NODES), BF16),
            pltpu.VMEM((3, 2, 128, 128), F32),
            pltpu.VMEM((3, 2, 128, 128), F32),
            pltpu.VMEM((3, 1, ROWS), F32),
            pltpu.VMEM((count, 3, ROWS), F32),
            pltpu.VMEM((close, 2, ROWS), F32),
            pltpu.VMEM((size, 1, 128), F32),
            dma((len(operands) + 3,)),
            dma((3,)),
            dma((3,)),
            dma((count,)),
            dma((count,)),
            dma((close,)),
            dma((close,)),
            dma((3, 2)),
            dma((3, 2)),
            dma,
            dma,
            pltpu.SemaphoreType.REGULAR((3, 2)),
        ],
        compiler_params=pltpu.CompilerParams(
            collective_id=0, has_side_effects=True, vmem_limit_bytes=32 * 1024 * 1024
        ),
        name="solve",
    )(*[pltpu.with_memory_space_constraint(operand, pltpu.HBM) for operand in operands])
    return pl.pallas_call(
        combine,
        out_shape=(out, out),
        in_specs=[vmem] * 6,
        out_specs=(hbm, hbm),
        scratch_shapes=[
            pltpu.VMEM((ROWS, NODES), F32),
            pltpu.VMEM((ROWS, NODES), F32),
            dma((2, PARTS)),
        ],
        compiler_params=pltpu.CompilerParams(vmem_limit_bytes=16 * 1024 * 1024),
        name="combine",
    )(*stored)


def solution(mesh):
    in_specs = (P(("elem", "face"), None), P(("elem", "face")), P(("elem", "face"), None))
    out_specs = (P(("elem", "face"), None), P(("elem", "face"), None))
    size = mesh.shape["elem"] * mesh.shape["face"]
    return jax.shard_map(
        functools.partial(per_device, size),
        mesh=mesh,
        in_specs=in_specs,
        out_specs=out_specs,
        check_vma=False,
    )
```

```python
import functools

import jax
import jax.numpy as jnp
import numpy as np
from jax import lax
from jax.experimental import pallas as pl
from jax.experimental.pallas import tpu as pltpu
from jax.sharding import PartitionSpec as P

EX = 8
EY = 32
ROWS = EX * EY
NODES = 512
REACT = 0.02
OMEGA = 0.6
REACH = 8
NEAR = 4
PARTS = 4
PIECES = ((0, 0), (0, 1), (0, 2), (1, 0), (1, 1), (2, 0))
MESH = pl.DeviceIdType.MESH
F32 = jnp.float32
BF16 = jnp.bfloat16


def legendre_seven(points):
    before = np.ones(8)
    current = np.array(points)
    for degree in range(1, 7):
        following = ((2 * degree + 1) * points * current - degree * before) / (degree + 1)
        before = current
        current = following
    return current


def element_tables():
    points = np.array(
        [
            -1.0,
            -0.8717401485096066,
            -0.5917001814331423,
            -0.2092992179024789,
            0.2092992179024789,
            0.5917001814331423,
            0.8717401485096066,
            1.0,
        ]
    )
    weights = np.array(
        [
            1.0 / 28.0,
            0.2107042271435061,
            0.3411226924835044,
            0.4124587946587038,
            0.4124587946587038,
            0.3411226924835044,
            0.2107042271435061,
            1.0 / 28.0,
        ]
    )
    legendre = legendre_seven(points)
    derivative = np.zeros((8, 8))
    for left_node in range(8):
        for right_node in range(8):
            if left_node != right_node:
                derivative[left_node, right_node] = legendre[left_node] / (
                    legendre[right_node] * (points[left_node] - points[right_node])
                )
    derivative[0, 0] = -14.0
    derivative[7, 7] = 14.0
    stiffness = derivative.T @ (weights[:, None] * derivative)
    mass = np.eye(8) * weights[None, :]
    full_stiff = (
        np.kron(np.kron(mass, mass), stiffness)
        + np.kron(np.kron(mass, stiffness), mass)
        + np.kron(np.kron(stiffness, mass), mass)
    )
    mass_nodes = np.kron(np.kron(weights, weights), weights)
    interp = np.stack([(1.0 - points) / 2.0, (1.0 + points) / 2.0], 1)
    prolong = np.kron(np.kron(interp, interp), interp)
    return full_stiff, mass_nodes, prolong


def pieces_of(table, count):
    parts = []
    for _ in range(count):
        part = table.astype(BF16).astype(np.float64)
        parts.append(part)
        table = table - part
    return parts


def ends(offset):
    if offset == 0:
        return list(range(8)), list(range(8))
    return ([7], [0]) if offset == 1 else ([0], [7])


def all_tables():
    full_stiff, mass_nodes, prolong = element_tables()
    face = np.concatenate([np.arange(64), np.arange(448, 512)])
    facing = np.concatenate([np.arange(448, 512), np.arange(64)])
    diag = np.diag(full_stiff).reshape(8, 8, 8)
    mass = mass_nodes.reshape(8, 8, 8)
    share = np.zeros((16, 8, 8, 8))
    fixed = np.zeros((8, 8, 8))
    for index in range(9):
        offsets = (0, index // 3 - 1, index % 3 - 1)
        mine = np.ix_(*[ends(offset)[0] for offset in offsets])
        theirs = np.ix_(*[ends(offset)[1] for offset in offsets])
        share[index][mine] += diag[theirs]
        fixed[mine] += REACT * mass[theirs]
    share, fixed = share.reshape(16, NODES), fixed.reshape(NODES)
    fixed_face = 2.0 * fixed[face]
    beside = np.zeros((24, 128))
    beside[0:18:2, :64] = share[0:9, facing[:64]]
    beside[1:18:2, 64:] = share[0:9, facing[64:]]
    beside = pieces_of(beside, 2)
    share_face = np.concatenate(
        [share[:, face], beside[0], beside[1], beside[0], np.zeros((8, 128))], 0
    )

    steep = full_stiff @ prolong
    heavy = REACT * mass_nodes[:, None] * prolong

    def stacked(table):
        parts = pieces_of(table, 3)
        return np.concatenate([parts[right] for _, right in PIECES], 0)

    spread = stacked(np.concatenate([prolong.T, steep.T], 1))
    facing_tables = np.concatenate([steep[facing].T, heavy[facing].T], 1)
    lower = facing_tables.copy()
    lower[:, 64:128] = 0.0
    lower[:, 192:256] = 0.0
    spread_face = np.concatenate([stacked(lower), stacked(facing_tables - lower)], 0)

    gather = pieces_of(np.concatenate([steep.T, heavy.T], 0), 2)
    gather = np.concatenate(gather, 0)
    first = np.concatenate(pieces_of(prolong.T, 2), 0)
    return {
        "stiff": full_stiff,
        "spread": spread,
        "spread_face": spread_face,
        "gather": np.concatenate([gather, first], 0),
        "share": share,
        "share_face": share_face,
        "rows": np.concatenate(
            [
                np.stack([fixed, REACT * mass_nodes]),
                np.pad(np.stack([fixed_face, REACT * mass_nodes[face]]), ((0, 0), (0, 384))),
            ],
            0,
        ),
    }


def split(value, pieces):
    parts = []
    for _ in range(pieces):
        part = value.astype(BF16)
        parts.append(part)
        value = value - part.astype(F32)
    return parts


def dot(left, right, dims=((1,), (0,))):
    return lax.dot_general(
        left, right, (dims, ((), ())), precision=lax.Precision.HIGHEST, preferred_element_type=F32
    )


def dot16(left, right, dims=((1,), (0,))):
    return lax.dot_general(left, right, (dims, ((), ())), preferred_element_type=F32)


def lanes(shape):
    return lax.broadcasted_iota(jnp.int32, shape, len(shape) - 1)


def roll_x(plane, by):
    size = plane.shape[1]
    along = lanes(plane.shape) % EX
    inside = pltpu.roll(plane, by % size, 1)
    around = pltpu.roll(plane, (by - EX * by) % size, 1)
    return jnp.where(along == (0 if by == 1 else EX - 1), around, inside)


def roll_y(plane, by):
    return pltpu.roll(plane, (by * EX) % plane.shape[1], 1)


def down(plane):
    return pltpu.roll(plane, plane.shape[0] - 1, 0)


def up(plane):
    return pltpu.roll(plane, 1, 0)


def shared_xy(tile):
    cube = tile.reshape(EY, EX, 128)
    lane = lanes(cube.shape)
    nx, ny = lane % 8, lane // 8 % 8
    after = pltpu.roll(pltpu.roll(cube, EX - 1, 1), 7, 2)
    before = pltpu.roll(pltpu.roll(cube, 1, 1), 128 - 7, 2)
    cube = cube + jnp.where(nx == 7, after, jnp.where(nx == 0, before, 0.0))
    after = pltpu.roll(jnp.concatenate([cube[1:], cube[:1]], 0), 56, 2)
    before = pltpu.roll(jnp.concatenate([cube[-1:], cube[:-1]], 0), 128 - 56, 2)
    cube = cube + jnp.where(ny == 7, after, jnp.where(ny == 0, before, 0.0))
    return cube.reshape(ROWS, 128)


def four(layer):
    moved = [layer, roll_x(layer, 1)]
    return moved + [roll_y(moved[0], 1), roll_y(moved[1], 1)]


def nine(layer):
    side = {0: layer, 1: roll_x(layer, -1), -1: roll_x(layer, 1)}
    return [
        side[dx] if dy == 0 else roll_y(side[dx], -dy) for dy in (-1, 0, 1) for dx in (-1, 0, 1)
    ]


def coarse_stencil(layer4, planes):
    found = {}
    for dy in (-1, 0, 1):
        for dx in (-1, 0, 1):
            rows = (0, 1) if dy == 0 else ((0,) if dy == 1 else (1,))
            cols = (0, 1) if dx == 0 else ((0,) if dx == 1 else (1,))
            differ = abs(dy) + abs(dx) + (1 - planes)
            count = len(rows) * len(cols) * (1 + planes)
            weight = REACT * count * 2.0 ** (3 - differ) / 27.0
            if differ >= 2:
                total = sum(layer4[2 * a + b] for a in rows for b in cols)
                found[dy, dx] = (-1.0 / 6.0) * total + weight
            elif differ == 1:
                found[dy, dx] = weight
    return found


def swept(vert, level, from_above, from_below):
    along = {0: vert, 1: roll_x(vert, -1), -1: roll_x(vert, 1)}
    spread = {}
    for dx, value in along.items():
        spread[0, dx] = value
        spread[1, dx] = roll_y(value, -1)
        spread[-1, dx] = roll_y(value, 1)
    total = (1.0 - OMEGA) * vert
    total += sum(level[key] * spread[key] for key in level)
    total += down(sum(from_above[key] * spread[key] for key in from_above))
    total += up(sum(from_below[key] * spread[key] for key in from_below))
    return total


NAMES = (
    "stiff",
    "spread",
    "spread_face",
    "gather",
    "share",
    "share_face",
    "rows",
)
FIELDS = ("load", "r0", "x0", "z0", "q", "qloc", "x1", "y", "w", "inverse", "stiffened")


def kernel(size, *refs):
    refs = list(refs)

    def take(count):
        taken = refs[:count]
        del refs[:count]
        return taken

    sources = take(3 + len(NAMES))
    sent_z0, sent_y, sent_r0, sent_q, sent_w, steps_ref = take(6)
    inputs = take(3 + len(NAMES))
    forcing_ref, kappa_ref, order_ref = inputs[:3]
    table = dict(zip(NAMES, inputs[3:]))
    field = dict(zip(FIELDS, take(len(FIELDS))))
    coeff_ref, own_columns_ref, own_face_ref, inner_rows_ref, stiff_ref, stiff_face_ref = take(6)
    edge_out, edge_in, layer, halo, rest, sums_ref = take(6)
    in_sem, layer_send, layer_recv, halo_send, halo_recv = take(5)
    rest_send, rest_recv, edge_send, edge_recv, sum_send, sum_recv, known_sem = take(7)

    core = lax.axis_index("face")
    me = lax.axis_index("elem") * 2 + core

    def ring(by):
        device = lax.rem(me + by + size, size)
        return lax.div(device, 2), lax.rem(device, 2)

    barrier = pltpu.get_barrier_semaphore()

    loads = {
        index: pltpu.make_async_copy(sources[index], inputs[index], in_sem.at[index])
        for index in range(1, len(inputs))
    }
    forcing_loads = [
        pltpu.make_async_copy(
            sources[0].at[:, pl.ds(at, width)],
            forcing_ref.at[:, pl.ds(at, width)],
            in_sem.at[len(inputs) + index],
        )
        for index, (at, width) in enumerate(((0, 128), (384, 128), (128, 256)))
    ]
    loads[2].start()
    forcing_loads[0].start()
    forcing_loads[1].start()
    loads[1].start()
    greeted = [by for by in range(-REACH, REACH + 1) if by != 0]
    for by in greeted:
        pl.semaphore_signal(barrier, inc=1, device_id=ring(by), device_id_type=MESH)
    forcing_loads[2].start()
    for index in range(len(inputs) - 1, 2, -1):
        loads[index].start()

    stages = []
    while REACH << len(stages) < size // 2:
        stages.append(REACH << len(stages))

    def tell(stage):
        if stage < len(stages):
            for way, by in enumerate((stages[stage], -stages[stage])):
                pl.semaphore_signal(
                    known_sem.at[stage, way], inc=1, device_id=ring(by), device_id_type=MESH
                )

    def hear(stage):
        if stage < len(stages):
            for way in range(2):
                pl.semaphore_wait(known_sem.at[stage, way], 1)

    def remote(source, target, send, recv, device):
        return pltpu.make_async_remote_copy(
            src_ref=source,
            dst_ref=target,
            send_sem=send,
            recv_sem=recv,
            device_id=device,
            device_id_type=MESH,
        )

    def to_ring(buffer, send, recv, reach):
        found = {}
        for by in sorted(range(-reach, reach + 1), key=abs):
            if by != 0:
                at = reach - by
                found[by] = remote(buffer.at[reach], buffer.at[at], send.at[at], recv.at[at], ring(by))
        return found

    half = lanes((ROWS, 128)) < 64

    def tile(ref, index):
        return ref[:, 128 * index : 128 * index + 128]

    def put(ref, index, value):
        ref[:, 128 * index : 128 * index + 128] = value

    def face_of(ref):
        return jnp.where(half, tile(ref, 0), tile(ref, 3))

    def put_face(ref, value):
        put(ref, 0, jnp.where(half, value, tile(ref, 0)))
        put(ref, 3, jnp.where(half, tile(ref, 3), value))

    def send_faces(face, turn, both=True):
        top, bottom, part = face[0:128], face[128:256], half[0:128]
        edge_out[turn, 0] = jnp.where(part, pltpu.roll(top, 64, 1), bottom)
        edge_out[turn, 1] = jnp.where(part, top, pltpu.roll(bottom, 64, 1))
        copies = [
            remote(
                edge_out.at[turn, way],
                edge_in.at[turn, way],
                edge_send.at[turn, way],
                edge_recv.at[turn, way],
                ring(1 - 2 * way),
            )
            for way in (1 - core, core)
        ]
        copies[0].start()
        if both:
            copies[1].start()
        return copies

    def faces_arrived(copies, turn):
        for copy in copies:
            copy.wait_recv()
        below, above, part = edge_in[turn, 0], edge_in[turn, 1], half[0:128]
        top = jnp.where(part, below, pltpu.roll(above, 64, 1))
        bottom = jnp.where(part, pltpu.roll(below, 64, 1), above)
        return jnp.concatenate([top, bottom], 0)

    def vertex_sums(each):
        corner = lax.broadcasted_iota(jnp.int32, each.shape, 0)
        each = jnp.where(corner % 2 == 1, roll_x(each, 1), each)
        each = jnp.where(corner // 2 % 2 == 1, roll_y(each, 1), each)
        low = jnp.sum(each[0:4], axis=0, keepdims=True)
        high = jnp.sum(each[4:8], axis=0, keepdims=True)
        return low, high

    def gathered(matrix, parts):
        whole = dot16(matrix, parts[0], ((1,), (1,)))
        return whole[0:16] + whole[16:32] + dot16(matrix[0:16], parts[1], ((1,), (1,)))

    def face_lanes(value):
        return jnp.concatenate([value[:, 0:64], value[:, 448:512]], 1)

    def columns(planes):
        return jnp.concatenate(planes, 0).T

    def corner_pieces(corners):
        parts = [part.astype(F32) for part in split(corners, 3)]
        return [parts[left] for left, _ in PIECES]

    row = lax.broadcasted_iota(jnp.int32, (ROWS, ROWS), 0)
    loads[2].wait()
    pick = jnp.where(row == order_ref[...], 1.0, 0.0)
    pick16 = pick.astype(BF16)
    loads[1].wait()
    kappa_rows = jnp.broadcast_to(kappa_ref[...], (16, ROWS))
    kappa = sum(dot16(part, pick16, ((1,), (1,))) for part in split(kappa_rows, 3))[0:8]
    layer[1] = kappa[0:1]
    halo[REACH, 2:3] = kappa[0:1]
    load_ref, r0_ref = field["load"], field["r0"]

    def permuted(matrix, value):
        return sum(dot16(matrix, part) for part in split(value, 3))

    for copy in forcing_loads[:2]:
        copy.wait()
    first_face = shared_xy(permuted(pick16, face_of(forcing_ref)))
    own9 = nine(kappa)
    own_rows = [plane[0:1] for plane in own9] + [jnp.zeros((7, ROWS), F32)]
    own_columns = columns(own_rows)
    coeff_ref[...] = jnp.broadcast_to(own_columns[:, 4:5], (ROWS, 128))
    own_columns_ref[...] = own_columns

    def interior(value, x_ref):
        inverse = field["inverse"]
        zero = jnp.zeros((ROWS, 128), F32)
        put(x_ref, 0, jnp.where(half, zero, tile(inverse, 0) * tile(value, 0)))
        put(x_ref, 1, tile(inverse, 1) * tile(value, 1))
        put(x_ref, 2, tile(inverse, 2) * tile(value, 2))
        put(x_ref, 3, jnp.where(half, tile(inverse, 3) * tile(value, 3), zero))
        parts = split(x_ref[...], 2)
        high, low = stiff_ref[0:NODES], stiff_ref[NODES:]
        field["stiffened"][...] = (
            dot16(parts[0], high) + dot16(parts[1], high) + dot16(parts[0], low)
        )
        return gathered(table["gather"][0:32].astype(BF16), parts)

    def prepare_halo():
        forcing_loads[2].wait()
        load_ref[...] = permuted(pick16, forcing_ref[...])
        for index in range(3, len(inputs)):
            loads[index].wait()
        parts = split(load_ref[...], 2)
        first = table["gather"][32:48].astype(BF16)
        each = dot16(first, parts[0], ((1,), (1,)))
        each = each[0:8] + each[8:16] + dot16(first, parts[1], ((1,), (1,)))[0:8]
        low, high = vertex_sums(each)
        halo[REACH, 0:1] = low
        halo[REACH, 1:2] = high

    def prepare_interior():
        own_columns = own_columns_ref[...]
        fixed = table["rows"][0:1]
        field["inverse"][...] = 1.0 / (dot(own_columns, table["share"][...]) + fixed)
        own_face_ref[...] = dot(own_columns, table["share_face"][0:16]) + table["rows"][2:3, 0:128]
        stiff = table["stiff"][...]
        upper_piece = stiff.astype(BF16)
        stiff_ref[0:NODES] = upper_piece
        stiff_ref[NODES:] = (stiff - upper_piece.astype(F32)).astype(BF16)
        for index in range(4):
            put(r0_ref, index, shared_xy(tile(load_ref, index)))
        inner_rows_ref[...] = interior(r0_ref, field["x0"])
        for at, piece in ((0, 0), (128, 0), (256, NODES)):
            stiff_face_ref[at : at + 64] = stiff_ref[piece : piece + 64]
            stiff_face_ref[at + 64 : at + 128] = stiff_ref[piece + 448 : piece + 512]

    ahead = me < REACH

    @pl.when(ahead)
    def _():
        prepare_halo()
        prepare_interior()

    pl.semaphore_wait(barrier, len(greeted))
    layer_copies = [
        remote(layer.at[1], layer.at[1 - by], layer_send.at[1 - by], layer_recv.at[1 - by], ring(by))
        for by in (1, -1)
    ]
    for copy in layer_copies:
        copy.start()
    edges = [send_faces(first_face, 0)]
    tell(0)

    @pl.when(jnp.logical_not(ahead))
    def _():
        prepare_halo()

    halo_copies = to_ring(halo, halo_send, halo_recv, REACH)
    for copy in halo_copies.values():
        copy.start()

    @pl.when(jnp.logical_not(ahead))
    def _():
        prepare_interior()

    inner_rows = inner_rows_ref[...]
    mass, mass_face = table["rows"][1:2], table["rows"][3:4, 0:128]
    own_face = own_face_ref[...]
    share_two = table["share_face"][16:96].astype(BF16)
    gather = table["gather"][0:32].astype(BF16)
    gather_face = face_lanes(gather)
    stiff_face_face = face_lanes(stiff_face_ref[...])

    hear(0)
    tell(1)
    for copy in layer_copies:
        copy.wait_recv()
    two = jnp.concatenate([layer[0], layer[2], jnp.zeros((6, ROWS), F32)], 0)
    two9 = jnp.concatenate([plane[0:2] for plane in nine(two)] + [two[2:8]], 0)
    two_pieces = [part.astype(F32) for part in split(two9, 2)]
    two_columns = columns([two_pieces[0], two_pieces[0], two_pieces[1], two])
    inverse_face = 1.0 / (own_face + dot16(two_columns.astype(BF16), share_two))
    coeff_beside = jnp.where(half, two_columns[:, 72:73], two_columns[:, 73:74])
    coeff = coeff_ref[...]
    face = first_face + faces_arrived(edges[0], 0)
    put_face(r0_ref, face)

    def outer(face, x_ref, rows):
        x_face = inverse_face * face
        put_face(x_ref, x_face)
        parts = split(x_face, 2)
        rows = rows + gathered(gather_face, parts)
        stacked = jnp.concatenate([parts[0], parts[1], parts[0]], 1)
        return x_face, stacked, rows, dot16(stacked, stiff_face_face)

    x_face, stacked, rows0, steep_face = outer(face, field["x0"], inner_rows)
    rough = coeff * (face_of(field["stiffened"]) + steep_face) + mass_face * x_face
    low, high = vertex_sums(kappa * rows0[0:8] + rows0[8:16])
    rest[NEAR, 0:1] = low
    rest[NEAR, 1:2] = high
    rest_copies = to_ring(rest, rest_send, rest_recv, NEAR)
    for copy in rest_copies.values():
        copy.start()
    edges.append(send_faces(shared_xy(rough), 1))

    hear(1)
    tell(2)
    field["stiffened"][...] += dot16(stacked, stiff_face_ref[...])
    spread_table = table["spread"][...].astype(BF16)
    spread_face_table = table["spread_face"][...].astype(BF16)
    spread_own_face = jnp.concatenate(
        [face_lanes(spread_table[:, 0:NODES]), face_lanes(spread_table[:, NODES:])], 1
    )
    for copy in halo_copies.values():
        copy.wait_recv()
    planes = list(range(-3, REACH + 1)) + list(range(1 - REACH, -3))

    def halo_rows(shift, which):
        return jnp.concatenate([halo[REACH + p + shift, which : which + 1] for p in planes], 0)

    under4, over4 = four(halo_rows(-1, 2)), four(halo_rows(0, 2))
    both4 = [a + b for a, b in zip(under4, over4)]
    diag = (2.0 / 3.0) * (both4[0] + both4[1] + both4[2] + both4[3]) + REACT * 64.0 / 27.0
    damp = -OMEGA / diag
    damp_down, damp_up = up(damp), down(damp)
    level = {key: damp * value for key, value in coarse_stencil(both4, 1).items()}
    from_above = {key: damp_down * value for key, value in coarse_stencil(under4, 0).items()}
    from_below = {key: damp_up * value for key, value in coarse_stencil(over4, 0).items()}
    start = -damp * (halo_rows(0, 0) + halo_rows(-1, 1))
    vert = start
    for _ in range(3):
        vert = start + swept(vert, level, from_above, from_below)
    remainder = (vert - swept(vert, level, from_above, from_below))[0:8]

    def corners_of(vert, lower):
        one = roll_x(vert, -1)
        found = [vert, one, roll_y(vert, -1), roll_y(one, -1)]
        return [
            jnp.concatenate(
                [c[k : k + 1] for c in found] + [c[k + 1 : k + 2] for c in found], 0
            )
            for k in lower
        ]

    own, under, over = corners_of(vert[0:8], (3, 2, 4))
    spread = dot16(columns(corner_pieces(own)).astype(BF16), spread_table)
    beside = dot16(
        columns(corner_pieces(under) + corner_pieces(over)).astype(BF16),
        spread_face_table,
    )
    beside = shared_xy(coeff_beside * beside[:, 0:128] + beside[:, 128:256])

    def total(value):
        return jnp.sum(jnp.sum(value.reshape(ROWS // 8, 8, 128), axis=0), axis=(0, 1), keepdims=True)

    def applied(x_ref, spread, z_ref, image_ref):
        for index in range(4):
            at = 128 * index
            z = tile(x_ref, index) + spread[:, at : at + 128]
            put(z_ref, index, z)
            put(
                image_ref,
                index,
                coeff * (tile(field["stiffened"], index) + spread[:, 512 + at : 640 + at])
                + mass[:, at : at + 128] * z,
            )

    def inner(left, right):
        return total(sum(tile(left, index) * tile(right, index) for index in range(4)))

    applied(field["x0"], spread, field["z0"], field["qloc"])
    rz = inner(load_ref, field["z0"])
    zq = inner(field["qloc"], field["z0"])
    for index in range(4):
        put(field["q"], index, shared_xy(tile(field["qloc"], index)))
    partial_face = face_of(field["q"]) + beside
    inner_rows = interior(field["q"], field["x1"])

    face_image = face_of(field["qloc"])
    steep_inner = face_of(field["stiffened"])
    yw = total(
        sum(
            tile(field["x1"], index)
            * (
                coeff * tile(field["stiffened"], index)
                + mass[:, 128 * index : 128 * index + 128] * tile(field["x1"], index)
            )
            for index in range(4)
        )
    )
    zero = jnp.zeros((ROWS, 128), F32)
    qy = inner(field["qloc"], field["x1"])
    back16 = pick.T.astype(BF16)

    def stored(value):
        return permuted(back16, value)

    sent_z0[...] = stored(field["z0"][...])
    sent_r0[...] = stored(r0_ref[...])

    for copy in rest_copies.values():
        copy.wait_recv()
    face = partial_face + faces_arrived(edges[1], 1)
    x_face, stacked, rows1, steep_face = outer(face, field["x1"], inner_rows)
    target = jnp.concatenate([rest[NEAR + p, 0:1] for p in range(-3, 5)], 0) + jnp.concatenate(
        [rest[NEAR + p - 1, 1:2] for p in range(-3, 5)], 0
    )

    def top(parts):
        return {key: value[0:8] for key, value in parts.items()}

    level, from_above, from_below = top(level), top(from_above), top(from_below)
    start = remainder - damp[0:8] * target
    vert = start
    for _ in range(3):
        vert = start + swept(vert, level, from_above, from_below)
    (own,) = corners_of(vert, (3,))

    own_pieces = columns(corner_pieces(own)).astype(BF16)
    spread = dot16(own_pieces, spread_own_face)
    y_face = x_face + spread[:, 0:128]
    w_face = coeff * (steep_inner + steep_face + spread[:, 128:256]) + mass_face * y_face
    late_face = shared_xy(w_face)

    def flipped(value, bit):
        corner = lax.broadcasted_iota(jnp.int32, value.shape, 0)
        return jnp.where(
            corner // bit % 2 == 0, pltpu.roll(value, 8 - bit, 0), pltpu.roll(value, bit, 0)
        )

    edge_sum = flipped(own, 1) + flipped(own, 2) + flipped(own, 4)
    all_sum = jnp.sum(own, axis=0, keepdims=True)
    weighed = own
    for bit in (1, 2, 4):
        weighed = (2.0 * weighed + flipped(weighed, bit)) * (1.0 / 3.0)
    steep = (5.0 / 6.0) * own + (1.0 / 6.0) * (edge_sum - all_sum)
    energy = own * (
        kappa * (steep + 2.0 * rows1[0:8]) + (REACT * weighed + 2.0 * rows1[8:16])
    )
    qy = qy + total(face_image * x_face) + jnp.sum((start * vert / -damp[0:8])[3:4], keepdims=True)
    yw = yw + jnp.sum(energy, keepdims=True)
    yw = yw + total(
        x_face * (coeff * (2.0 * steep_inner + steep_face) + mass_face * x_face)
    )

    hear(2)
    lane = lanes((1, 128))
    mine = jnp.zeros((1, 128), F32)
    for index, value in enumerate((rz, zq, qy, yw)):
        mine = jnp.where(lane == index, value, mine)
    sums_ref[0] = mine

    def send_sums(by):
        remote(sums_ref.at[0], sums_ref.at[by], sum_send, sum_recv, ring(by)).start()

    def both_ways(by, carry):
        send_sums(by)
        send_sums(size - by)
        return carry

    lax.fori_loop(1, REACH, both_ways, 0)
    edges.append(send_faces(late_face, 2))
    lax.fori_loop(REACH, size // 2, both_ways, 0)
    send_sums(size // 2)

    field["stiffened"][...] += dot16(stacked, stiff_face_ref[...])
    applied(field["x1"], dot16(own_pieces, spread_table), field["y"], field["w"])
    for index in range(4):
        put(field["w"], index, shared_xy(tile(field["w"], index)))
    put_face(field["q"], face)
    sent_y[...] = stored(field["y"][...])
    sent_q[...] = stored(field["q"][...])
    sent_w[...] = stored(field["w"][...])
    face = stored(faces_arrived(edges[2], 2))
    sent_w[:, 0:128] += jnp.where(half, face, zero)
    sent_w[:, 384:512] += jnp.where(half, zero, face)
    others = sums_ref.at[pl.ds(1, size - 1)]
    all_sums = remote(others, others, sum_send, sum_recv, ring(1))
    all_sums.wait_recv()
    sums = jnp.sum(sums_ref[...], axis=0)
    rz, zq, qy, yw = (sums[:, index : index + 1] for index in range(4))
    first = rz / zq
    gamma = first * first * qy - rz
    grown = 1.0 + gamma / rz
    second = gamma / (grown * grown * zq - 2.0 * first * grown * qy + first * first * yw)
    straight, bent = first + second * grown, first * second
    steps_ref[0:1] = jnp.broadcast_to(straight, (1, 128))
    steps_ref[1:2] = jnp.broadcast_to(bent, (1, 128))

    all_sums.wait_send()
    for copies in [layer_copies, halo_copies.values(), rest_copies.values()] + edges:
        for copy in copies:
            copy.wait_send()


def combine(z0, y, r0, q, w, steps, solution_ref, residual_ref, solution_part, residual_part, sem):
    straight, bent = steps[0:1, 0:1], steps[1:2, 0:1]
    copies = []
    rows = ROWS // PARTS
    for part in range(PARTS):
        at = pl.ds(part * rows, rows)
        solution_part[at] = straight * z0[at] - bent * y[at]
        copies.append(
            pltpu.make_async_copy(solution_part.at[at], solution_ref.at[at], sem.at[0, part])
        )
        copies[-1].start()
        residual_part[at] = r0[at] - straight * q[at] + bent * w[at]
        copies.append(
            pltpu.make_async_copy(residual_part.at[at], residual_ref.at[at], sem.at[1, part])
        )
        copies[-1].start()
    for copy in copies:
        copy.wait()


def per_device(size, forcing, kappa, elem_order):
    tables = all_tables()
    operands = [forcing, kappa.reshape(1, ROWS), elem_order]
    operands += [jnp.asarray(tables[name], F32) for name in NAMES]
    out = jax.ShapeDtypeStruct((ROWS, NODES), F32)
    steps = jax.ShapeDtypeStruct((8, 128), F32)
    count, close = 2 * REACH + 1, 2 * NEAR + 1
    dma = pltpu.SemaphoreType.DMA
    vmem = pl.BlockSpec(memory_space=pltpu.VMEM)
    hbm = pl.BlockSpec(memory_space=pltpu.HBM)
    stored = pl.pallas_call(
        functools.partial(kernel, size),
        out_shape=(out,) * 5 + (steps,),
        in_specs=[hbm] * len(operands),
        out_specs=(vmem,) * 6,
        scratch_shapes=[pltpu.VMEM(operand.shape, operand.dtype) for operand in operands]
        + [pltpu.VMEM((ROWS, NODES), F32)] * len(FIELDS)
        + [
            pltpu.VMEM((ROWS, 128), F32),
            pltpu.VMEM((ROWS, 16), F32),
            pltpu.VMEM((ROWS, 128), F32),
            pltpu.VMEM((16, ROWS), F32),
            pltpu.VMEM((2 * NODES, NODES), BF16),
            pltpu.VMEM((384, NODES), BF16),
            pltpu.VMEM((3, 2, 128, 128), F32),
            pltpu.VMEM((3, 2, 128, 128), F32),
            pltpu.VMEM((3, 1, ROWS), F32),
            pltpu.VMEM((count, 3, ROWS), F32),
            pltpu.VMEM((close, 2, ROWS), F32),
            pltpu.VMEM((size, 1, 128), F32),
            dma((len(operands) + 3,)),
            dma((3,)),
            dma((3,)),
            dma((count,)),
            dma((count,)),
            dma((close,)),
            dma((close,)),
            dma((3, 2)),
            dma((3, 2)),
            dma,
            dma,
            pltpu.SemaphoreType.REGULAR((3, 2)),
        ],
        compiler_params=pltpu.CompilerParams(
            collective_id=0, has_side_effects=True, vmem_limit_bytes=32 * 1024 * 1024
        ),
        name="solve",
    )(*[pltpu.with_memory_space_constraint(operand, pltpu.HBM) for operand in operands])
    return pl.pallas_call(
        combine,
        out_shape=(out, out),
        in_specs=[vmem] * 6,
        out_specs=(hbm, hbm),
        scratch_shapes=[
            pltpu.VMEM((ROWS, NODES), F32),
            pltpu.VMEM((ROWS, NODES), F32),
            dma((2, PARTS)),
        ],
        compiler_params=pltpu.CompilerParams(vmem_limit_bytes=16 * 1024 * 1024),
        name="combine",
    )(*stored)


def solution(mesh):
    in_specs = (P(("elem", "face"), None), P(("elem", "face")), P(("elem", "face"), None))
    out_specs = (P(("elem", "face"), None), P(("elem", "face"), None))
    size = mesh.shape["elem"] * mesh.shape["face"]
    return jax.shard_map(
        functools.partial(per_device, size),
        mesh=mesh,
        in_specs=in_specs,
        out_specs=out_specs,
        check_vma=False,
    )
```

```python
import functools

import jax
import jax.numpy as jnp
import numpy as np
from jax import lax
from jax.experimental import pallas as pl
from jax.experimental.pallas import tpu as pltpu
from jax.sharding import PartitionSpec as P

EX = 8
EY = 32
ROWS = EX * EY
NODES = 512
REACT = 0.02
OMEGA = 0.6
REACH = 8
NEAR = 4
PARTS = 4
PIECES = ((0, 0), (0, 1), (0, 2), (1, 0), (1, 1), (2, 0))
MESH = pl.DeviceIdType.MESH
F32 = jnp.float32
BF16 = jnp.bfloat16


def legendre_seven(points):
    before = np.ones(8)
    current = np.array(points)
    for degree in range(1, 7):
        following = ((2 * degree + 1) * points * current - degree * before) / (degree + 1)
        before = current
        current = following
    return current


def element_tables():
    points = np.array(
        [
            -1.0,
            -0.8717401485096066,
            -0.5917001814331423,
            -0.2092992179024789,
            0.2092992179024789,
            0.5917001814331423,
            0.8717401485096066,
            1.0,
        ]
    )
    weights = np.array(
        [
            1.0 / 28.0,
            0.2107042271435061,
            0.3411226924835044,
            0.4124587946587038,
            0.4124587946587038,
            0.3411226924835044,
            0.2107042271435061,
            1.0 / 28.0,
        ]
    )
    legendre = legendre_seven(points)
    derivative = np.zeros((8, 8))
    for left_node in range(8):
        for right_node in range(8):
            if left_node != right_node:
                derivative[left_node, right_node] = legendre[left_node] / (
                    legendre[right_node] * (points[left_node] - points[right_node])
                )
    derivative[0, 0] = -14.0
    derivative[7, 7] = 14.0
    stiffness = derivative.T @ (weights[:, None] * derivative)
    mass = np.eye(8) * weights[None, :]
    full_stiff = (
        np.kron(np.kron(mass, mass), stiffness)
        + np.kron(np.kron(mass, stiffness), mass)
        + np.kron(np.kron(stiffness, mass), mass)
    )
    mass_nodes = np.kron(np.kron(weights, weights), weights)
    interp = np.stack([(1.0 - points) / 2.0, (1.0 + points) / 2.0], 1)
    prolong = np.kron(np.kron(interp, interp), interp)
    return full_stiff, mass_nodes, prolong


def pieces_of(table, count):
    parts = []
    for _ in range(count):
        part = table.astype(BF16).astype(np.float64)
        parts.append(part)
        table = table - part
    return parts


def ends(offset):
    if offset == 0:
        return list(range(8)), list(range(8))
    return ([7], [0]) if offset == 1 else ([0], [7])


def all_tables():
    full_stiff, mass_nodes, prolong = element_tables()
    face = np.concatenate([np.arange(64), np.arange(448, 512)])
    facing = np.concatenate([np.arange(448, 512), np.arange(64)])
    diag = np.diag(full_stiff).reshape(8, 8, 8)
    mass = mass_nodes.reshape(8, 8, 8)
    share = np.zeros((16, 8, 8, 8))
    fixed = np.zeros((8, 8, 8))
    for index in range(9):
        offsets = (0, index // 3 - 1, index % 3 - 1)
        mine = np.ix_(*[ends(offset)[0] for offset in offsets])
        theirs = np.ix_(*[ends(offset)[1] for offset in offsets])
        share[index][mine] += diag[theirs]
        fixed[mine] += REACT * mass[theirs]
    share, fixed = share.reshape(16, NODES), fixed.reshape(NODES)
    fixed_face = 2.0 * fixed[face]
    beside = np.zeros((24, 128))
    beside[0:18:2, :64] = share[0:9, facing[:64]]
    beside[1:18:2, 64:] = share[0:9, facing[64:]]
    beside = pieces_of(beside, 2)
    share_face = np.concatenate(
        [share[:, face], beside[0], beside[1], beside[0], np.zeros((8, 128))], 0
    )

    steep = full_stiff @ prolong
    heavy = REACT * mass_nodes[:, None] * prolong

    def stacked(table):
        parts = pieces_of(table, 3)
        return np.concatenate([parts[right] for _, right in PIECES], 0)

    spread = stacked(np.concatenate([prolong.T, steep.T], 1))
    facing_tables = np.concatenate([steep[facing].T, heavy[facing].T], 1)
    lower = facing_tables.copy()
    lower[:, 64:128] = 0.0
    lower[:, 192:256] = 0.0
    spread_face = np.concatenate([stacked(lower), stacked(facing_tables - lower)], 0)

    gather = pieces_of(np.concatenate([steep.T, heavy.T], 0), 2)
    gather = np.concatenate(gather, 0)
    first = np.concatenate(pieces_of(prolong.T, 2), 0)
    return {
        "stiff": full_stiff,
        "spread": spread,
        "spread_face": spread_face,
        "gather": np.concatenate([gather, first], 0),
        "share": share,
        "share_face": share_face,
        "rows": np.concatenate(
            [
                np.stack([fixed, REACT * mass_nodes]),
                np.pad(np.stack([fixed_face, REACT * mass_nodes[face]]), ((0, 0), (0, 384))),
            ],
            0,
        ),
    }


def split(value, pieces):
    parts = []
    for _ in range(pieces):
        part = value.astype(BF16)
        parts.append(part)
        value = value - part.astype(F32)
    return parts


def dot(left, right, dims=((1,), (0,))):
    return lax.dot_general(
        left, right, (dims, ((), ())), precision=lax.Precision.HIGHEST, preferred_element_type=F32
    )


def dot16(left, right, dims=((1,), (0,))):
    return lax.dot_general(left, right, (dims, ((), ())), preferred_element_type=F32)


def lanes(shape):
    return lax.broadcasted_iota(jnp.int32, shape, len(shape) - 1)


def shifted(plane, dy, dx):
    size = plane.shape[1]
    if dy == 0 and dx == 0:
        return plane
    inside = pltpu.roll(plane, -(EX * dy + dx) % size, 1)
    if dx == 0:
        return inside
    around = pltpu.roll(plane, -(EX * dy + dx - EX * dx) % size, 1)
    return jnp.where(lanes(plane.shape) % EX == (EX - 1 if dx == 1 else 0), around, inside)


def added(terms):
    terms = list(terms)
    while len(terms) > 1:
        terms = [sum(terms[at : at + 2]) for at in range(0, len(terms), 2)]
    return terms[0]


def down(plane):
    return pltpu.roll(plane, plane.shape[0] - 1, 0)


def up(plane):
    return pltpu.roll(plane, 1, 0)


def shared_xy(tile):
    cube = tile.reshape(EY, EX, 128)
    lane = lanes(cube.shape)
    nx, ny = lane % 8, lane // 8 % 8
    after = pltpu.roll(pltpu.roll(cube, EX - 1, 1), 7, 2)
    before = pltpu.roll(pltpu.roll(cube, 1, 1), 128 - 7, 2)
    cube = cube + jnp.where(nx == 7, after, jnp.where(nx == 0, before, 0.0))
    after = pltpu.roll(jnp.concatenate([cube[1:], cube[:1]], 0), 56, 2)
    before = pltpu.roll(jnp.concatenate([cube[-1:], cube[:-1]], 0), 128 - 56, 2)
    cube = cube + jnp.where(ny == 7, after, jnp.where(ny == 0, before, 0.0))
    return cube.reshape(ROWS, 128)


def four(layer):
    return [shifted(layer, 0, 0), shifted(layer, 0, -1), shifted(layer, -1, 0), shifted(layer, -1, -1)]


def nine(layer):
    return [shifted(layer, dy, dx) for dy in (-1, 0, 1) for dx in (-1, 0, 1)]


def coarse_stencil(layer4, planes):
    found = {}
    for dy in (-1, 0, 1):
        for dx in (-1, 0, 1):
            rows = (0, 1) if dy == 0 else ((0,) if dy == 1 else (1,))
            cols = (0, 1) if dx == 0 else ((0,) if dx == 1 else (1,))
            differ = abs(dy) + abs(dx) + (1 - planes)
            count = len(rows) * len(cols) * (1 + planes)
            weight = REACT * count * 2.0 ** (3 - differ) / 27.0
            if differ >= 2:
                total = sum(layer4[2 * a + b] for a in rows for b in cols)
                found[dy, dx] = (-1.0 / 6.0) * total + weight
            elif differ == 1:
                found[dy, dx] = weight
    return found


def swept(vert, level, from_above, from_below):
    spread = {key: shifted(vert, *key) for key in from_above}
    above = down(added(from_above[key] * spread[key] for key in from_above))
    below = up(added(from_below[key] * spread[key] for key in from_below))
    here = added([(1.0 - OMEGA) * vert] + [level[key] * spread[key] for key in level])
    return here + (above + below)


NAMES = (
    "stiff",
    "spread",
    "spread_face",
    "gather",
    "share",
    "share_face",
    "rows",
)
FIELDS = ("load", "r0", "x0", "z0", "q", "qloc", "x1", "y", "w", "inverse", "stiffened")


def kernel(size, *refs):
    refs = list(refs)

    def take(count):
        taken = refs[:count]
        del refs[:count]
        return taken

    sources = take(3 + len(NAMES))
    sent_z0, sent_y, sent_r0, sent_q, sent_w, steps_ref = take(6)
    inputs = take(3 + len(NAMES))
    forcing_ref, kappa_ref, order_ref = inputs[:3]
    table = dict(zip(NAMES, inputs[3:]))
    field = dict(zip(FIELDS, take(len(FIELDS))))
    coeff_ref, own_columns_ref, own_face_ref, inner_rows_ref, stiff_ref, stiff_face_ref = take(6)
    edge_out, edge_in, layer, halo, rest, sums_ref = take(6)
    in_sem, layer_send, layer_recv, halo_send, halo_recv = take(5)
    rest_send, rest_recv, edge_send, edge_recv, sum_send, sum_recv, known_sem = take(7)

    core = lax.axis_index("face")
    me = lax.axis_index("elem") * 2 + core

    def ring(by):
        device = lax.rem(me + by + size, size)
        return lax.div(device, 2), lax.rem(device, 2)

    barrier = pltpu.get_barrier_semaphore()
    greeted = [by for by in range(-REACH, REACH + 1) if by != 0]
    for by in greeted:
        pl.semaphore_signal(barrier, inc=1, device_id=ring(by), device_id_type=MESH)

    loads = {
        index: pltpu.make_async_copy(sources[index], inputs[index], in_sem.at[index])
        for index in range(1, len(inputs))
    }
    forcing_loads = [
        pltpu.make_async_copy(
            sources[0].at[:, pl.ds(at, width)],
            forcing_ref.at[:, pl.ds(at, width)],
            in_sem.at[len(inputs) + index],
        )
        for index, (at, width) in enumerate(((0, 128), (384, 128), (128, 256)))
    ]
    loads[2].start()
    forcing_loads[0].start()
    forcing_loads[1].start()
    loads[1].start()
    forcing_loads[2].start()
    for index in range(len(inputs) - 1, 2, -1):
        loads[index].start()

    stages = []
    while REACH << len(stages) < size // 2:
        stages.append(REACH << len(stages))

    def tell(stage):
        if stage < len(stages):
            for way, by in enumerate((stages[stage], -stages[stage])):
                pl.semaphore_signal(
                    known_sem.at[stage, way], inc=1, device_id=ring(by), device_id_type=MESH
                )

    def hear(stage):
        if stage < len(stages):
            for way in range(2):
                pl.semaphore_wait(known_sem.at[stage, way], 1)

    def remote(source, target, send, recv, device):
        return pltpu.make_async_remote_copy(
            src_ref=source,
            dst_ref=target,
            send_sem=send,
            recv_sem=recv,
            device_id=device,
            device_id_type=MESH,
        )

    def to_ring(buffer, send, recv, reach):
        found = {}
        for by in sorted(range(-reach, reach + 1), key=abs):
            if by != 0:
                at = reach - by
                found[by] = remote(buffer.at[reach], buffer.at[at], send.at[at], recv.at[at], ring(by))
        return found

    half = lanes((ROWS, 128)) < 64

    def tile(ref, index):
        return ref[:, 128 * index : 128 * index + 128]

    def put(ref, index, value):
        ref[:, 128 * index : 128 * index + 128] = value

    def face_of(ref):
        return jnp.where(half, tile(ref, 0), tile(ref, 3))

    def put_face(ref, value):
        put(ref, 0, jnp.where(half, value, tile(ref, 0)))
        put(ref, 3, jnp.where(half, tile(ref, 3), value))

    def send_faces(face, turn, both=True):
        top, bottom, part = face[0:128], face[128:256], half[0:128]
        edge_out[turn, 0] = jnp.where(part, pltpu.roll(top, 64, 1), bottom)
        edge_out[turn, 1] = jnp.where(part, top, pltpu.roll(bottom, 64, 1))
        copies = [
            remote(
                edge_out.at[turn, way],
                edge_in.at[turn, way],
                edge_send.at[turn, way],
                edge_recv.at[turn, way],
                ring(1 - 2 * way),
            )
            for way in (1 - core, core)
        ]
        copies[0].start()
        if both:
            copies[1].start()
        return copies

    def faces_arrived(copies, turn):
        for copy in copies:
            copy.wait_recv()
        below, above, part = edge_in[turn, 0], edge_in[turn, 1], half[0:128]
        top = jnp.where(part, below, pltpu.roll(above, 64, 1))
        bottom = jnp.where(part, pltpu.roll(below, 64, 1), above)
        return jnp.concatenate([top, bottom], 0)

    def vertex_sums(each):
        corner = lax.broadcasted_iota(jnp.int32, each.shape, 0)
        even = jnp.where(corner // 2 % 2 == 1, shifted(each, -1, 0), each)
        odd = jnp.where(corner // 2 % 2 == 1, shifted(each, -1, -1), shifted(each, 0, -1))
        each = jnp.where(corner % 2 == 1, odd, even)
        low = jnp.sum(each[0:4], axis=0, keepdims=True)
        high = jnp.sum(each[4:8], axis=0, keepdims=True)
        return low, high

    def gathered(matrix, parts):
        whole = dot16(matrix, parts[0], ((1,), (1,)))
        return whole[0:16] + whole[16:32] + dot16(matrix[0:16], parts[1], ((1,), (1,)))

    def face_lanes(value):
        return jnp.concatenate([value[:, 0:64], value[:, 448:512]], 1)

    def columns(planes):
        return jnp.concatenate(planes, 0).T

    def corner_pieces(corners):
        parts = [part.astype(F32) for part in split(corners, 3)]
        return [parts[left] for left, _ in PIECES]

    row = lax.broadcasted_iota(jnp.int32, (ROWS, ROWS), 0)
    loads[2].wait()
    pick = jnp.where(row == order_ref[...], 1.0, 0.0)
    pick16 = pick.astype(BF16)
    loads[1].wait()
    kappa_rows = jnp.broadcast_to(kappa_ref[...], (16, ROWS))
    kappa = sum(dot16(part, pick16, ((1,), (1,))) for part in split(kappa_rows, 3))[0:8]
    layer[1] = kappa[0:1]
    halo[REACH, 2:3] = kappa[0:1]
    load_ref, r0_ref = field["load"], field["r0"]

    def permuted(matrix, value):
        return sum(dot16(matrix, part) for part in split(value, 3))

    for copy in forcing_loads[:2]:
        copy.wait()
    first_face = shared_xy(permuted(pick16, face_of(forcing_ref)))
    own9 = nine(kappa)
    own_rows = [plane[0:1] for plane in own9] + [jnp.zeros((7, ROWS), F32)]
    own_columns = columns(own_rows)
    coeff_ref[...] = jnp.broadcast_to(own_columns[:, 4:5], (ROWS, 128))
    own_columns_ref[...] = own_columns

    def interior(value, x_ref):
        inverse = field["inverse"]
        zero = jnp.zeros((ROWS, 128), F32)
        put(x_ref, 0, jnp.where(half, zero, tile(inverse, 0) * tile(value, 0)))
        put(x_ref, 1, tile(inverse, 1) * tile(value, 1))
        put(x_ref, 2, tile(inverse, 2) * tile(value, 2))
        put(x_ref, 3, jnp.where(half, tile(inverse, 3) * tile(value, 3), zero))
        parts = split(x_ref[...], 2)
        high, low = stiff_ref[0:NODES], stiff_ref[NODES:]
        field["stiffened"][...] = (
            dot16(parts[0], high) + dot16(parts[1], high) + dot16(parts[0], low)
        )
        return gathered(table["gather"][0:32].astype(BF16), parts)

    def prepare_halo():
        forcing_loads[2].wait()
        load_ref[...] = permuted(pick16, forcing_ref[...])
        for index in range(3, len(inputs)):
            loads[index].wait()
        parts = split(load_ref[...], 2)
        first = table["gather"][32:48].astype(BF16)
        each = dot16(first, parts[0], ((1,), (1,)))
        each = each[0:8] + each[8:16] + dot16(first, parts[1], ((1,), (1,)))[0:8]
        low, high = vertex_sums(each)
        halo[REACH, 0:1] = low
        halo[REACH, 1:2] = high

    def prepare_interior():
        own_columns = own_columns_ref[...]
        fixed = table["rows"][0:1]
        field["inverse"][...] = 1.0 / (dot(own_columns, table["share"][...]) + fixed)
        own_face_ref[...] = dot(own_columns, table["share_face"][0:16]) + table["rows"][2:3, 0:128]
        stiff = table["stiff"][...]
        upper_piece = stiff.astype(BF16)
        stiff_ref[0:NODES] = upper_piece
        stiff_ref[NODES:] = (stiff - upper_piece.astype(F32)).astype(BF16)
        for index in range(4):
            put(r0_ref, index, shared_xy(tile(load_ref, index)))
        inner_rows_ref[...] = interior(r0_ref, field["x0"])
        for at, piece in ((0, 0), (128, 0), (256, NODES)):
            stiff_face_ref[at : at + 64] = stiff_ref[piece : piece + 64]
            stiff_face_ref[at + 64 : at + 128] = stiff_ref[piece + 448 : piece + 512]

    ahead = me < REACH

    @pl.when(ahead)
    def _():
        prepare_halo()
        prepare_interior()

    pl.semaphore_wait(barrier, len(greeted))
    layer_copies = [
        remote(layer.at[1], layer.at[1 - by], layer_send.at[1 - by], layer_recv.at[1 - by], ring(by))
        for by in (1, -1)
    ]
    for copy in layer_copies:
        copy.start()
    edges = [send_faces(first_face, 0)]
    tell(0)

    @pl.when(jnp.logical_not(ahead))
    def _():
        prepare_halo()

    halo_copies = to_ring(halo, halo_send, halo_recv, REACH)
    for copy in halo_copies.values():
        copy.start()

    @pl.when(jnp.logical_not(ahead))
    def _():
        prepare_interior()

    inner_rows = inner_rows_ref[...]
    mass, mass_face = table["rows"][1:2], table["rows"][3:4, 0:128]
    own_face = own_face_ref[...]
    share_two = table["share_face"][16:96].astype(BF16)
    gather = table["gather"][0:32].astype(BF16)
    gather_face = face_lanes(gather)
    stiff_face_face = face_lanes(stiff_face_ref[...])

    hear(0)
    tell(1)
    for copy in layer_copies:
        copy.wait_recv()
    two = jnp.concatenate([layer[0], layer[2], jnp.zeros((6, ROWS), F32)], 0)
    two9 = jnp.concatenate([plane[0:2] for plane in nine(two)] + [two[2:8]], 0)
    two_pieces = [part.astype(F32) for part in split(two9, 2)]
    two_columns = columns([two_pieces[0], two_pieces[0], two_pieces[1], two])
    inverse_face = 1.0 / (own_face + dot16(two_columns.astype(BF16), share_two))
    coeff_beside = jnp.where(half, two_columns[:, 72:73], two_columns[:, 73:74])
    coeff = coeff_ref[...]
    face = first_face + faces_arrived(edges[0], 0)
    put_face(r0_ref, face)

    def outer(face, x_ref, rows):
        x_face = inverse_face * face
        put_face(x_ref, x_face)
        parts = split(x_face, 2)
        rows = rows + gathered(gather_face, parts)
        stacked = jnp.concatenate([parts[0], parts[1], parts[0]], 1)
        return x_face, stacked, rows, dot16(stacked, stiff_face_face)

    x_face, stacked, rows0, steep_face = outer(face, field["x0"], inner_rows)
    rough = coeff * (face_of(field["stiffened"]) + steep_face) + mass_face * x_face
    low, high = vertex_sums(kappa * rows0[0:8] + rows0[8:16])
    rest[NEAR, 0:1] = low
    rest[NEAR, 1:2] = high
    rest_copies = to_ring(rest, rest_send, rest_recv, NEAR)
    for copy in rest_copies.values():
        copy.start()
    edges.append(send_faces(shared_xy(rough), 1))

    hear(1)
    tell(2)
    field["stiffened"][...] += dot16(stacked, stiff_face_ref[...])
    spread_table = table["spread"][...].astype(BF16)
    spread_face_table = table["spread_face"][...].astype(BF16)
    spread_own_face = jnp.concatenate(
        [face_lanes(spread_table[:, 0:NODES]), face_lanes(spread_table[:, NODES:])], 1
    )
    for copy in halo_copies.values():
        copy.wait_recv()
    planes = list(range(-3, REACH + 1)) + list(range(1 - REACH, -3))

    def halo_rows(shift, which):
        return jnp.concatenate([halo[REACH + p + shift, which : which + 1] for p in planes], 0)

    under4, over4 = four(halo_rows(-1, 2)), four(halo_rows(0, 2))
    both4 = [a + b for a, b in zip(under4, over4)]
    diag = (2.0 / 3.0) * (both4[0] + both4[1] + both4[2] + both4[3]) + REACT * 64.0 / 27.0
    damp = -OMEGA / diag
    damp_down, damp_up = up(damp), down(damp)
    level = {key: damp * value for key, value in coarse_stencil(both4, 1).items()}
    from_above = {key: damp_down * value for key, value in coarse_stencil(under4, 0).items()}
    from_below = {key: damp_up * value for key, value in coarse_stencil(over4, 0).items()}
    start = -damp * (halo_rows(0, 0) + halo_rows(-1, 1))
    vert = start
    for _ in range(3):
        vert = start + swept(vert, level, from_above, from_below)
    remainder = (vert - swept(vert, level, from_above, from_below))[0:8]

    def corners_of(vert, lower):
        found = [shifted(vert, *key) for key in ((0, 0), (0, 1), (1, 0), (1, 1))]
        return [
            jnp.concatenate(
                [c[k : k + 1] for c in found] + [c[k + 1 : k + 2] for c in found], 0
            )
            for k in lower
        ]

    own, under, over = corners_of(vert[0:8], (3, 2, 4))
    spread = dot16(columns(corner_pieces(own)).astype(BF16), spread_table)
    beside = dot16(
        columns(corner_pieces(under) + corner_pieces(over)).astype(BF16),
        spread_face_table,
    )
    beside = shared_xy(coeff_beside * beside[:, 0:128] + beside[:, 128:256])

    def total(value):
        quarter = ROWS // 4
        value = added(value[at * quarter : at * quarter + quarter] for at in range(4))
        return jnp.sum(
            jnp.sum(value.reshape(quarter // 8, 8, 128), axis=0), axis=(0, 1), keepdims=True
        )

    def applied(x_ref, spread, z_ref, image_ref):
        for index in range(4):
            at = 128 * index
            z = tile(x_ref, index) + spread[:, at : at + 128]
            put(z_ref, index, z)
            put(
                image_ref,
                index,
                coeff * (tile(field["stiffened"], index) + spread[:, 512 + at : 640 + at])
                + mass[:, at : at + 128] * z,
            )

    def inner(left, right):
        return total(added(tile(left, index) * tile(right, index) for index in range(4)))

    applied(field["x0"], spread, field["z0"], field["qloc"])
    rz = inner(load_ref, field["z0"])
    zq = inner(field["qloc"], field["z0"])
    for index in range(4):
        put(field["q"], index, shared_xy(tile(field["qloc"], index)))
    partial_face = face_of(field["q"]) + beside
    inner_rows = interior(field["q"], field["x1"])

    face_image = face_of(field["qloc"])
    steep_inner = face_of(field["stiffened"])
    yw = total(
        sum(
            tile(field["x1"], index)
            * (
                coeff * tile(field["stiffened"], index)
                + mass[:, 128 * index : 128 * index + 128] * tile(field["x1"], index)
            )
            for index in range(4)
        )
    )
    zero = jnp.zeros((ROWS, 128), F32)
    qy = inner(field["qloc"], field["x1"])
    back16 = pick.T.astype(BF16)

    def stored(value):
        return permuted(back16, value)

    sent_z0[...] = stored(field["z0"][...])
    sent_r0[...] = stored(r0_ref[...])

    for copy in rest_copies.values():
        copy.wait_recv()
    face = partial_face + faces_arrived(edges[1], 1)
    x_face, stacked, rows1, steep_face = outer(face, field["x1"], inner_rows)
    target = jnp.concatenate([rest[NEAR + p, 0:1] for p in range(-3, 5)], 0) + jnp.concatenate(
        [rest[NEAR + p - 1, 1:2] for p in range(-3, 5)], 0
    )

    def top(parts):
        return {key: value[0:8] for key, value in parts.items()}

    level, from_above, from_below = top(level), top(from_above), top(from_below)
    start = remainder - damp[0:8] * target
    vert = start
    for _ in range(3):
        vert = start + swept(vert, level, from_above, from_below)
    (own,) = corners_of(vert, (3,))

    own_pieces = columns(corner_pieces(own)).astype(BF16)
    spread = dot16(own_pieces, spread_own_face)
    y_face = x_face + spread[:, 0:128]
    w_face = coeff * (steep_inner + steep_face + spread[:, 128:256]) + mass_face * y_face
    late_face = shared_xy(w_face)

    def flipped(value, bit):
        corner = lax.broadcasted_iota(jnp.int32, value.shape, 0)
        return jnp.where(
            corner // bit % 2 == 0, pltpu.roll(value, 8 - bit, 0), pltpu.roll(value, bit, 0)
        )

    edge_sum = flipped(own, 1) + flipped(own, 2) + flipped(own, 4)
    all_sum = jnp.sum(own, axis=0, keepdims=True)
    weighed = own
    for bit in (1, 2, 4):
        weighed = (2.0 * weighed + flipped(weighed, bit)) * (1.0 / 3.0)
    steep = (5.0 / 6.0) * own + (1.0 / 6.0) * (edge_sum - all_sum)
    energy = own * (
        kappa * (steep + 2.0 * rows1[0:8]) + (REACT * weighed + 2.0 * rows1[8:16])
    )
    qy = qy + total(face_image * x_face) + jnp.sum((start * vert / -damp[0:8])[3:4], keepdims=True)
    yw = yw + jnp.sum(energy, keepdims=True)
    yw = yw + total(
        x_face * (coeff * (2.0 * steep_inner + steep_face) + mass_face * x_face)
    )

    hear(2)
    lane = lanes((1, 128))
    mine = jnp.zeros((1, 128), F32)
    for index, value in enumerate((rz, zq, qy, yw)):
        mine = jnp.where(lane == index, value, mine)
    sums_ref[0] = mine

    def send_sums(turn, carry):
        by = lax.rem(turn + jnp.where(turn >= me, 1, 0) - me + size, size)
        remote(sums_ref.at[0], sums_ref.at[by], sum_send, sum_recv, ring(by)).start()
        return carry

    lax.fori_loop(0, REACH, send_sums, 0)
    edges.append(send_faces(late_face, 2))
    lax.fori_loop(REACH, size - 1, send_sums, 0)

    field["stiffened"][...] += dot16(stacked, stiff_face_ref[...])
    applied(field["x1"], dot16(own_pieces, spread_table), field["y"], field["w"])
    for index in range(4):
        put(field["w"], index, shared_xy(tile(field["w"], index)))
    put_face(field["q"], face)
    sent_y[...] = stored(field["y"][...])
    sent_q[...] = stored(field["q"][...])
    sent_w[...] = stored(field["w"][...])
    face = stored(faces_arrived(edges[2], 2))
    sent_w[:, 0:128] += jnp.where(half, face, zero)
    sent_w[:, 384:512] += jnp.where(half, zero, face)
    others = sums_ref.at[pl.ds(1, size - 1)]
    all_sums = remote(others, others, sum_send, sum_recv, ring(1))
    all_sums.wait_recv()
    eighth = size // 8
    sums = added(sums_ref[at * eighth : at * eighth + eighth] for at in range(8))
    sums = jnp.sum(sums, axis=0)
    rz, zq, qy, yw = (sums[:, index : index + 1] for index in range(4))
    first = rz / zq
    gamma = first * first * qy - rz
    grown = 1.0 + gamma / rz
    second = gamma / (grown * grown * zq - 2.0 * first * grown * qy + first * first * yw)
    straight, bent = first + second * grown, first * second
    steps_ref[0:1] = jnp.broadcast_to(straight, (1, 128))
    steps_ref[1:2] = jnp.broadcast_to(bent, (1, 128))

    all_sums.wait_send()
    for copies in [layer_copies, halo_copies.values(), rest_copies.values()] + edges:
        for copy in copies:
            copy.wait_send()


def combine(z0, y, r0, q, w, steps, solution_ref, residual_ref, solution_part, residual_part, sem):
    straight, bent = steps[0:1, 0:1], steps[1:2, 0:1]
    copies = []
    rows = ROWS // PARTS
    for part in range(PARTS):
        at = pl.ds(part * rows, rows)
        solution_part[at] = straight * z0[at] - bent * y[at]
        copies.append(
            pltpu.make_async_copy(solution_part.at[at], solution_ref.at[at], sem.at[0, part])
        )
        copies[-1].start()
        residual_part[at] = r0[at] - straight * q[at] + bent * w[at]
        copies.append(
            pltpu.make_async_copy(residual_part.at[at], residual_ref.at[at], sem.at[1, part])
        )
        copies[-1].start()
    for copy in copies:
        copy.wait()


def per_device(size, forcing, kappa, elem_order):
    tables = all_tables()
    operands = [forcing, kappa.reshape(1, ROWS), elem_order]
    operands += [jnp.asarray(tables[name], F32) for name in NAMES]
    out = jax.ShapeDtypeStruct((ROWS, NODES), F32)
    steps = jax.ShapeDtypeStruct((8, 128), F32)
    count, close = 2 * REACH + 1, 2 * NEAR + 1
    dma = pltpu.SemaphoreType.DMA
    vmem = pl.BlockSpec(memory_space=pltpu.VMEM)
    hbm = pl.BlockSpec(memory_space=pltpu.HBM)
    stored = pl.pallas_call(
        functools.partial(kernel, size),
        out_shape=(out,) * 5 + (steps,),
        in_specs=[hbm] * len(operands),
        out_specs=(vmem,) * 6,
        scratch_shapes=[pltpu.VMEM(operand.shape, operand.dtype) for operand in operands]
        + [pltpu.VMEM((ROWS, NODES), F32)] * len(FIELDS)
        + [
            pltpu.VMEM((ROWS, 128), F32),
            pltpu.VMEM((ROWS, 16), F32),
            pltpu.VMEM((ROWS, 128), F32),
            pltpu.VMEM((16, ROWS), F32),
            pltpu.VMEM((2 * NODES, NODES), BF16),
            pltpu.VMEM((384, NODES), BF16),
            pltpu.VMEM((3, 2, 128, 128), F32),
            pltpu.VMEM((3, 2, 128, 128), F32),
            pltpu.VMEM((3, 1, ROWS), F32),
            pltpu.VMEM((count, 3, ROWS), F32),
            pltpu.VMEM((close, 2, ROWS), F32),
            pltpu.VMEM((size, 1, 128), F32),
            dma((len(operands) + 3,)),
            dma((3,)),
            dma((3,)),
            dma((count,)),
            dma((count,)),
            dma((close,)),
            dma((close,)),
            dma((3, 2)),
            dma((3, 2)),
            dma,
            dma,
            pltpu.SemaphoreType.REGULAR((3, 2)),
        ],
        compiler_params=pltpu.CompilerParams(
            collective_id=0, has_side_effects=True, vmem_limit_bytes=32 * 1024 * 1024
        ),
        name="solve",
    )(*[pltpu.with_memory_space_constraint(operand, pltpu.HBM) for operand in operands])
    return pl.pallas_call(
        combine,
        out_shape=(out, out),
        in_specs=[vmem] * 6,
        out_specs=(hbm, hbm),
        scratch_shapes=[
            pltpu.VMEM((ROWS, NODES), F32),
            pltpu.VMEM((ROWS, NODES), F32),
            dma((2, PARTS)),
        ],
        compiler_params=pltpu.CompilerParams(vmem_limit_bytes=16 * 1024 * 1024),
        name="combine",
    )(*stored)


def solution(mesh):
    in_specs = (P(("elem", "face"), None), P(("elem", "face")), P(("elem", "face"), None))
    out_specs = (P(("elem", "face"), None), P(("elem", "face"), None))
    size = mesh.shape["elem"] * mesh.shape["face"]
    return jax.shard_map(
        functools.partial(per_device, size),
        mesh=mesh,
        in_specs=in_specs,
        out_specs=out_specs,
        check_vma=False,
    )
```

```python
import functools

import jax
import jax.numpy as jnp
import numpy as np
from jax import lax
from jax.experimental import pallas as pl
from jax.experimental.pallas import tpu as pltpu
from jax.sharding import PartitionSpec as P

EX = 8
EY = 32
ROWS = EX * EY
NODES = 512
REACT = 0.02
OMEGA = 0.6
REACH = 8
NEAR = 4
PARTS = 4
PIECES = ((0, 0), (0, 1), (0, 2), (1, 0), (1, 1), (2, 0))
MESH = pl.DeviceIdType.MESH
F32 = jnp.float32
BF16 = jnp.bfloat16


def legendre_seven(points):
    before = np.ones(8)
    current = np.array(points)
    for degree in range(1, 7):
        following = ((2 * degree + 1) * points * current - degree * before) / (degree + 1)
        before = current
        current = following
    return current


def element_tables():
    points = np.array(
        [
            -1.0,
            -0.8717401485096066,
            -0.5917001814331423,
            -0.2092992179024789,
            0.2092992179024789,
            0.5917001814331423,
            0.8717401485096066,
            1.0,
        ]
    )
    weights = np.array(
        [
            1.0 / 28.0,
            0.2107042271435061,
            0.3411226924835044,
            0.4124587946587038,
            0.4124587946587038,
            0.3411226924835044,
            0.2107042271435061,
            1.0 / 28.0,
        ]
    )
    legendre = legendre_seven(points)
    derivative = np.zeros((8, 8))
    for left_node in range(8):
        for right_node in range(8):
            if left_node != right_node:
                derivative[left_node, right_node] = legendre[left_node] / (
                    legendre[right_node] * (points[left_node] - points[right_node])
                )
    derivative[0, 0] = -14.0
    derivative[7, 7] = 14.0
    stiffness = derivative.T @ (weights[:, None] * derivative)
    mass = np.eye(8) * weights[None, :]
    full_stiff = (
        np.kron(np.kron(mass, mass), stiffness)
        + np.kron(np.kron(mass, stiffness), mass)
        + np.kron(np.kron(stiffness, mass), mass)
    )
    mass_nodes = np.kron(np.kron(weights, weights), weights)
    interp = np.stack([(1.0 - points) / 2.0, (1.0 + points) / 2.0], 1)
    prolong = np.kron(np.kron(interp, interp), interp)
    return full_stiff, mass_nodes, prolong


def pieces_of(table, count):
    parts = []
    for _ in range(count):
        part = table.astype(BF16).astype(np.float64)
        parts.append(part)
        table = table - part
    return parts


def ends(offset):
    if offset == 0:
        return list(range(8)), list(range(8))
    return ([7], [0]) if offset == 1 else ([0], [7])


def all_tables():
    full_stiff, mass_nodes, prolong = element_tables()
    face = np.concatenate([np.arange(64), np.arange(448, 512)])
    facing = np.concatenate([np.arange(448, 512), np.arange(64)])
    diag = np.diag(full_stiff).reshape(8, 8, 8)
    mass = mass_nodes.reshape(8, 8, 8)
    share = np.zeros((16, 8, 8, 8))
    fixed = np.zeros((8, 8, 8))
    for index in range(9):
        offsets = (0, index // 3 - 1, index % 3 - 1)
        mine = np.ix_(*[ends(offset)[0] for offset in offsets])
        theirs = np.ix_(*[ends(offset)[1] for offset in offsets])
        share[index][mine] += diag[theirs]
        fixed[mine] += REACT * mass[theirs]
    share, fixed = share.reshape(16, NODES), fixed.reshape(NODES)
    fixed_face = 2.0 * fixed[face]
    beside = np.zeros((24, 128))
    beside[0:18:2, :64] = share[0:9, facing[:64]]
    beside[1:18:2, 64:] = share[0:9, facing[64:]]
    beside = pieces_of(beside, 2)
    share_face = np.concatenate(
        [share[:, face], beside[0], beside[1], beside[0], np.zeros((8, 128))], 0
    )

    steep = full_stiff @ prolong
    heavy = REACT * mass_nodes[:, None] * prolong

    def stacked(table):
        parts = pieces_of(table, 3)
        return np.concatenate([parts[right] for _, right in PIECES], 0)

    spread = stacked(np.concatenate([prolong.T, steep.T], 1))
    facing_tables = np.concatenate([steep[facing].T, heavy[facing].T], 1)
    lower = facing_tables.copy()
    lower[:, 64:128] = 0.0
    lower[:, 192:256] = 0.0
    spread_face = np.concatenate([stacked(lower), stacked(facing_tables - lower)], 0)

    gather = pieces_of(np.concatenate([steep.T, heavy.T], 0), 2)
    gather = np.concatenate(gather, 0)
    first = np.concatenate(pieces_of(prolong.T, 2), 0)
    return {
        "stiff": full_stiff,
        "spread": spread,
        "spread_face": spread_face,
        "gather": np.concatenate([gather, first], 0),
        "share": share,
        "share_face": share_face,
        "rows": np.concatenate(
            [
                np.stack([fixed, REACT * mass_nodes]),
                np.pad(np.stack([fixed_face, REACT * mass_nodes[face]]), ((0, 0), (0, 384))),
            ],
            0,
        ),
    }


def split(value, pieces):
    parts = []
    for _ in range(pieces):
        part = value.astype(BF16)
        parts.append(part)
        value = value - part.astype(F32)
    return parts


def dot(left, right, dims=((1,), (0,))):
    return lax.dot_general(
        left, right, (dims, ((), ())), precision=lax.Precision.HIGHEST, preferred_element_type=F32
    )


def dot16(left, right, dims=((1,), (0,))):
    return lax.dot_general(left, right, (dims, ((), ())), preferred_element_type=F32)


def lanes(shape):
    return lax.broadcasted_iota(jnp.int32, shape, len(shape) - 1)


def shifted(plane, dy, dx):
    size = plane.shape[1]
    if dy == 0 and dx == 0:
        return plane
    inside = pltpu.roll(plane, -(EX * dy + dx) % size, 1)
    if dx == 0:
        return inside
    around = pltpu.roll(plane, -(EX * dy + dx - EX * dx) % size, 1)
    return jnp.where(lanes(plane.shape) % EX == (EX - 1 if dx == 1 else 0), around, inside)


def added(terms):
    terms = list(terms)
    while len(terms) > 1:
        terms = [sum(terms[at : at + 2]) for at in range(0, len(terms), 2)]
    return terms[0]


def down(plane):
    return pltpu.roll(plane, plane.shape[0] - 1, 0)


def up(plane):
    return pltpu.roll(plane, 1, 0)


def shared_xy(tile):
    cube = tile.reshape(EY, EX, 128)
    lane = lanes(cube.shape)
    nx, ny = lane % 8, lane // 8 % 8
    after = pltpu.roll(pltpu.roll(cube, EX - 1, 1), 7, 2)
    before = pltpu.roll(pltpu.roll(cube, 1, 1), 128 - 7, 2)
    cube = cube + jnp.where(nx == 7, after, jnp.where(nx == 0, before, 0.0))
    after = pltpu.roll(jnp.concatenate([cube[1:], cube[:1]], 0), 56, 2)
    before = pltpu.roll(jnp.concatenate([cube[-1:], cube[:-1]], 0), 128 - 56, 2)
    cube = cube + jnp.where(ny == 7, after, jnp.where(ny == 0, before, 0.0))
    return cube.reshape(ROWS, 128)


def four(layer):
    return [shifted(layer, 0, 0), shifted(layer, 0, -1), shifted(layer, -1, 0), shifted(layer, -1, -1)]


def nine(layer):
    return [shifted(layer, dy, dx) for dy in (-1, 0, 1) for dx in (-1, 0, 1)]


def coarse_stencil(layer4, planes):
    found = {}
    for dy in (-1, 0, 1):
        for dx in (-1, 0, 1):
            rows = (0, 1) if dy == 0 else ((0,) if dy == 1 else (1,))
            cols = (0, 1) if dx == 0 else ((0,) if dx == 1 else (1,))
            differ = abs(dy) + abs(dx) + (1 - planes)
            count = len(rows) * len(cols) * (1 + planes)
            weight = REACT * count * 2.0 ** (3 - differ) / 27.0
            if differ >= 2:
                total = sum(layer4[2 * a + b] for a in rows for b in cols)
                found[dy, dx] = (-1.0 / 6.0) * total + weight
            elif differ == 1:
                found[dy, dx] = weight
    return found


def swept(vert, level, from_above, from_below):
    spread = {key: shifted(vert, *key) for key in from_above}
    above = down(added(from_above[key] * spread[key] for key in from_above))
    below = up(added(from_below[key] * spread[key] for key in from_below))
    here = added([(1.0 - OMEGA) * vert] + [level[key] * spread[key] for key in level])
    return here + (above + below)


NAMES = (
    "stiff",
    "spread",
    "spread_face",
    "gather",
    "share",
    "share_face",
    "rows",
)
FIELDS = ("load", "r0", "x0", "z0", "q", "qloc", "x1", "y", "w", "inverse", "stiffened")


def kernel(size, *refs):
    refs = list(refs)

    def take(count):
        taken = refs[:count]
        del refs[:count]
        return taken

    sources = take(3 + len(NAMES))
    sent_z0, sent_y, sent_r0, sent_q, sent_w, steps_ref = take(6)
    inputs = take(3 + len(NAMES))
    forcing_ref, kappa_ref, order_ref = inputs[:3]
    table = dict(zip(NAMES, inputs[3:]))
    field = dict(zip(FIELDS, take(len(FIELDS))))
    coeff_ref, own_columns_ref, own_face_ref, inner_rows_ref, stiff_ref, stiff_face_ref = take(6)
    edge_out, edge_in, layer, halo, rest, sums_ref = take(6)
    in_sem, layer_send, layer_recv, halo_send, halo_recv = take(5)
    rest_send, rest_recv, edge_send, edge_recv, sum_send, sum_recv, known_sem = take(7)

    core = lax.axis_index("face")
    me = lax.axis_index("elem") * 2 + core

    def ring(by):
        device = lax.rem(me + by + size, size)
        return lax.div(device, 2), lax.rem(device, 2)

    barrier = pltpu.get_barrier_semaphore()
    greeted = [by for by in range(-REACH, REACH + 1) if by != 0]
    for by in greeted:
        pl.semaphore_signal(barrier, inc=1, device_id=ring(by), device_id_type=MESH)

    loads = {
        index: pltpu.make_async_copy(sources[index], inputs[index], in_sem.at[index])
        for index in range(1, len(inputs))
    }
    forcing_loads = [
        pltpu.make_async_copy(
            sources[0].at[:, pl.ds(at, width)],
            forcing_ref.at[:, pl.ds(at, width)],
            in_sem.at[len(inputs) + index],
        )
        for index, (at, width) in enumerate(((0, 128), (384, 128), (128, 256)))
    ]
    loads[2].start()
    forcing_loads[0].start()
    forcing_loads[1].start()
    loads[1].start()
    forcing_loads[2].start()
    for index in range(len(inputs) - 1, 2, -1):
        loads[index].start()

    stages = []
    while REACH << len(stages) < size // 2:
        stages.append(REACH << len(stages))

    def tell(stage):
        if stage < len(stages):
            for way, by in enumerate((stages[stage], -stages[stage])):
                pl.semaphore_signal(
                    known_sem.at[stage, way], inc=1, device_id=ring(by), device_id_type=MESH
                )

    def hear(stage):
        if stage < len(stages):
            for way in range(2):
                pl.semaphore_wait(known_sem.at[stage, way], 1)

    def remote(source, target, send, recv, device):
        return pltpu.make_async_remote_copy(
            src_ref=source,
            dst_ref=target,
            send_sem=send,
            recv_sem=recv,
            device_id=device,
            device_id_type=MESH,
        )

    def slot(place, reach):
        return 2 * reach if place == reach else place - (place > reach)

    def to_ring(buffer, send, recv, reach):
        for by in sorted(range(-reach, reach + 1), key=abs):
            if by != 0:
                remote(
                    buffer.at[2 * reach], buffer.at[slot(reach - by, reach)], send, recv, ring(by)
                ).start()
        others = buffer.at[pl.ds(0, 2 * reach)]
        return remote(others, others, send, recv, ring(1))

    half = lanes((ROWS, 128)) < 64

    def tile(ref, index):
        return ref[:, 128 * index : 128 * index + 128]

    def put(ref, index, value):
        ref[:, 128 * index : 128 * index + 128] = value

    def face_of(ref):
        return jnp.where(half, tile(ref, 0), tile(ref, 3))

    def put_face(ref, value):
        put(ref, 0, jnp.where(half, value, tile(ref, 0)))
        put(ref, 3, jnp.where(half, tile(ref, 3), value))

    def send_faces(face, turn):
        top, bottom, part = face[0:128], face[128:256], half[0:128]
        edge_out[turn, 0] = jnp.where(part, pltpu.roll(top, 64, 1), bottom)
        edge_out[turn, 1] = jnp.where(part, top, pltpu.roll(bottom, 64, 1))
        copies = [
            remote(
                edge_out.at[turn, way],
                edge_in.at[turn, way],
                edge_send.at[turn],
                edge_recv.at[turn],
                ring(1 - 2 * way),
            )
            for way in (1 - core, core)
        ]
        for copy in copies:
            copy.start()
        return remote(
            edge_out.at[turn], edge_in.at[turn], edge_send.at[turn], edge_recv.at[turn], ring(1)
        )

    def faces_arrived(copies, turn):
        copies.wait_recv()
        below, above, part = edge_in[turn, 0], edge_in[turn, 1], half[0:128]
        top = jnp.where(part, below, pltpu.roll(above, 64, 1))
        bottom = jnp.where(part, pltpu.roll(below, 64, 1), above)
        return jnp.concatenate([top, bottom], 0)

    def vertex_sums(each):
        corner = lax.broadcasted_iota(jnp.int32, each.shape, 0)
        even = jnp.where(corner // 2 % 2 == 1, shifted(each, -1, 0), each)
        odd = jnp.where(corner // 2 % 2 == 1, shifted(each, -1, -1), shifted(each, 0, -1))
        each = jnp.where(corner % 2 == 1, odd, even)
        low = jnp.sum(each[0:4], axis=0, keepdims=True)
        high = jnp.sum(each[4:8], axis=0, keepdims=True)
        return low, high

    def gathered(matrix, parts):
        whole = dot16(matrix, parts[0], ((1,), (1,)))
        return whole[0:16] + whole[16:32] + dot16(matrix[0:16], parts[1], ((1,), (1,)))

    def face_lanes(value):
        return jnp.concatenate([value[:, 0:64], value[:, 448:512]], 1)

    def columns(planes):
        return jnp.concatenate(planes, 0).T

    def corner_pieces(corners):
        parts = [part.astype(F32) for part in split(corners, 3)]
        return [parts[left] for left, _ in PIECES]

    row = lax.broadcasted_iota(jnp.int32, (ROWS, ROWS), 0)
    loads[2].wait()
    pick = jnp.where(row == order_ref[...], 1.0, 0.0)
    pick16 = pick.astype(BF16)
    loads[1].wait()
    kappa_rows = jnp.broadcast_to(kappa_ref[...], (16, ROWS))
    kappa = sum(dot16(part, pick16, ((1,), (1,))) for part in split(kappa_rows, 3))[0:8]
    layer[2] = kappa[0:1]
    halo[2 * REACH, 2:3] = kappa[0:1]
    load_ref, r0_ref = field["load"], field["r0"]

    def permuted(matrix, value):
        return sum(dot16(matrix, part) for part in split(value, 3))

    for copy in forcing_loads[:2]:
        copy.wait()
    first_face = shared_xy(permuted(pick16, face_of(forcing_ref)))
    own9 = nine(kappa)
    own_rows = [plane[0:1] for plane in own9] + [jnp.zeros((7, ROWS), F32)]
    own_columns = columns(own_rows)
    coeff_ref[...] = jnp.broadcast_to(own_columns[:, 4:5], (ROWS, 128))
    own_columns_ref[...] = own_columns

    def interior(value, x_ref):
        inverse = field["inverse"]
        zero = jnp.zeros((ROWS, 128), F32)
        put(x_ref, 0, jnp.where(half, zero, tile(inverse, 0) * tile(value, 0)))
        put(x_ref, 1, tile(inverse, 1) * tile(value, 1))
        put(x_ref, 2, tile(inverse, 2) * tile(value, 2))
        put(x_ref, 3, jnp.where(half, tile(inverse, 3) * tile(value, 3), zero))
        parts = split(x_ref[...], 2)
        high, low = stiff_ref[0:NODES], stiff_ref[NODES:]
        field["stiffened"][...] = (
            dot16(parts[0], high) + dot16(parts[1], high) + dot16(parts[0], low)
        )
        return gathered(table["gather"][0:32].astype(BF16), parts)

    def prepare_halo():
        forcing_loads[2].wait()
        load_ref[...] = permuted(pick16, forcing_ref[...])
        for index in range(3, len(inputs)):
            loads[index].wait()
        parts = split(load_ref[...], 2)
        first = table["gather"][32:48].astype(BF16)
        each = dot16(first, parts[0], ((1,), (1,)))
        each = each[0:8] + each[8:16] + dot16(first, parts[1], ((1,), (1,)))[0:8]
        low, high = vertex_sums(each)
        halo[2 * REACH, 0:1] = low
        halo[2 * REACH, 1:2] = high

    def prepare_interior():
        own_columns = own_columns_ref[...]
        fixed = table["rows"][0:1]
        field["inverse"][...] = 1.0 / (dot(own_columns, table["share"][...]) + fixed)
        own_face_ref[...] = dot(own_columns, table["share_face"][0:16]) + table["rows"][2:3, 0:128]
        stiff = table["stiff"][...]
        upper_piece = stiff.astype(BF16)
        stiff_ref[0:NODES] = upper_piece
        stiff_ref[NODES:] = (stiff - upper_piece.astype(F32)).astype(BF16)
        for index in range(4):
            put(r0_ref, index, shared_xy(tile(load_ref, index)))
        inner_rows_ref[...] = interior(r0_ref, field["x0"])
        for at, piece in ((0, 0), (128, 0), (256, NODES)):
            stiff_face_ref[at : at + 64] = stiff_ref[piece : piece + 64]
            stiff_face_ref[at + 64 : at + 128] = stiff_ref[piece + 448 : piece + 512]

    ahead = me < REACH

    @pl.when(ahead)
    def _():
        prepare_halo()
        prepare_interior()

    pl.semaphore_wait(barrier, len(greeted))
    layer_copies = to_ring(layer, layer_send, layer_recv, 1)
    edges = [send_faces(first_face, 0)]
    tell(0)

    @pl.when(jnp.logical_not(ahead))
    def _():
        prepare_halo()

    halo_copies = to_ring(halo, halo_send, halo_recv, REACH)

    @pl.when(jnp.logical_not(ahead))
    def _():
        prepare_interior()

    inner_rows = inner_rows_ref[...]
    mass, mass_face = table["rows"][1:2], table["rows"][3:4, 0:128]
    own_face = own_face_ref[...]
    share_two = table["share_face"][16:96].astype(BF16)
    gather = table["gather"][0:32].astype(BF16)
    gather_face = face_lanes(gather)
    stiff_face_face = face_lanes(stiff_face_ref[...])

    hear(0)
    tell(1)
    layer_copies.wait_recv()
    two = jnp.concatenate([layer[0], layer[1], jnp.zeros((6, ROWS), F32)], 0)
    two9 = jnp.concatenate([plane[0:2] for plane in nine(two)] + [two[2:8]], 0)
    two_pieces = [part.astype(F32) for part in split(two9, 2)]
    two_columns = columns([two_pieces[0], two_pieces[0], two_pieces[1], two])
    inverse_face = 1.0 / (own_face + dot16(two_columns.astype(BF16), share_two))
    coeff_beside = jnp.where(half, two_columns[:, 72:73], two_columns[:, 73:74])
    coeff = coeff_ref[...]
    face = first_face + faces_arrived(edges[0], 0)
    put_face(r0_ref, face)

    def outer(face, x_ref, rows):
        x_face = inverse_face * face
        put_face(x_ref, x_face)
        parts = split(x_face, 2)
        rows = rows + gathered(gather_face, parts)
        stacked = jnp.concatenate([parts[0], parts[1], parts[0]], 1)
        return x_face, stacked, rows, dot16(stacked, stiff_face_face)

    x_face, stacked, rows0, steep_face = outer(face, field["x0"], inner_rows)
    rough = coeff * (face_of(field["stiffened"]) + steep_face) + mass_face * x_face
    low, high = vertex_sums(kappa * rows0[0:8] + rows0[8:16])
    rest[2 * NEAR, 0:1] = low
    rest[2 * NEAR, 1:2] = high
    rest_copies = to_ring(rest, rest_send, rest_recv, NEAR)
    edges.append(send_faces(shared_xy(rough), 1))

    hear(1)
    tell(2)
    field["stiffened"][...] += dot16(stacked, stiff_face_ref[...])
    spread_table = table["spread"][...].astype(BF16)
    spread_face_table = table["spread_face"][...].astype(BF16)
    spread_own_face = jnp.concatenate(
        [face_lanes(spread_table[:, 0:NODES]), face_lanes(spread_table[:, NODES:])], 1
    )
    halo_copies.wait_recv()
    planes = list(range(-3, REACH + 1)) + list(range(1 - REACH, -3))

    def halo_rows(shift, which):
        places = [slot(REACH + p + shift, REACH) for p in planes]
        return jnp.concatenate([halo[place, which : which + 1] for place in places], 0)

    under4, over4 = four(halo_rows(-1, 2)), four(halo_rows(0, 2))
    both4 = [a + b for a, b in zip(under4, over4)]
    diag = (2.0 / 3.0) * (both4[0] + both4[1] + both4[2] + both4[3]) + REACT * 64.0 / 27.0
    damp = -OMEGA / diag
    damp_down, damp_up = up(damp), down(damp)
    level = {key: damp * value for key, value in coarse_stencil(both4, 1).items()}
    from_above = {key: damp_down * value for key, value in coarse_stencil(under4, 0).items()}
    from_below = {key: damp_up * value for key, value in coarse_stencil(over4, 0).items()}
    start = -damp * (halo_rows(0, 0) + halo_rows(-1, 1))
    vert = start
    for _ in range(3):
        vert = start + swept(vert, level, from_above, from_below)
    remainder = (vert - swept(vert, level, from_above, from_below))[0:8]

    def corners_of(vert, lower):
        found = [shifted(vert, *key) for key in ((0, 0), (0, 1), (1, 0), (1, 1))]
        return [
            jnp.concatenate(
                [c[k : k + 1] for c in found] + [c[k + 1 : k + 2] for c in found], 0
            )
            for k in lower
        ]

    own, under, over = corners_of(vert[0:8], (3, 2, 4))
    spread = dot16(columns(corner_pieces(own)).astype(BF16), spread_table)
    beside = dot16(
        columns(corner_pieces(under) + corner_pieces(over)).astype(BF16),
        spread_face_table,
    )
    beside = shared_xy(coeff_beside * beside[:, 0:128] + beside[:, 128:256])

    def total(value):
        quarter = ROWS // 4
        value = added(value[at * quarter : at * quarter + quarter] for at in range(4))
        return jnp.sum(
            jnp.sum(value.reshape(quarter // 8, 8, 128), axis=0), axis=(0, 1), keepdims=True
        )

    def applied(x_ref, spread, z_ref, image_ref):
        for index in range(4):
            at = 128 * index
            z = tile(x_ref, index) + spread[:, at : at + 128]
            put(z_ref, index, z)
            put(
                image_ref,
                index,
                coeff * (tile(field["stiffened"], index) + spread[:, 512 + at : 640 + at])
                + mass[:, at : at + 128] * z,
            )

    def inner(left, right):
        return total(added(tile(left, index) * tile(right, index) for index in range(4)))

    applied(field["x0"], spread, field["z0"], field["qloc"])
    rz = inner(load_ref, field["z0"])
    zq = inner(field["qloc"], field["z0"])
    for index in range(4):
        put(field["q"], index, shared_xy(tile(field["qloc"], index)))
    partial_face = face_of(field["q"]) + beside
    inner_rows = interior(field["q"], field["x1"])

    face_image = face_of(field["qloc"])
    steep_inner = face_of(field["stiffened"])
    yw = total(
        sum(
            tile(field["x1"], index)
            * (
                coeff * tile(field["stiffened"], index)
                + mass[:, 128 * index : 128 * index + 128] * tile(field["x1"], index)
            )
            for index in range(4)
        )
    )
    zero = jnp.zeros((ROWS, 128), F32)
    qy = inner(field["qloc"], field["x1"])
    back16 = pick.T.astype(BF16)

    def stored(value):
        return permuted(back16, value)

    sent_z0[...] = stored(field["z0"][...])
    sent_r0[...] = stored(r0_ref[...])

    rest_copies.wait_recv()
    face = partial_face + faces_arrived(edges[1], 1)
    x_face, stacked, rows1, steep_face = outer(face, field["x1"], inner_rows)
    target = jnp.concatenate(
        [rest[slot(NEAR + p, NEAR), 0:1] for p in range(-3, 5)], 0
    ) + jnp.concatenate([rest[slot(NEAR + p - 1, NEAR), 1:2] for p in range(-3, 5)], 0)

    def top(parts):
        return {key: value[0:8] for key, value in parts.items()}

    level, from_above, from_below = top(level), top(from_above), top(from_below)
    start = remainder - damp[0:8] * target
    vert = start
    for _ in range(3):
        vert = start + swept(vert, level, from_above, from_below)
    (own,) = corners_of(vert, (3,))

    own_pieces = columns(corner_pieces(own)).astype(BF16)
    spread = dot16(own_pieces, spread_own_face)
    y_face = x_face + spread[:, 0:128]
    w_face = coeff * (steep_inner + steep_face + spread[:, 128:256]) + mass_face * y_face
    late_face = shared_xy(w_face)

    def flipped(value, bit):
        corner = lax.broadcasted_iota(jnp.int32, value.shape, 0)
        return jnp.where(
            corner // bit % 2 == 0, pltpu.roll(value, 8 - bit, 0), pltpu.roll(value, bit, 0)
        )

    edge_sum = flipped(own, 1) + flipped(own, 2) + flipped(own, 4)
    all_sum = jnp.sum(own, axis=0, keepdims=True)
    weighed = own
    for bit in (1, 2, 4):
        weighed = (2.0 * weighed + flipped(weighed, bit)) * (1.0 / 3.0)
    steep = (5.0 / 6.0) * own + (1.0 / 6.0) * (edge_sum - all_sum)
    energy = own * (
        kappa * (steep + 2.0 * rows1[0:8]) + (REACT * weighed + 2.0 * rows1[8:16])
    )
    qy = qy + total(face_image * x_face) + jnp.sum((start * vert / -damp[0:8])[3:4], keepdims=True)
    yw = yw + jnp.sum(energy, keepdims=True)
    yw = yw + total(
        x_face * (coeff * (2.0 * steep_inner + steep_face) + mass_face * x_face)
    )

    hear(2)
    lane = lanes((1, 128))
    mine = jnp.zeros((1, 128), F32)
    for index, value in enumerate((rz, zq, qy, yw)):
        mine = jnp.where(lane == index, value, mine)
    sums_ref[0] = mine

    def send_sums(turn, carry):
        by = lax.rem(turn + jnp.where(turn >= me, 1, 0) - me + size, size)
        remote(sums_ref.at[0], sums_ref.at[by], sum_send, sum_recv, ring(by)).start()
        return carry

    lax.fori_loop(0, REACH, send_sums, 0)
    edges.append(send_faces(late_face, 2))
    lax.fori_loop(REACH, size - 1, send_sums, 0)

    field["stiffened"][...] += dot16(stacked, stiff_face_ref[...])
    applied(field["x1"], dot16(own_pieces, spread_table), field["y"], field["w"])
    for index in range(4):
        put(field["w"], index, shared_xy(tile(field["w"], index)))
    put_face(field["q"], face)
    sent_y[...] = stored(field["y"][...])
    sent_q[...] = stored(field["q"][...])
    sent_w[...] = stored(field["w"][...])
    others = sums_ref.at[pl.ds(1, size - 1)]
    all_sums = remote(others, others, sum_send, sum_recv, ring(1))
    all_sums.wait_send()
    for copies in [layer_copies, halo_copies, rest_copies] + edges:
        copies.wait_send()
    face = stored(faces_arrived(edges[2], 2))
    sent_w[:, 0:128] += jnp.where(half, face, zero)
    sent_w[:, 384:512] += jnp.where(half, zero, face)
    all_sums.wait_recv()
    eighth = size // 8
    sums = added(sums_ref[at * eighth : at * eighth + eighth] for at in range(8))
    sums = jnp.sum(sums, axis=0)
    rz, zq, qy, yw = (sums[:, index : index + 1] for index in range(4))
    first = rz / zq
    gamma = first * first * qy - rz
    grown = 1.0 + gamma / rz
    second = gamma / (grown * grown * zq - 2.0 * first * grown * qy + first * first * yw)
    straight, bent = first + second * grown, first * second
    steps_ref[0:1] = jnp.broadcast_to(straight, (1, 128))
    steps_ref[1:2] = jnp.broadcast_to(bent, (1, 128))


def combine(z0, y, r0, q, w, steps, solution_ref, residual_ref, solution_part, residual_part, sem):
    straight, bent = steps[0:1, 0:1], steps[1:2, 0:1]
    copies = []
    rows = ROWS // PARTS
    for part in range(PARTS):
        at = pl.ds(part * rows, rows)
        solution_part[at] = straight * z0[at] - bent * y[at]
        copies.append(
            pltpu.make_async_copy(solution_part.at[at], solution_ref.at[at], sem.at[0, part])
        )
        copies[-1].start()
        residual_part[at] = r0[at] - straight * q[at] + bent * w[at]
        copies.append(
            pltpu.make_async_copy(residual_part.at[at], residual_ref.at[at], sem.at[1, part])
        )
        copies[-1].start()
    for copy in copies:
        copy.wait()


def per_device(size, forcing, kappa, elem_order):
    tables = all_tables()
    operands = [forcing, kappa.reshape(1, ROWS), elem_order]
    operands += [jnp.asarray(tables[name], F32) for name in NAMES]
    out = jax.ShapeDtypeStruct((ROWS, NODES), F32)
    steps = jax.ShapeDtypeStruct((8, 128), F32)
    count, close = 2 * REACH + 1, 2 * NEAR + 1
    dma = pltpu.SemaphoreType.DMA
    vmem = pl.BlockSpec(memory_space=pltpu.VMEM)
    hbm = pl.BlockSpec(memory_space=pltpu.HBM)
    stored = pl.pallas_call(
        functools.partial(kernel, size),
        out_shape=(out,) * 5 + (steps,),
        in_specs=[hbm] * len(operands),
        out_specs=(vmem,) * 6,
        scratch_shapes=[pltpu.VMEM(operand.shape, operand.dtype) for operand in operands]
        + [pltpu.VMEM((ROWS, NODES), F32)] * len(FIELDS)
        + [
            pltpu.VMEM((ROWS, 128), F32),
            pltpu.VMEM((ROWS, 16), F32),
            pltpu.VMEM((ROWS, 128), F32),
            pltpu.VMEM((16, ROWS), F32),
            pltpu.VMEM((2 * NODES, NODES), BF16),
            pltpu.VMEM((384, NODES), BF16),
            pltpu.VMEM((3, 2, 128, 128), F32),
            pltpu.VMEM((3, 2, 128, 128), F32),
            pltpu.VMEM((3, 1, ROWS), F32),
            pltpu.VMEM((count, 3, ROWS), F32),
            pltpu.VMEM((close, 2, ROWS), F32),
            pltpu.VMEM((size, 1, 128), F32),
            dma((len(operands) + 3,)),
            dma,
            dma,
            dma,
            dma,
            dma,
            dma,
            dma((3,)),
            dma((3,)),
            dma,
            dma,
            pltpu.SemaphoreType.REGULAR((3, 2)),
        ],
        compiler_params=pltpu.CompilerParams(
            collective_id=0, has_side_effects=True, vmem_limit_bytes=32 * 1024 * 1024
        ),
        name="solve",
    )(*[pltpu.with_memory_space_constraint(operand, pltpu.HBM) for operand in operands])
    return pl.pallas_call(
        combine,
        out_shape=(out, out),
        in_specs=[vmem] * 6,
        out_specs=(hbm, hbm),
        scratch_shapes=[
            pltpu.VMEM((ROWS, NODES), F32),
            pltpu.VMEM((ROWS, NODES), F32),
            dma((2, PARTS)),
        ],
        compiler_params=pltpu.CompilerParams(vmem_limit_bytes=16 * 1024 * 1024),
        name="combine",
    )(*stored)


def solution(mesh):
    in_specs = (P(("elem", "face"), None), P(("elem", "face")), P(("elem", "face"), None))
    out_specs = (P(("elem", "face"), None), P(("elem", "face"), None))
    size = mesh.shape["elem"] * mesh.shape["face"]
    return jax.shard_map(
        functools.partial(per_device, size),
        mesh=mesh,
        in_specs=in_specs,
        out_specs=out_specs,
        check_vma=False,
    )
```

```python
import functools

import jax
import jax.numpy as jnp
import numpy as np
from jax import lax
from jax.experimental import pallas as pl
from jax.experimental.pallas import tpu as pltpu
from jax.sharding import PartitionSpec as P

EX = 8
EY = 32
ROWS = EX * EY
NODES = 512
REACT = 0.02
OMEGA = 0.6
REACH = 8
NEAR = 4
PARTS = 4
PIECES = ((0, 0), (0, 1), (0, 2), (1, 0), (1, 1), (2, 0))
MESH = pl.DeviceIdType.MESH
F32 = jnp.float32
BF16 = jnp.bfloat16


def legendre_seven(points):
    before = np.ones(8)
    current = np.array(points)
    for degree in range(1, 7):
        following = ((2 * degree + 1) * points * current - degree * before) / (degree + 1)
        before = current
        current = following
    return current


def element_tables():
    points = np.array(
        [
            -1.0,
            -0.8717401485096066,
            -0.5917001814331423,
            -0.2092992179024789,
            0.2092992179024789,
            0.5917001814331423,
            0.8717401485096066,
            1.0,
        ]
    )
    weights = np.array(
        [
            1.0 / 28.0,
            0.2107042271435061,
            0.3411226924835044,
            0.4124587946587038,
            0.4124587946587038,
            0.3411226924835044,
            0.2107042271435061,
            1.0 / 28.0,
        ]
    )
    legendre = legendre_seven(points)
    derivative = np.zeros((8, 8))
    for left_node in range(8):
        for right_node in range(8):
            if left_node != right_node:
                derivative[left_node, right_node] = legendre[left_node] / (
                    legendre[right_node] * (points[left_node] - points[right_node])
                )
    derivative[0, 0] = -14.0
    derivative[7, 7] = 14.0
    stiffness = derivative.T @ (weights[:, None] * derivative)
    mass = np.eye(8) * weights[None, :]
    full_stiff = (
        np.kron(np.kron(mass, mass), stiffness)
        + np.kron(np.kron(mass, stiffness), mass)
        + np.kron(np.kron(stiffness, mass), mass)
    )
    mass_nodes = np.kron(np.kron(weights, weights), weights)
    interp = np.stack([(1.0 - points) / 2.0, (1.0 + points) / 2.0], 1)
    prolong = np.kron(np.kron(interp, interp), interp)
    return full_stiff, mass_nodes, prolong


def pieces_of(table, count):
    parts = []
    for _ in range(count):
        part = table.astype(BF16).astype(np.float64)
        parts.append(part)
        table = table - part
    return parts


def ends(offset):
    if offset == 0:
        return list(range(8)), list(range(8))
    return ([7], [0]) if offset == 1 else ([0], [7])


def all_tables():
    full_stiff, mass_nodes, prolong = element_tables()
    face = np.concatenate([np.arange(64), np.arange(448, 512)])
    facing = np.concatenate([np.arange(448, 512), np.arange(64)])
    diag = np.diag(full_stiff).reshape(8, 8, 8)
    mass = mass_nodes.reshape(8, 8, 8)
    share = np.zeros((16, 8, 8, 8))
    fixed = np.zeros((8, 8, 8))
    for index in range(9):
        offsets = (0, index // 3 - 1, index % 3 - 1)
        mine = np.ix_(*[ends(offset)[0] for offset in offsets])
        theirs = np.ix_(*[ends(offset)[1] for offset in offsets])
        share[index][mine] += diag[theirs]
        fixed[mine] += REACT * mass[theirs]
    share, fixed = share.reshape(16, NODES), fixed.reshape(NODES)
    fixed_face = 2.0 * fixed[face]
    beside = np.zeros((24, 128))
    beside[0:18:2, :64] = share[0:9, facing[:64]]
    beside[1:18:2, 64:] = share[0:9, facing[64:]]
    beside = pieces_of(beside, 2)
    share_face = np.concatenate(
        [share[:, face], beside[0], beside[1], beside[0], np.zeros((8, 128))], 0
    )

    steep = full_stiff @ prolong
    heavy = REACT * mass_nodes[:, None] * prolong

    def stacked(table):
        parts = pieces_of(table, 3)
        return np.concatenate([parts[right] for _, right in PIECES], 0)

    spread = stacked(np.concatenate([prolong.T, steep.T], 1))
    facing_tables = np.concatenate([steep[facing].T, heavy[facing].T], 1)
    lower = facing_tables.copy()
    lower[:, 64:128] = 0.0
    lower[:, 192:256] = 0.0
    spread_face = np.concatenate([stacked(lower), stacked(facing_tables - lower)], 0)

    gather = pieces_of(np.concatenate([steep.T, heavy.T], 0), 2)
    gather = np.concatenate(gather, 0)
    first = np.concatenate(pieces_of(prolong.T, 2), 0)
    return {
        "stiff": full_stiff,
        "spread": spread,
        "spread_face": spread_face,
        "gather": np.concatenate([gather, first], 0),
        "share": share,
        "share_face": share_face,
        "rows": np.concatenate(
            [
                np.stack([fixed, REACT * mass_nodes]),
                np.pad(np.stack([fixed_face, REACT * mass_nodes[face]]), ((0, 0), (0, 384))),
            ],
            0,
        ),
    }


def split(value, pieces):
    parts = []
    for _ in range(pieces):
        part = value.astype(BF16)
        parts.append(part)
        value = value - part.astype(F32)
    return parts


def dot(left, right, dims=((1,), (0,))):
    return lax.dot_general(
        left, right, (dims, ((), ())), precision=lax.Precision.HIGHEST, preferred_element_type=F32
    )


def dot16(left, right, dims=((1,), (0,))):
    return lax.dot_general(left, right, (dims, ((), ())), preferred_element_type=F32)


def lanes(shape):
    return lax.broadcasted_iota(jnp.int32, shape, len(shape) - 1)


def shifted(plane, dy, dx):
    size = plane.shape[1]
    if dy == 0 and dx == 0:
        return plane
    inside = pltpu.roll(plane, -(EX * dy + dx) % size, 1)
    if dx == 0:
        return inside
    around = pltpu.roll(plane, -(EX * dy + dx - EX * dx) % size, 1)
    return jnp.where(lanes(plane.shape) % EX == (EX - 1 if dx == 1 else 0), around, inside)


def added(terms):
    terms = list(terms)
    while len(terms) > 1:
        terms = [sum(terms[at : at + 2]) for at in range(0, len(terms), 2)]
    return terms[0]


def down(plane):
    return pltpu.roll(plane, plane.shape[0] - 1, 0)


def up(plane):
    return pltpu.roll(plane, 1, 0)


def shared_xy(tile):
    cube = tile.reshape(EY, EX, 128)
    lane = lanes(cube.shape)
    nx, ny = lane % 8, lane // 8 % 8
    after = pltpu.roll(pltpu.roll(cube, EX - 1, 1), 7, 2)
    before = pltpu.roll(pltpu.roll(cube, 1, 1), 128 - 7, 2)
    cube = cube + jnp.where(nx == 7, after, jnp.where(nx == 0, before, 0.0))
    after = pltpu.roll(jnp.concatenate([cube[1:], cube[:1]], 0), 56, 2)
    before = pltpu.roll(jnp.concatenate([cube[-1:], cube[:-1]], 0), 128 - 56, 2)
    cube = cube + jnp.where(ny == 7, after, jnp.where(ny == 0, before, 0.0))
    return cube.reshape(ROWS, 128)


def four(layer):
    return [shifted(layer, 0, 0), shifted(layer, 0, -1), shifted(layer, -1, 0), shifted(layer, -1, -1)]


def nine(layer):
    return [shifted(layer, dy, dx) for dy in (-1, 0, 1) for dx in (-1, 0, 1)]


def coarse_stencil(layer4, planes):
    found = {}
    for dy in (-1, 0, 1):
        for dx in (-1, 0, 1):
            rows = (0, 1) if dy == 0 else ((0,) if dy == 1 else (1,))
            cols = (0, 1) if dx == 0 else ((0,) if dx == 1 else (1,))
            differ = abs(dy) + abs(dx) + (1 - planes)
            count = len(rows) * len(cols) * (1 + planes)
            weight = REACT * count * 2.0 ** (3 - differ) / 27.0
            if differ >= 2:
                total = sum(layer4[2 * a + b] for a in rows for b in cols)
                found[dy, dx] = (-1.0 / 6.0) * total + weight
            elif differ == 1:
                found[dy, dx] = weight
    return found


def swept(vert, level, from_above, from_below):
    spread = {key: shifted(vert, *key) for key in from_above}
    above = down(added(from_above[key] * spread[key] for key in from_above))
    below = up(added(from_below[key] * spread[key] for key in from_below))
    here = added([(1.0 - OMEGA) * vert] + [level[key] * spread[key] for key in level])
    return here + (above + below)


NAMES = (
    "stiff",
    "spread",
    "spread_face",
    "gather",
    "share",
    "share_face",
    "rows",
)
FIELDS = ("load", "r0", "x0", "z0", "q", "qloc", "x1", "y", "w", "inverse", "stiffened")


def kernel(size, *refs):
    refs = list(refs)

    def take(count):
        taken = refs[:count]
        del refs[:count]
        return taken

    sources = take(3 + len(NAMES))
    sent_z0, sent_y, sent_r0, sent_q, sent_w, steps_ref = take(6)
    inputs = take(3 + len(NAMES))
    forcing_ref, kappa_ref, order_ref = inputs[:3]
    table = dict(zip(NAMES, inputs[3:]))
    field = dict(zip(FIELDS, take(len(FIELDS))))
    coeff_ref, own_columns_ref, own_face_ref, inner_rows_ref, stiff_ref, stiff_face_ref = take(6)
    edge_out, edge_in, layer, halo, rest, sums_ref = take(6)
    in_sem, layer_send, layer_recv, halo_send, halo_recv = take(5)
    rest_send, rest_recv, edge_send, edge_recv, sum_send, sum_recv, known_sem = take(7)

    core = lax.axis_index("face")
    me = lax.axis_index("elem") * 2 + core

    def ring(by):
        device = lax.rem(me + by + size, size)
        return lax.div(device, 2), lax.rem(device, 2)

    barrier = pltpu.get_barrier_semaphore()
    greeted = [by for by in range(-REACH, REACH + 1) if by != 0]
    for by in greeted:
        pl.semaphore_signal(barrier, inc=1, device_id=ring(by), device_id_type=MESH)

    loads = {
        index: pltpu.make_async_copy(sources[index], inputs[index], in_sem.at[index])
        for index in range(1, len(inputs))
    }
    forcing_loads = [
        pltpu.make_async_copy(
            sources[0].at[:, pl.ds(at, width)],
            forcing_ref.at[:, pl.ds(at, width)],
            in_sem.at[len(inputs) + index],
        )
        for index, (at, width) in enumerate(((0, 128), (384, 128), (128, 256)))
    ]
    loads[2].start()
    forcing_loads[0].start()
    forcing_loads[1].start()
    loads[1].start()
    forcing_loads[2].start()
    for index in range(len(inputs) - 1, 2, -1):
        loads[index].start()

    stages = []
    while REACH << len(stages) < size // 2:
        stages.append(REACH << len(stages))

    def tell(stage):
        if stage < len(stages):
            for way, by in enumerate((stages[stage], -stages[stage])):
                pl.semaphore_signal(
                    known_sem.at[stage, way], inc=1, device_id=ring(by), device_id_type=MESH
                )

    def hear(stage):
        if stage < len(stages):
            for way in range(2):
                pl.semaphore_wait(known_sem.at[stage, way], 1)

    def remote(source, target, send, recv, device):
        return pltpu.make_async_remote_copy(
            src_ref=source,
            dst_ref=target,
            send_sem=send,
            recv_sem=recv,
            device_id=device,
            device_id_type=MESH,
        )

    def slot(place, reach):
        return 2 * reach if place == reach else place - (place > reach)

    def to_ring(buffer, send, recv, reach):
        for by in sorted(range(-reach, reach + 1), key=abs):
            if by != 0:
                remote(
                    buffer.at[2 * reach], buffer.at[slot(reach - by, reach)], send, recv, ring(by)
                ).start()
        others = buffer.at[pl.ds(0, 2 * reach)]
        return remote(others, others, send, recv, ring(1))

    half = lanes((ROWS, 128)) < 64

    def tile(ref, index):
        return ref[:, 128 * index : 128 * index + 128]

    def put(ref, index, value):
        ref[:, 128 * index : 128 * index + 128] = value

    def face_of(ref):
        return jnp.where(half, tile(ref, 0), tile(ref, 3))

    def put_face(ref, value):
        put(ref, 0, jnp.where(half, value, tile(ref, 0)))
        put(ref, 3, jnp.where(half, tile(ref, 3), value))

    def send_faces(face, turn):
        top, bottom, part = face[0:128], face[128:256], half[0:128]
        edge_out[turn, 0] = jnp.where(part, pltpu.roll(top, 64, 1), bottom)
        edge_out[turn, 1] = jnp.where(part, top, pltpu.roll(bottom, 64, 1))
        copies = [
            remote(
                edge_out.at[turn, way],
                edge_in.at[turn, way],
                edge_send.at[turn],
                edge_recv.at[turn],
                ring(1 - 2 * way),
            )
            for way in (1 - core, core)
        ]
        for copy in copies:
            copy.start()
        return remote(
            edge_out.at[turn], edge_in.at[turn], edge_send.at[turn], edge_recv.at[turn], ring(1)
        )

    def faces_arrived(copies, turn):
        copies.wait_recv()
        below, above, part = edge_in[turn, 0], edge_in[turn, 1], half[0:128]
        top = jnp.where(part, below, pltpu.roll(above, 64, 1))
        bottom = jnp.where(part, pltpu.roll(below, 64, 1), above)
        return jnp.concatenate([top, bottom], 0)

    def vertex_sums(each):
        corner = lax.broadcasted_iota(jnp.int32, each.shape, 0)
        even = jnp.where(corner // 2 % 2 == 1, shifted(each, -1, 0), each)
        odd = jnp.where(corner // 2 % 2 == 1, shifted(each, -1, -1), shifted(each, 0, -1))
        each = jnp.where(corner % 2 == 1, odd, even)
        low = jnp.sum(each[0:4], axis=0, keepdims=True)
        high = jnp.sum(each[4:8], axis=0, keepdims=True)
        return low, high

    def gathered(matrix, parts):
        whole = dot16(matrix, parts[0], ((1,), (1,)))
        return whole[0:16] + whole[16:32] + dot16(matrix[0:16], parts[1], ((1,), (1,)))

    def face_lanes(value):
        return jnp.concatenate([value[:, 0:64], value[:, 448:512]], 1)

    def columns(planes):
        return jnp.concatenate(planes, 0).T

    def corner_pieces(corners):
        parts = [part.astype(F32) for part in split(corners, 3)]
        return [parts[left] for left, _ in PIECES]

    row = lax.broadcasted_iota(jnp.int32, (ROWS, ROWS), 0)
    loads[2].wait()
    pick = jnp.where(row == order_ref[...], 1.0, 0.0)
    pick16 = pick.astype(BF16)
    loads[1].wait()
    kappa_rows = jnp.broadcast_to(kappa_ref[...], (16, ROWS))
    kappa = sum(dot16(part, pick16, ((1,), (1,))) for part in split(kappa_rows, 3))[0:8]
    layer[2] = kappa[0:1]
    halo[2 * REACH, 2:3] = kappa[0:1]
    load_ref, r0_ref = field["load"], field["r0"]

    def permuted(matrix, value):
        return sum(dot16(matrix, part) for part in split(value, 3))

    for copy in forcing_loads[:2]:
        copy.wait()
    first_face = shared_xy(permuted(pick16, face_of(forcing_ref)))
    own9 = nine(kappa)
    own_rows = [plane[0:1] for plane in own9] + [jnp.zeros((7, ROWS), F32)]
    own_columns = columns(own_rows)
    coeff_ref[...] = jnp.broadcast_to(own_columns[:, 4:5], (ROWS, 128))
    own_columns_ref[...] = own_columns

    def interior(value, x_ref):
        inverse = field["inverse"]
        zero = jnp.zeros((ROWS, 128), F32)
        put(x_ref, 0, jnp.where(half, zero, tile(inverse, 0) * tile(value, 0)))
        put(x_ref, 1, tile(inverse, 1) * tile(value, 1))
        put(x_ref, 2, tile(inverse, 2) * tile(value, 2))
        put(x_ref, 3, jnp.where(half, tile(inverse, 3) * tile(value, 3), zero))
        parts = split(x_ref[...], 2)
        high, low = stiff_ref[0:NODES], stiff_ref[NODES:]
        field["stiffened"][...] = (
            dot16(parts[0], high) + dot16(parts[1], high) + dot16(parts[0], low)
        )
        return gathered(table["gather"][0:32].astype(BF16), parts)

    def prepare_halo():
        forcing_loads[2].wait()
        load_ref[...] = permuted(pick16, forcing_ref[...])
        for index in range(3, len(inputs)):
            loads[index].wait()
        parts = split(load_ref[...], 2)
        first = table["gather"][32:48].astype(BF16)
        each = dot16(first, parts[0], ((1,), (1,)))
        each = each[0:8] + each[8:16] + dot16(first, parts[1], ((1,), (1,)))[0:8]
        low, high = vertex_sums(each)
        halo[2 * REACH, 0:1] = low
        halo[2 * REACH, 1:2] = high

    def prepare_interior():
        own_columns = own_columns_ref[...]
        fixed = table["rows"][0:1]
        field["inverse"][...] = 1.0 / (dot(own_columns, table["share"][...]) + fixed)
        own_face_ref[...] = dot(own_columns, table["share_face"][0:16]) + table["rows"][2:3, 0:128]
        stiff = table["stiff"][...]
        upper_piece = stiff.astype(BF16)
        stiff_ref[0:NODES] = upper_piece
        stiff_ref[NODES:] = (stiff - upper_piece.astype(F32)).astype(BF16)
        for index in range(4):
            put(r0_ref, index, shared_xy(tile(load_ref, index)))
        inner_rows_ref[...] = interior(r0_ref, field["x0"])
        for at, piece in ((0, 0), (128, 0), (256, NODES)):
            stiff_face_ref[at : at + 64] = stiff_ref[piece : piece + 64]
            stiff_face_ref[at + 64 : at + 128] = stiff_ref[piece + 448 : piece + 512]

    ahead = me < REACH

    @pl.when(ahead)
    def _():
        prepare_halo()
        prepare_interior()

    pl.semaphore_wait(barrier, len(greeted))
    layer_copies = to_ring(layer, layer_send, layer_recv, 1)
    edges = [send_faces(first_face, 0)]
    tell(0)

    @pl.when(jnp.logical_not(ahead))
    def _():
        prepare_halo()

    halo_copies = to_ring(halo, halo_send, halo_recv, REACH)

    @pl.when(jnp.logical_not(ahead))
    def _():
        prepare_interior()

    inner_rows = inner_rows_ref[...]
    mass, mass_face = table["rows"][1:2], table["rows"][3:4, 0:128]
    own_face = own_face_ref[...]
    share_two = table["share_face"][16:96].astype(BF16)
    gather = table["gather"][0:32].astype(BF16)
    gather_face = face_lanes(gather)
    stiff_face_face = face_lanes(stiff_face_ref[...])

    hear(0)
    tell(1)
    layer_copies.wait_recv()
    two = jnp.concatenate([layer[0], layer[1], jnp.zeros((6, ROWS), F32)], 0)
    two9 = jnp.concatenate([plane[0:2] for plane in nine(two)] + [two[2:8]], 0)
    two_pieces = [part.astype(F32) for part in split(two9, 2)]
    two_columns = columns([two_pieces[0], two_pieces[0], two_pieces[1], two])
    inverse_face = 1.0 / (own_face + dot16(two_columns.astype(BF16), share_two))
    coeff_beside = jnp.where(half, two_columns[:, 72:73], two_columns[:, 73:74])
    coeff = coeff_ref[...]
    face = first_face + faces_arrived(edges[0], 0)
    put_face(r0_ref, face)

    def outer(face, x_ref, rows):
        x_face = inverse_face * face
        put_face(x_ref, x_face)
        parts = split(x_face, 2)
        rows = rows + gathered(gather_face, parts)
        stacked = jnp.concatenate([parts[0], parts[1], parts[0]], 1)
        return x_face, stacked, rows, dot16(stacked, stiff_face_face)

    x_face, stacked, rows0, steep_face = outer(face, field["x0"], inner_rows)
    rough = coeff * (face_of(field["stiffened"]) + steep_face) + mass_face * x_face
    low, high = vertex_sums(kappa * rows0[0:8] + rows0[8:16])
    rest[2 * NEAR, 0:1] = low
    rest[2 * NEAR, 1:2] = high
    rest_copies = to_ring(rest, rest_send, rest_recv, NEAR)
    edges.append(send_faces(shared_xy(rough), 1))

    hear(1)
    tell(2)
    field["stiffened"][...] += dot16(stacked, stiff_face_ref[...])
    spread_table = table["spread"][...].astype(BF16)
    spread_face_table = table["spread_face"][...].astype(BF16)
    spread_own_face = jnp.concatenate(
        [face_lanes(spread_table[:, 0:NODES]), face_lanes(spread_table[:, NODES:])], 1
    )
    halo_copies.wait_recv()
    planes = list(range(-3, REACH + 1)) + list(range(1 - REACH, -3))

    def halo_rows(shift, which):
        places = [slot(REACH + p + shift, REACH) for p in planes]
        return jnp.concatenate([halo[place, which : which + 1] for place in places], 0)

    under4, over4 = four(halo_rows(-1, 2)), four(halo_rows(0, 2))
    both4 = [a + b for a, b in zip(under4, over4)]
    diag = (2.0 / 3.0) * (both4[0] + both4[1] + both4[2] + both4[3]) + REACT * 64.0 / 27.0
    damp = -OMEGA / diag
    damp_down, damp_up = up(damp), down(damp)
    level = {key: damp * value for key, value in coarse_stencil(both4, 1).items()}
    from_above = {key: damp_down * value for key, value in coarse_stencil(under4, 0).items()}
    from_below = {key: damp_up * value for key, value in coarse_stencil(over4, 0).items()}
    start = -damp * (halo_rows(0, 0) + halo_rows(-1, 1))
    vert = start
    for _ in range(3):
        vert = start + swept(vert, level, from_above, from_below)
    remainder = (vert - swept(vert, level, from_above, from_below))[0:8]

    def corners_of(vert, lower):
        found = [shifted(vert, *key) for key in ((0, 0), (0, 1), (1, 0), (1, 1))]
        return [
            jnp.concatenate(
                [c[k : k + 1] for c in found] + [c[k + 1 : k + 2] for c in found], 0
            )
            for k in lower
        ]

    own, under, over = corners_of(vert[0:8], (3, 2, 4))
    spread = dot16(columns(corner_pieces(own)).astype(BF16), spread_table)
    beside = dot16(
        columns(corner_pieces(under) + corner_pieces(over)).astype(BF16),
        spread_face_table,
    )
    beside = shared_xy(coeff_beside * beside[:, 0:128] + beside[:, 128:256])

    def total(value):
        quarter = ROWS // 4
        value = added(value[at * quarter : at * quarter + quarter] for at in range(4))
        return jnp.sum(
            jnp.sum(value.reshape(quarter // 8, 8, 128), axis=0), axis=(0, 1), keepdims=True
        )

    def applied(x_ref, spread, z_ref, image_ref):
        for index in range(4):
            at = 128 * index
            z = tile(x_ref, index) + spread[:, at : at + 128]
            put(z_ref, index, z)
            put(
                image_ref,
                index,
                coeff * (tile(field["stiffened"], index) + spread[:, 512 + at : 640 + at])
                + mass[:, at : at + 128] * z,
            )

    def inner(left, right):
        return total(added(tile(left, index) * tile(right, index) for index in range(4)))

    applied(field["x0"], spread, field["z0"], field["qloc"])
    rz = inner(load_ref, field["z0"])
    zq = inner(field["qloc"], field["z0"])
    for index in range(4):
        put(field["q"], index, shared_xy(tile(field["qloc"], index)))
    partial_face = face_of(field["q"]) + beside
    inner_rows = interior(field["q"], field["x1"])

    face_image = face_of(field["qloc"])
    steep_inner = face_of(field["stiffened"])
    yw = total(
        sum(
            tile(field["x1"], index)
            * (
                coeff * tile(field["stiffened"], index)
                + mass[:, 128 * index : 128 * index + 128] * tile(field["x1"], index)
            )
            for index in range(4)
        )
    )
    zero = jnp.zeros((ROWS, 128), F32)
    qy = inner(field["qloc"], field["x1"])
    back16 = pick.T.astype(BF16)

    def stored(value):
        return sum(dot16(back16, part) for part in split(value, 2))

    sent_z0[...] = stored(field["z0"][...])
    sent_r0[...] = stored(r0_ref[...])

    rest_copies.wait_recv()
    face = partial_face + faces_arrived(edges[1], 1)
    x_face, stacked, rows1, steep_face = outer(face, field["x1"], inner_rows)
    target = jnp.concatenate(
        [rest[slot(NEAR + p, NEAR), 0:1] for p in range(-3, 5)], 0
    ) + jnp.concatenate([rest[slot(NEAR + p - 1, NEAR), 1:2] for p in range(-3, 5)], 0)

    def top(parts):
        return {key: value[0:8] for key, value in parts.items()}

    level, from_above, from_below = top(level), top(from_above), top(from_below)
    start = remainder - damp[0:8] * target
    vert = start
    for _ in range(3):
        vert = start + swept(vert, level, from_above, from_below)
    (own,) = corners_of(vert, (3,))

    own_pieces = columns(corner_pieces(own)).astype(BF16)
    spread = dot16(own_pieces, spread_own_face)
    y_face = x_face + spread[:, 0:128]
    w_face = coeff * (steep_inner + steep_face + spread[:, 128:256]) + mass_face * y_face
    late_face = shared_xy(w_face)

    def flipped(value, bit):
        corner = lax.broadcasted_iota(jnp.int32, value.shape, 0)
        return jnp.where(
            corner // bit % 2 == 0, pltpu.roll(value, 8 - bit, 0), pltpu.roll(value, bit, 0)
        )

    edge_sum = flipped(own, 1) + flipped(own, 2) + flipped(own, 4)
    all_sum = jnp.sum(own, axis=0, keepdims=True)
    weighed = own
    for bit in (1, 2, 4):
        weighed = (2.0 * weighed + flipped(weighed, bit)) * (1.0 / 3.0)
    steep = (5.0 / 6.0) * own + (1.0 / 6.0) * (edge_sum - all_sum)
    energy = own * (
        kappa * (steep + 2.0 * rows1[0:8]) + (REACT * weighed + 2.0 * rows1[8:16])
    )
    qy = qy + total(face_image * x_face) + jnp.sum((start * vert / -damp[0:8])[3:4], keepdims=True)
    yw = yw + jnp.sum(energy, keepdims=True)
    yw = yw + total(
        x_face * (coeff * (2.0 * steep_inner + steep_face) + mass_face * x_face)
    )

    hear(2)
    lane = lanes((1, 128))
    mine = jnp.zeros((1, 128), F32)
    for index, value in enumerate((rz, zq, qy, yw)):
        mine = jnp.where(lane == index, value, mine)
    sums_ref[0] = mine

    def send_sums(turn, carry):
        by = lax.rem(turn + jnp.where(turn >= me, 1, 0) - me + size, size)
        remote(sums_ref.at[0], sums_ref.at[by], sum_send, sum_recv, ring(by)).start()
        return carry

    lax.fori_loop(0, REACH, send_sums, 0)
    edges.append(send_faces(late_face, 2))
    lax.fori_loop(REACH, size - 1, send_sums, 0)

    field["stiffened"][...] += dot16(stacked, stiff_face_ref[...])
    applied(field["x1"], dot16(own_pieces, spread_table), field["y"], field["w"])
    for index in range(4):
        put(field["w"], index, shared_xy(tile(field["w"], index)))
    put_face(field["q"], face)
    sent_y[...] = stored(field["y"][...])
    sent_q[...] = stored(field["q"][...])
    sent_w[...] = stored(field["w"][...])
    others = sums_ref.at[pl.ds(1, size - 1)]
    all_sums = remote(others, others, sum_send, sum_recv, ring(1))
    all_sums.wait_send()
    for copies in [layer_copies, halo_copies, rest_copies] + edges:
        copies.wait_send()
    face = stored(faces_arrived(edges[2], 2))
    sent_w[:, 0:128] += jnp.where(half, face, zero)
    sent_w[:, 384:512] += jnp.where(half, zero, face)
    all_sums.wait_recv()
    eighth = size // 8
    sums = added(sums_ref[at * eighth : at * eighth + eighth] for at in range(8))
    sums = jnp.sum(sums, axis=0)
    rz, zq, qy, yw = (sums[:, index : index + 1] for index in range(4))
    first = rz / zq
    gamma = first * first * qy - rz
    grown = 1.0 + gamma / rz
    second = gamma / (grown * grown * zq - 2.0 * first * grown * qy + first * first * yw)
    straight, bent = first + second * grown, first * second
    steps_ref[0:1] = jnp.broadcast_to(straight, (1, 128))
    steps_ref[1:2] = jnp.broadcast_to(bent, (1, 128))


def combine(z0, y, r0, q, w, steps, solution_ref, residual_ref, solution_part, residual_part, sem):
    straight, bent = steps[0:1, 0:1], steps[1:2, 0:1]
    copies = []
    rows = ROWS // PARTS
    for part in range(PARTS):
        at = pl.ds(part * rows, rows)
        solution_part[at] = straight * z0[at] - bent * y[at]
        copies.append(
            pltpu.make_async_copy(solution_part.at[at], solution_ref.at[at], sem.at[0, part])
        )
        copies[-1].start()
        residual_part[at] = r0[at] - straight * q[at] + bent * w[at]
        copies.append(
            pltpu.make_async_copy(residual_part.at[at], residual_ref.at[at], sem.at[1, part])
        )
        copies[-1].start()
    for copy in copies:
        copy.wait()


def per_device(size, forcing, kappa, elem_order):
    tables = all_tables()
    operands = [forcing, kappa.reshape(1, ROWS), elem_order]
    operands += [jnp.asarray(tables[name], F32) for name in NAMES]
    out = jax.ShapeDtypeStruct((ROWS, NODES), F32)
    steps = jax.ShapeDtypeStruct((8, 128), F32)
    count, close = 2 * REACH + 1, 2 * NEAR + 1
    dma = pltpu.SemaphoreType.DMA
    vmem = pl.BlockSpec(memory_space=pltpu.VMEM)
    hbm = pl.BlockSpec(memory_space=pltpu.HBM)
    stored = pl.pallas_call(
        functools.partial(kernel, size),
        out_shape=(out,) * 5 + (steps,),
        in_specs=[hbm] * len(operands),
        out_specs=(vmem,) * 6,
        scratch_shapes=[pltpu.VMEM(operand.shape, operand.dtype) for operand in operands]
        + [pltpu.VMEM((ROWS, NODES), F32)] * len(FIELDS)
        + [
            pltpu.VMEM((ROWS, 128), F32),
            pltpu.VMEM((ROWS, 16), F32),
            pltpu.VMEM((ROWS, 128), F32),
            pltpu.VMEM((16, ROWS), F32),
            pltpu.VMEM((2 * NODES, NODES), BF16),
            pltpu.VMEM((384, NODES), BF16),
            pltpu.VMEM((3, 2, 128, 128), F32),
            pltpu.VMEM((3, 2, 128, 128), F32),
            pltpu.VMEM((3, 1, ROWS), F32),
            pltpu.VMEM((count, 3, ROWS), F32),
            pltpu.VMEM((close, 2, ROWS), F32),
            pltpu.VMEM((size, 1, 128), F32),
            dma((len(operands) + 3,)),
            dma,
            dma,
            dma,
            dma,
            dma,
            dma,
            dma((3,)),
            dma((3,)),
            dma,
            dma,
            pltpu.SemaphoreType.REGULAR((3, 2)),
        ],
        compiler_params=pltpu.CompilerParams(
            collective_id=0, has_side_effects=True, vmem_limit_bytes=32 * 1024 * 1024
        ),
        name="solve",
    )(*[pltpu.with_memory_space_constraint(operand, pltpu.HBM) for operand in operands])
    return pl.pallas_call(
        combine,
        out_shape=(out, out),
        in_specs=[vmem] * 6,
        out_specs=(hbm, hbm),
        scratch_shapes=[
            pltpu.VMEM((ROWS, NODES), F32),
            pltpu.VMEM((ROWS, NODES), F32),
            dma((2, PARTS)),
        ],
        compiler_params=pltpu.CompilerParams(vmem_limit_bytes=16 * 1024 * 1024),
        name="combine",
    )(*stored)


def solution(mesh):
    in_specs = (P(("elem", "face"), None), P(("elem", "face")), P(("elem", "face"), None))
    out_specs = (P(("elem", "face"), None), P(("elem", "face"), None))
    size = mesh.shape["elem"] * mesh.shape["face"]
    return jax.shard_map(
        functools.partial(per_device, size),
        mesh=mesh,
        in_specs=in_specs,
        out_specs=out_specs,
        check_vma=False,
    )
```

```python
import functools

import jax
import jax.numpy as jnp
import numpy as np
from jax import lax
from jax.experimental import pallas as pl
from jax.experimental.pallas import tpu as pltpu
from jax.sharding import PartitionSpec as P

EX = 8
EY = 32
ROWS = EX * EY
NODES = 512
REACT = 0.02
OMEGA = 0.6
REACH = 8
NEAR = 4
PARTS = 4
PIECES = ((0, 0), (0, 1), (0, 2), (1, 0), (1, 1), (2, 0))
MESH = pl.DeviceIdType.MESH
F32 = jnp.float32
BF16 = jnp.bfloat16


def legendre_seven(points):
    before = np.ones(8)
    current = np.array(points)
    for degree in range(1, 7):
        following = ((2 * degree + 1) * points * current - degree * before) / (degree + 1)
        before = current
        current = following
    return current


def element_tables():
    points = np.array(
        [
            -1.0,
            -0.8717401485096066,
            -0.5917001814331423,
            -0.2092992179024789,
            0.2092992179024789,
            0.5917001814331423,
            0.8717401485096066,
            1.0,
        ]
    )
    weights = np.array(
        [
            1.0 / 28.0,
            0.2107042271435061,
            0.3411226924835044,
            0.4124587946587038,
            0.4124587946587038,
            0.3411226924835044,
            0.2107042271435061,
            1.0 / 28.0,
        ]
    )
    legendre = legendre_seven(points)
    derivative = np.zeros((8, 8))
    for left_node in range(8):
        for right_node in range(8):
            if left_node != right_node:
                derivative[left_node, right_node] = legendre[left_node] / (
                    legendre[right_node] * (points[left_node] - points[right_node])
                )
    derivative[0, 0] = -14.0
    derivative[7, 7] = 14.0
    stiffness = derivative.T @ (weights[:, None] * derivative)
    mass = np.eye(8) * weights[None, :]
    full_stiff = (
        np.kron(np.kron(mass, mass), stiffness)
        + np.kron(np.kron(mass, stiffness), mass)
        + np.kron(np.kron(stiffness, mass), mass)
    )
    mass_nodes = np.kron(np.kron(weights, weights), weights)
    interp = np.stack([(1.0 - points) / 2.0, (1.0 + points) / 2.0], 1)
    prolong = np.kron(np.kron(interp, interp), interp)
    return full_stiff, mass_nodes, prolong


def pieces_of(table, count):
    parts = []
    for _ in range(count):
        part = table.astype(BF16).astype(np.float64)
        parts.append(part)
        table = table - part
    return parts


def ends(offset):
    if offset == 0:
        return list(range(8)), list(range(8))
    return ([7], [0]) if offset == 1 else ([0], [7])


def all_tables():
    full_stiff, mass_nodes, prolong = element_tables()
    face = np.concatenate([np.arange(64), np.arange(448, 512)])
    facing = np.concatenate([np.arange(448, 512), np.arange(64)])
    diag = np.diag(full_stiff).reshape(8, 8, 8)
    mass = mass_nodes.reshape(8, 8, 8)
    share = np.zeros((16, 8, 8, 8))
    fixed = np.zeros((8, 8, 8))
    for index in range(9):
        offsets = (0, index // 3 - 1, index % 3 - 1)
        mine = np.ix_(*[ends(offset)[0] for offset in offsets])
        theirs = np.ix_(*[ends(offset)[1] for offset in offsets])
        share[index][mine] += diag[theirs]
        fixed[mine] += REACT * mass[theirs]
    share, fixed = share.reshape(16, NODES), fixed.reshape(NODES)
    fixed_face = 2.0 * fixed[face]
    beside = np.zeros((24, 128))
    beside[0:18:2, :64] = share[0:9, facing[:64]]
    beside[1:18:2, 64:] = share[0:9, facing[64:]]
    beside = pieces_of(beside, 2)
    share_face = np.concatenate(
        [share[:, face], beside[0], beside[1], beside[0], np.zeros((8, 128))], 0
    )

    steep = full_stiff @ prolong
    heavy = REACT * mass_nodes[:, None] * prolong

    def stacked(table):
        parts = pieces_of(table, 3)
        return np.concatenate([parts[right] for _, right in PIECES], 0)

    spread = stacked(np.concatenate([prolong.T, steep.T], 1))
    facing_tables = np.concatenate([steep[facing].T, heavy[facing].T], 1)
    lower = facing_tables.copy()
    lower[:, 64:128] = 0.0
    lower[:, 192:256] = 0.0
    spread_face = np.concatenate([stacked(lower), stacked(facing_tables - lower)], 0)

    gather = pieces_of(np.concatenate([steep.T, heavy.T], 0), 2)
    gather = np.concatenate(gather, 0)
    first = np.concatenate(pieces_of(prolong.T, 2), 0)
    return {
        "stiff": full_stiff,
        "spread": spread,
        "spread_face": spread_face,
        "gather": np.concatenate([gather, first], 0),
        "share": share,
        "share_face": share_face,
        "rows": np.concatenate(
            [
                np.stack([fixed, REACT * mass_nodes]),
                np.pad(np.stack([fixed_face, REACT * mass_nodes[face]]), ((0, 0), (0, 384))),
            ],
            0,
        ),
    }


def split(value, pieces):
    parts = []
    for _ in range(pieces):
        part = value.astype(BF16)
        parts.append(part)
        value = value - part.astype(F32)
    return parts


def dot(left, right, dims=((1,), (0,))):
    return lax.dot_general(
        left, right, (dims, ((), ())), precision=lax.Precision.HIGHEST, preferred_element_type=F32
    )


def dot16(left, right, dims=((1,), (0,))):
    return lax.dot_general(left, right, (dims, ((), ())), preferred_element_type=F32)


def lanes(shape):
    return lax.broadcasted_iota(jnp.int32, shape, len(shape) - 1)


def shifted(plane, dy, dx):
    size = plane.shape[1]
    if dy == 0 and dx == 0:
        return plane
    inside = pltpu.roll(plane, -(EX * dy + dx) % size, 1)
    if dx == 0:
        return inside
    around = pltpu.roll(plane, -(EX * dy + dx - EX * dx) % size, 1)
    return jnp.where(lanes(plane.shape) % EX == (EX - 1 if dx == 1 else 0), around, inside)


def added(terms):
    terms = list(terms)
    while len(terms) > 1:
        terms = [sum(terms[at : at + 2]) for at in range(0, len(terms), 2)]
    return terms[0]


def down(plane):
    return pltpu.roll(plane, plane.shape[0] - 1, 0)


def up(plane):
    return pltpu.roll(plane, 1, 0)


def shared_xy(tile):
    cube = tile.reshape(EY, EX, 128)
    lane = lanes(cube.shape)
    nx, ny = lane % 8, lane // 8 % 8
    after = pltpu.roll(pltpu.roll(cube, EX - 1, 1), 7, 2)
    before = pltpu.roll(pltpu.roll(cube, 1, 1), 128 - 7, 2)
    cube = cube + jnp.where(nx == 7, after, jnp.where(nx == 0, before, 0.0))
    after = pltpu.roll(jnp.concatenate([cube[1:], cube[:1]], 0), 56, 2)
    before = pltpu.roll(jnp.concatenate([cube[-1:], cube[:-1]], 0), 128 - 56, 2)
    cube = cube + jnp.where(ny == 7, after, jnp.where(ny == 0, before, 0.0))
    return cube.reshape(ROWS, 128)


def four(layer):
    return [shifted(layer, 0, 0), shifted(layer, 0, -1), shifted(layer, -1, 0), shifted(layer, -1, -1)]


def nine(layer):
    return [shifted(layer, dy, dx) for dy in (-1, 0, 1) for dx in (-1, 0, 1)]


def coarse_stencil(layer4, planes):
    found = {}
    for dy in (-1, 0, 1):
        for dx in (-1, 0, 1):
            rows = (0, 1) if dy == 0 else ((0,) if dy == 1 else (1,))
            cols = (0, 1) if dx == 0 else ((0,) if dx == 1 else (1,))
            differ = abs(dy) + abs(dx) + (1 - planes)
            count = len(rows) * len(cols) * (1 + planes)
            weight = REACT * count * 2.0 ** (3 - differ) / 27.0
            if differ >= 2:
                total = sum(layer4[2 * a + b] for a in rows for b in cols)
                found[dy, dx] = (-1.0 / 6.0) * total + weight
            elif differ == 1:
                found[dy, dx] = weight
    return found


def swept(vert, level, from_above, from_below):
    spread = {key: shifted(vert, *key) for key in from_above}
    above = down(added(from_above[key] * spread[key] for key in from_above))
    below = up(added(from_below[key] * spread[key] for key in from_below))
    here = added([(1.0 - OMEGA) * vert] + [level[key] * spread[key] for key in level])
    return here + (above + below)


NAMES = (
    "stiff",
    "spread",
    "spread_face",
    "gather",
    "share",
    "share_face",
    "rows",
)
FIELDS = ("load", "r0", "x0", "z0", "q", "qloc", "x1", "y", "w", "inverse", "stiffened")


def kernel(size, *refs):
    refs = list(refs)

    def take(count):
        taken = refs[:count]
        del refs[:count]
        return taken

    sources = take(3 + len(NAMES))
    sent_z0, sent_y, sent_r0, sent_q, sent_w, steps_ref = take(6)
    inputs = take(3 + len(NAMES))
    forcing_ref, kappa_ref, order_ref = inputs[:3]
    table = dict(zip(NAMES, inputs[3:]))
    field = dict(zip(FIELDS, take(len(FIELDS))))
    coeff_ref, own_columns_ref, own_face_ref, inner_rows_ref, stiff_ref, stiff_face_ref = take(6)
    edge_out, edge_in, layer, halo, rest, sums_ref = take(6)
    in_sem, layer_send, layer_recv, halo_send, halo_recv = take(5)
    rest_send, rest_recv, edge_send, edge_recv, sum_send, sum_recv, known_sem = take(7)

    core = lax.axis_index("face")
    me = lax.axis_index("elem") * 2 + core

    def ring(by):
        device = lax.rem(me + by + size, size)
        return lax.div(device, 2), lax.rem(device, 2)

    barrier = pltpu.get_barrier_semaphore()
    greeted = [by for by in range(-REACH, REACH + 1) if by != 0]
    for by in greeted:
        pl.semaphore_signal(barrier, inc=1, device_id=ring(by), device_id_type=MESH)

    loads = {
        index: pltpu.make_async_copy(sources[index], inputs[index], in_sem.at[index])
        for index in range(1, len(inputs))
    }
    forcing_loads = [
        pltpu.make_async_copy(
            sources[0].at[:, pl.ds(at, width)],
            forcing_ref.at[:, pl.ds(at, width)],
            in_sem.at[len(inputs) + index],
        )
        for index, (at, width) in enumerate(((0, 128), (384, 128), (128, 256)))
    ]
    loads[2].start()
    forcing_loads[0].start()
    forcing_loads[1].start()
    loads[1].start()
    forcing_loads[2].start()
    for index in range(len(inputs) - 1, 2, -1):
        loads[index].start()

    stages = []
    while REACH << len(stages) < size // 2:
        stages.append(REACH << len(stages))

    def tell(stage):
        if stage < len(stages):
            for way, by in enumerate((stages[stage], -stages[stage])):
                pl.semaphore_signal(
                    known_sem.at[stage, way], inc=1, device_id=ring(by), device_id_type=MESH
                )

    def hear(stage):
        if stage < len(stages):
            for way in range(2):
                pl.semaphore_wait(known_sem.at[stage, way], 1)

    def remote(source, target, send, recv, device):
        return pltpu.make_async_remote_copy(
            src_ref=source,
            dst_ref=target,
            send_sem=send,
            recv_sem=recv,
            device_id=device,
            device_id_type=MESH,
        )

    def slot(place, reach):
        return 2 * reach if place == reach else place - (place > reach)

    def to_ring(buffer, send, recv, reach):
        for by in sorted(range(-reach, reach + 1), key=abs):
            if by != 0:
                remote(
                    buffer.at[2 * reach], buffer.at[slot(reach - by, reach)], send, recv, ring(by)
                ).start()
        others = buffer.at[pl.ds(0, 2 * reach)]
        return remote(others, others, send, recv, ring(1))

    half = lanes((ROWS, 128)) < 64

    def tile(ref, index):
        return ref[:, 128 * index : 128 * index + 128]

    def put(ref, index, value):
        ref[:, 128 * index : 128 * index + 128] = value

    def face_of(ref):
        return jnp.where(half, tile(ref, 0), tile(ref, 3))

    def put_face(ref, value):
        put(ref, 0, jnp.where(half, value, tile(ref, 0)))
        put(ref, 3, jnp.where(half, tile(ref, 3), value))

    def send_faces(face, turn):
        top, bottom, part = face[0:128], face[128:256], half[0:128]
        edge_out[turn, 0] = jnp.where(part, pltpu.roll(top, 64, 1), bottom)
        edge_out[turn, 1] = jnp.where(part, top, pltpu.roll(bottom, 64, 1))
        copies = [
            remote(
                edge_out.at[turn, way],
                edge_in.at[turn, way],
                edge_send.at[turn],
                edge_recv.at[turn],
                ring(1 - 2 * way),
            )
            for way in (1 - core, core)
        ]
        for copy in copies:
            copy.start()
        return remote(
            edge_out.at[turn], edge_in.at[turn], edge_send.at[turn], edge_recv.at[turn], ring(1)
        )

    def faces_arrived(copies, turn):
        copies.wait_recv()
        below, above, part = edge_in[turn, 0], edge_in[turn, 1], half[0:128]
        top = jnp.where(part, below, pltpu.roll(above, 64, 1))
        bottom = jnp.where(part, pltpu.roll(below, 64, 1), above)
        return jnp.concatenate([top, bottom], 0)

    def vertex_sums(each):
        corner = lax.broadcasted_iota(jnp.int32, each.shape, 0)
        even = jnp.where(corner // 2 % 2 == 1, shifted(each, -1, 0), each)
        odd = jnp.where(corner // 2 % 2 == 1, shifted(each, -1, -1), shifted(each, 0, -1))
        each = jnp.where(corner % 2 == 1, odd, even)
        low = jnp.sum(each[0:4], axis=0, keepdims=True)
        high = jnp.sum(each[4:8], axis=0, keepdims=True)
        return low, high

    def gathered(matrix, parts):
        whole = dot16(matrix, parts[0], ((1,), (1,)))
        return whole[0:16] + whole[16:32] + dot16(matrix[0:16], parts[1], ((1,), (1,)))

    def face_lanes(value):
        return jnp.concatenate([value[:, 0:64], value[:, 448:512]], 1)

    def columns(planes):
        return jnp.concatenate(planes, 0).T

    def corner_pieces(corners):
        parts = [part.astype(F32) for part in split(corners, 3)]
        return [parts[left] for left, _ in PIECES]

    row = lax.broadcasted_iota(jnp.int32, (ROWS, ROWS), 0)
    loads[2].wait()
    pick = jnp.where(row == order_ref[...], 1.0, 0.0)
    pick16 = pick.astype(BF16)
    loads[1].wait()
    kappa_rows = jnp.broadcast_to(kappa_ref[...], (16, ROWS))
    kappa = sum(dot16(part, pick16, ((1,), (1,))) for part in split(kappa_rows, 3))[0:8]
    layer[2] = kappa[0:1]
    halo[2 * REACH, 2:3] = kappa[0:1]
    load_ref, r0_ref = field["load"], field["r0"]

    def permuted(matrix, value):
        return sum(dot16(matrix, part) for part in split(value, 2))

    for copy in forcing_loads[:2]:
        copy.wait()
    first_face = shared_xy(permuted(pick16, face_of(forcing_ref)))
    own9 = nine(kappa)
    own_rows = [plane[0:1] for plane in own9] + [jnp.zeros((7, ROWS), F32)]
    own_columns = columns(own_rows)
    coeff_ref[...] = jnp.broadcast_to(own_columns[:, 4:5], (ROWS, 128))
    own_columns_ref[...] = own_columns

    def interior(value, x_ref):
        inverse = field["inverse"]
        zero = jnp.zeros((ROWS, 128), F32)
        put(x_ref, 0, jnp.where(half, zero, tile(inverse, 0) * tile(value, 0)))
        put(x_ref, 1, tile(inverse, 1) * tile(value, 1))
        put(x_ref, 2, tile(inverse, 2) * tile(value, 2))
        put(x_ref, 3, jnp.where(half, tile(inverse, 3) * tile(value, 3), zero))
        parts = split(x_ref[...], 2)
        high, low = stiff_ref[0:NODES], stiff_ref[NODES:]
        field["stiffened"][...] = (
            dot16(parts[0], high) + dot16(parts[1], high) + dot16(parts[0], low)
        )
        return gathered(table["gather"][0:32].astype(BF16), parts)

    def prepare_halo():
        forcing_loads[2].wait()
        load_ref[...] = permuted(pick16, forcing_ref[...])
        for index in range(3, len(inputs)):
            loads[index].wait()
        parts = split(load_ref[...], 2)
        first = table["gather"][32:48].astype(BF16)
        each = dot16(first, parts[0], ((1,), (1,)))
        each = each[0:8] + each[8:16] + dot16(first, parts[1], ((1,), (1,)))[0:8]
        low, high = vertex_sums(each)
        halo[2 * REACH, 0:1] = low
        halo[2 * REACH, 1:2] = high

    def prepare_interior():
        own_columns = own_columns_ref[...]
        fixed = table["rows"][0:1]
        field["inverse"][...] = 1.0 / (dot(own_columns, table["share"][...]) + fixed)
        own_face_ref[...] = dot(own_columns, table["share_face"][0:16]) + table["rows"][2:3, 0:128]
        stiff = table["stiff"][...]
        upper_piece = stiff.astype(BF16)
        stiff_ref[0:NODES] = upper_piece
        stiff_ref[NODES:] = (stiff - upper_piece.astype(F32)).astype(BF16)
        for index in range(4):
            put(r0_ref, index, shared_xy(tile(load_ref, index)))
        inner_rows_ref[...] = interior(r0_ref, field["x0"])
        for at, piece in ((0, 0), (128, 0), (256, NODES)):
            stiff_face_ref[at : at + 64] = stiff_ref[piece : piece + 64]
            stiff_face_ref[at + 64 : at + 128] = stiff_ref[piece + 448 : piece + 512]

    ahead = me < REACH

    @pl.when(ahead)
    def _():
        prepare_halo()
        prepare_interior()

    pl.semaphore_wait(barrier, len(greeted))
    layer_copies = to_ring(layer, layer_send, layer_recv, 1)
    edges = [send_faces(first_face, 0)]
    tell(0)

    @pl.when(jnp.logical_not(ahead))
    def _():
        prepare_halo()

    halo_copies = to_ring(halo, halo_send, halo_recv, REACH)

    @pl.when(jnp.logical_not(ahead))
    def _():
        prepare_interior()

    inner_rows = inner_rows_ref[...]
    mass, mass_face = table["rows"][1:2], table["rows"][3:4, 0:128]
    own_face = own_face_ref[...]
    share_two = table["share_face"][16:96].astype(BF16)
    gather = table["gather"][0:32].astype(BF16)
    gather_face = face_lanes(gather)
    stiff_face_face = face_lanes(stiff_face_ref[...])

    hear(0)
    tell(1)
    layer_copies.wait_recv()
    two = jnp.concatenate([layer[0], layer[1], jnp.zeros((6, ROWS), F32)], 0)
    two9 = jnp.concatenate([plane[0:2] for plane in nine(two)] + [two[2:8]], 0)
    two_pieces = [part.astype(F32) for part in split(two9, 2)]
    two_columns = columns([two_pieces[0], two_pieces[0], two_pieces[1], two])
    inverse_face = 1.0 / (own_face + dot16(two_columns.astype(BF16), share_two))
    coeff_beside = jnp.where(half, two_columns[:, 72:73], two_columns[:, 73:74])
    coeff = coeff_ref[...]
    face = first_face + faces_arrived(edges[0], 0)
    put_face(r0_ref, face)

    def outer(face, x_ref, rows):
        x_face = inverse_face * face
        put_face(x_ref, x_face)
        parts = split(x_face, 2)
        rows = rows + gathered(gather_face, parts)
        stacked = jnp.concatenate([parts[0], parts[1], parts[0]], 1)
        return x_face, stacked, rows, dot16(stacked, stiff_face_face)

    x_face, stacked, rows0, steep_face = outer(face, field["x0"], inner_rows)
    rough = coeff * (face_of(field["stiffened"]) + steep_face) + mass_face * x_face
    low, high = vertex_sums(kappa * rows0[0:8] + rows0[8:16])
    rest[2 * NEAR, 0:1] = low
    rest[2 * NEAR, 1:2] = high
    rest_copies = to_ring(rest, rest_send, rest_recv, NEAR)
    edges.append(send_faces(shared_xy(rough), 1))

    hear(1)
    tell(2)
    field["stiffened"][...] += dot16(stacked, stiff_face_ref[...])
    spread_table = table["spread"][...].astype(BF16)
    spread_face_table = table["spread_face"][...].astype(BF16)
    spread_own_face = jnp.concatenate(
        [face_lanes(spread_table[:, 0:NODES]), face_lanes(spread_table[:, NODES:])], 1
    )
    halo_copies.wait_recv()
    planes = list(range(-3, REACH + 1)) + list(range(1 - REACH, -3))

    def halo_rows(shift, which):
        places = [slot(REACH + p + shift, REACH) for p in planes]
        return jnp.concatenate([halo[place, which : which + 1] for place in places], 0)

    under4, over4 = four(halo_rows(-1, 2)), four(halo_rows(0, 2))
    both4 = [a + b for a, b in zip(under4, over4)]
    diag = (2.0 / 3.0) * (both4[0] + both4[1] + both4[2] + both4[3]) + REACT * 64.0 / 27.0
    damp = -OMEGA / diag
    damp_down, damp_up = up(damp), down(damp)
    level = {key: damp * value for key, value in coarse_stencil(both4, 1).items()}
    from_above = {key: damp_down * value for key, value in coarse_stencil(under4, 0).items()}
    from_below = {key: damp_up * value for key, value in coarse_stencil(over4, 0).items()}
    start = -damp * (halo_rows(0, 0) + halo_rows(-1, 1))
    vert = start
    for _ in range(3):
        vert = start + swept(vert, level, from_above, from_below)
    remainder = (vert - swept(vert, level, from_above, from_below))[0:8]

    def corners_of(vert, lower):
        found = [shifted(vert, *key) for key in ((0, 0), (0, 1), (1, 0), (1, 1))]
        return [
            jnp.concatenate(
                [c[k : k + 1] for c in found] + [c[k + 1 : k + 2] for c in found], 0
            )
            for k in lower
        ]

    own, under, over = corners_of(vert[0:8], (3, 2, 4))
    spread = dot16(columns(corner_pieces(own)).astype(BF16), spread_table)
    beside = dot16(
        columns(corner_pieces(under) + corner_pieces(over)).astype(BF16),
        spread_face_table,
    )
    beside = shared_xy(coeff_beside * beside[:, 0:128] + beside[:, 128:256])

    def total(value):
        quarter = ROWS // 4
        value = added(value[at * quarter : at * quarter + quarter] for at in range(4))
        return jnp.sum(
            jnp.sum(value.reshape(quarter // 8, 8, 128), axis=0), axis=(0, 1), keepdims=True
        )

    def applied(x_ref, spread, z_ref, image_ref):
        for index in range(4):
            at = 128 * index
            z = tile(x_ref, index) + spread[:, at : at + 128]
            put(z_ref, index, z)
            put(
                image_ref,
                index,
                coeff * (tile(field["stiffened"], index) + spread[:, 512 + at : 640 + at])
                + mass[:, at : at + 128] * z,
            )

    def inner(left, right):
        return total(added(tile(left, index) * tile(right, index) for index in range(4)))

    applied(field["x0"], spread, field["z0"], field["qloc"])
    rz = inner(load_ref, field["z0"])
    zq = inner(field["qloc"], field["z0"])
    for index in range(4):
        put(field["q"], index, shared_xy(tile(field["qloc"], index)))
    partial_face = face_of(field["q"]) + beside
    inner_rows = interior(field["q"], field["x1"])

    face_image = face_of(field["qloc"])
    steep_inner = face_of(field["stiffened"])
    yw = total(
        sum(
            tile(field["x1"], index)
            * (
                coeff * tile(field["stiffened"], index)
                + mass[:, 128 * index : 128 * index + 128] * tile(field["x1"], index)
            )
            for index in range(4)
        )
    )
    zero = jnp.zeros((ROWS, 128), F32)
    qy = inner(field["qloc"], field["x1"])
    back16 = pick.T.astype(BF16)

    def stored(value):
        return permuted(back16, value)

    sent_z0[...] = stored(field["z0"][...])
    sent_r0[...] = stored(r0_ref[...])

    rest_copies.wait_recv()
    face = partial_face + faces_arrived(edges[1], 1)
    x_face, stacked, rows1, steep_face = outer(face, field["x1"], inner_rows)
    target = jnp.concatenate(
        [rest[slot(NEAR + p, NEAR), 0:1] for p in range(-3, 5)], 0
    ) + jnp.concatenate([rest[slot(NEAR + p - 1, NEAR), 1:2] for p in range(-3, 5)], 0)

    def top(parts):
        return {key: value[0:8] for key, value in parts.items()}

    level, from_above, from_below = top(level), top(from_above), top(from_below)
    start = remainder - damp[0:8] * target
    vert = start
    for _ in range(3):
        vert = start + swept(vert, level, from_above, from_below)
    (own,) = corners_of(vert, (3,))

    own_pieces = columns(corner_pieces(own)).astype(BF16)
    spread = dot16(own_pieces, spread_own_face)
    y_face = x_face + spread[:, 0:128]
    w_face = coeff * (steep_inner + steep_face + spread[:, 128:256]) + mass_face * y_face
    late_face = shared_xy(w_face)

    def flipped(value, bit):
        corner = lax.broadcasted_iota(jnp.int32, value.shape, 0)
        return jnp.where(
            corner // bit % 2 == 0, pltpu.roll(value, 8 - bit, 0), pltpu.roll(value, bit, 0)
        )

    edge_sum = flipped(own, 1) + flipped(own, 2) + flipped(own, 4)
    all_sum = jnp.sum(own, axis=0, keepdims=True)
    weighed = own
    for bit in (1, 2, 4):
        weighed = (2.0 * weighed + flipped(weighed, bit)) * (1.0 / 3.0)
    steep = (5.0 / 6.0) * own + (1.0 / 6.0) * (edge_sum - all_sum)
    energy = own * (
        kappa * (steep + 2.0 * rows1[0:8]) + (REACT * weighed + 2.0 * rows1[8:16])
    )
    qy = qy + total(face_image * x_face) + jnp.sum((start * vert / -damp[0:8])[3:4], keepdims=True)
    yw = yw + jnp.sum(energy, keepdims=True)
    yw = yw + total(
        x_face * (coeff * (2.0 * steep_inner + steep_face) + mass_face * x_face)
    )

    hear(2)
    lane = lanes((1, 128))
    mine = jnp.zeros((1, 128), F32)
    for index, value in enumerate((rz, zq, qy, yw)):
        mine = jnp.where(lane == index, value, mine)
    sums_ref[0] = mine

    def send_sums(turn, carry):
        by = lax.rem(turn + jnp.where(turn >= me, 1, 0) - me + size, size)
        remote(sums_ref.at[0], sums_ref.at[by], sum_send, sum_recv, ring(by)).start()
        return carry

    lax.fori_loop(0, REACH, send_sums, 0)
    edges.append(send_faces(late_face, 2))
    lax.fori_loop(REACH, size - 1, send_sums, 0)

    field["stiffened"][...] += dot16(stacked, stiff_face_ref[...])
    applied(field["x1"], dot16(own_pieces, spread_table), field["y"], field["w"])
    for index in range(4):
        put(field["w"], index, shared_xy(tile(field["w"], index)))
    put_face(field["q"], face)
    sent_y[...] = stored(field["y"][...])
    sent_q[...] = stored(field["q"][...])
    sent_w[...] = stored(field["w"][...])
    others = sums_ref.at[pl.ds(1, size - 1)]
    all_sums = remote(others, others, sum_send, sum_recv, ring(1))
    all_sums.wait_send()
    for copies in [layer_copies, halo_copies, rest_copies] + edges:
        copies.wait_send()
    face = stored(faces_arrived(edges[2], 2))
    sent_w[:, 0:128] += jnp.where(half, face, zero)
    sent_w[:, 384:512] += jnp.where(half, zero, face)
    all_sums.wait_recv()
    eighth = size // 8
    sums = added(sums_ref[at * eighth : at * eighth + eighth] for at in range(8))
    sums = jnp.sum(sums, axis=0)
    rz, zq, qy, yw = (sums[:, index : index + 1] for index in range(4))
    first = rz / zq
    gamma = first * first * qy - rz
    grown = 1.0 + gamma / rz
    second = gamma / (grown * grown * zq - 2.0 * first * grown * qy + first * first * yw)
    straight, bent = first + second * grown, first * second
    steps_ref[0:1] = jnp.broadcast_to(straight, (1, 128))
    steps_ref[1:2] = jnp.broadcast_to(bent, (1, 128))


def combine(z0, y, r0, q, w, steps, solution_ref, residual_ref, solution_part, residual_part, sem):
    straight, bent = steps[0:1, 0:1], steps[1:2, 0:1]
    copies = []
    rows = ROWS // PARTS
    for part in range(PARTS):
        at = pl.ds(part * rows, rows)
        solution_part[at] = straight * z0[at] - bent * y[at]
        copies.append(
            pltpu.make_async_copy(solution_part.at[at], solution_ref.at[at], sem.at[0, part])
        )
        copies[-1].start()
        residual_part[at] = r0[at] - straight * q[at] + bent * w[at]
        copies.append(
            pltpu.make_async_copy(residual_part.at[at], residual_ref.at[at], sem.at[1, part])
        )
        copies[-1].start()
    for copy in copies:
        copy.wait()


def per_device(size, forcing, kappa, elem_order):
    tables = all_tables()
    operands = [forcing, kappa.reshape(1, ROWS), elem_order]
    operands += [jnp.asarray(tables[name], F32) for name in NAMES]
    out = jax.ShapeDtypeStruct((ROWS, NODES), F32)
    steps = jax.ShapeDtypeStruct((8, 128), F32)
    count, close = 2 * REACH + 1, 2 * NEAR + 1
    dma = pltpu.SemaphoreType.DMA
    vmem = pl.BlockSpec(memory_space=pltpu.VMEM)
    hbm = pl.BlockSpec(memory_space=pltpu.HBM)
    stored = pl.pallas_call(
        functools.partial(kernel, size),
        out_shape=(out,) * 5 + (steps,),
        in_specs=[hbm] * len(operands),
        out_specs=(vmem,) * 6,
        scratch_shapes=[pltpu.VMEM(operand.shape, operand.dtype) for operand in operands]
        + [pltpu.VMEM((ROWS, NODES), F32)] * len(FIELDS)
        + [
            pltpu.VMEM((ROWS, 128), F32),
            pltpu.VMEM((ROWS, 16), F32),
            pltpu.VMEM((ROWS, 128), F32),
            pltpu.VMEM((16, ROWS), F32),
            pltpu.VMEM((2 * NODES, NODES), BF16),
            pltpu.VMEM((384, NODES), BF16),
            pltpu.VMEM((3, 2, 128, 128), F32),
            pltpu.VMEM((3, 2, 128, 128), F32),
            pltpu.VMEM((3, 1, ROWS), F32),
            pltpu.VMEM((count, 3, ROWS), F32),
            pltpu.VMEM((close, 2, ROWS), F32),
            pltpu.VMEM((size, 1, 128), F32),
            dma((len(operands) + 3,)),
            dma,
            dma,
            dma,
            dma,
            dma,
            dma,
            dma((3,)),
            dma((3,)),
            dma,
            dma,
            pltpu.SemaphoreType.REGULAR((3, 2)),
        ],
        compiler_params=pltpu.CompilerParams(
            collective_id=0, has_side_effects=True, vmem_limit_bytes=32 * 1024 * 1024
        ),
        name="solve",
    )(*[pltpu.with_memory_space_constraint(operand, pltpu.HBM) for operand in operands])
    return pl.pallas_call(
        combine,
        out_shape=(out, out),
        in_specs=[vmem] * 6,
        out_specs=(hbm, hbm),
        scratch_shapes=[
            pltpu.VMEM((ROWS, NODES), F32),
            pltpu.VMEM((ROWS, NODES), F32),
            dma((2, PARTS)),
        ],
        compiler_params=pltpu.CompilerParams(vmem_limit_bytes=16 * 1024 * 1024),
        name="combine",
    )(*stored)


def solution(mesh):
    in_specs = (P(("elem", "face"), None), P(("elem", "face")), P(("elem", "face"), None))
    out_specs = (P(("elem", "face"), None), P(("elem", "face"), None))
    size = mesh.shape["elem"] * mesh.shape["face"]
    return jax.shard_map(
        functools.partial(per_device, size),
        mesh=mesh,
        in_specs=in_specs,
        out_specs=out_specs,
        check_vma=False,
    )
```
